32 devices in a mesh: groups: 2 (over x), dp: 2 (over core), tensor: 8 (over z, y).
Axes of the slice: x: 2, y: 2, z: 4, core: 2. Of those that a mesh axis runs over, the one named last changes fastest.
Arguments:
- query_cotangent: bfloat16 [4096, 8192], P(('groups', 'dp'), 'tensor'), parts along dimension 0, may hold values from -6 to 6
- projection_input: bfloat16 [4096, 8192], P(('groups', 'dp'), 'tensor'), parts along dimension 0, may hold values from -0.125 to 0.125
- saved_lowrank: bfloat16 [4096, 128], P(('groups', 'dp')), parts along dimension 0, may hold values from -0.125 to 0.125
- query_matrix: bfloat16 [8192, 8192], P(None, 'tensor'), may hold values from -0.09375 to 0.09375
- adapter_shrink: bfloat16 [16, 8192, 128], P(None, 'tensor'), may hold values from -0.0625 to 0.0625
- adapter_expand: bfloat16 [16, 128, 8192], P(None, None, 'tensor'), may hold values from -0.0625 to 0.0625
- tenant_per_block: int32 [32], P(('groups', 'dp')), parts along dimension 0, may hold values from 0 to 15
- tenant_adapter_rank: int32 [16], replicated, may hold values from 16 to 128, as said below
- tenant_owner_index: int32 [16], replicated, may hold values from 0 to 1, as said below
Outputs:
- input_gradient: bfloat16 [4096, 8192], P(('groups', 'dp'), 'tensor'), parts along dimension 0
- grad_shrink: float32 [32, 8192, 128], P(('groups', 'dp'), 'tensor'), parts along dimension 0
- grad_expand: float32 [32, 128, 8192], P(('groups', 'dp'), None, 'tensor'), parts along dimension 0
The draws below stay inside these ranges and needn't reach their ends.
There are 2 independent parts, one for each index of `groups`. The reference program is written for one: setup_inputs(seed, part) draws one part's arguments, and reference() takes and returns one part's arrays. A program takes and returns all parts, laid end to end along the dimension named above; an argument that names none is the same for every part. Nothing has to cross between parts.
Inputs may be any that keep to these rules, and one draw needn't show every extreme that they name: `tenant_adapter_rank`: a multiple of 16; some tenant has rank 128 and some has rank 16. `tenant_owner_index`: each of the 2 dp indices owns exactly 8 tenants.
All inputs are finite; a program needn't handle non-finite values.
Results may differ from the reference program's by a relative error of at most 0.015.
Values may be sent and summed in bfloat16 or wider, within the bound.
No kernel may reach another device: no remote copies, remote signals or barrier semaphores. Data moves between devices by JAX's collectives and lax.ppermute only.
A program may use at most 192 MiB of HBM per device.

```python
import math
import jax
import jax.numpy as jnp
import numpy as np
from jax import lax

MODEL_WIDTH = 8192
LARGEST_RANK = 128
TENANT_TOTAL = 16
TOKENS = 2048
BLOCKS = 16
N_DP = 2
N_TENSOR = 8


def draw_tenant_adapter_rank(key, part):
    key = jax.random.fold_in(key, 11)
    first_key, second_key, third_key = jax.random.split(key, 3)
    levels = LARGEST_RANK // 16
    values = 16 * jax.random.randint(first_key, (TENANT_TOTAL,), 1, levels + 1)
    top_place = jax.random.randint(second_key, (), 0, TENANT_TOTAL)
    low_place = (top_place + jax.random.randint(third_key, (), 1, TENANT_TOTAL)) % TENANT_TOTAL
    positions = jnp.arange(TENANT_TOTAL)
    values = jnp.where(positions == top_place, LARGEST_RANK, values)
    values = jnp.where(positions == low_place, 16, values)
    return values.astype(jnp.int32)


def draw_tenant_owner_index(key, part):
    key = jax.random.fold_in(key, 23)
    shuffled = jax.random.permutation(key, TENANT_TOTAL)
    return (shuffled % N_DP).astype(jnp.int32)


def plant(entries, key, least, top_value):
    extent = entries.shape
    place = [jax.random.randint(jax.random.fold_in(key, axis), (), 0, extent[axis]) for axis in range(len(extent))]
    entries = entries.at[tuple(place)].set(least)
    longest = extent.index(max(extent))
    place[longest] = (place[longest] + 1) % extent[longest]
    return entries.at[tuple(place)].set(top_value)


def with_spikes(entries, stream_key, source, target, shards_of, factor):
    def block_of(dim):
        return (jnp.arange(entries.shape[dim]) // (entries.shape[dim] // shards_of)).reshape((-1,) + (1,) * (entries.ndim - 1 - dim))

    near = jax.random.permutation(stream_key, shards_of)[block_of(target)]
    other_side = (block_of(target) + shards_of // 2) % shards_of
    return jnp.where((block_of(source) == near) | (block_of(source) == other_side), factor * entries, entries)


def shard_levels(key, dims, pieces, least, top_value):
    level = 1.0
    for axis_at, blocks in pieces:
        draws = jax.random.uniform(jax.random.fold_in(jax.random.fold_in(key, 6), axis_at), (blocks,), jnp.float32, least / len(pieces), top_value / len(pieces))
        level = level * jnp.repeat(jnp.exp(draws), dims[axis_at] // blocks).reshape((-1,) + (1,) * (len(dims) - 1 - axis_at))
    return level


def cumulative_ranks(number_of, slope):
    portions = [(1 << 20) // math.isqrt(grade ** slope) + 1 for grade in range(1, number_of + 1)]
    spread = 1 + sum(portions) // (1 << 30)
    return np.cumsum(np.array([max(1, weight // spread) for weight in portions]))


def skewed_ids(key, shape, amount, skew):
    grid = cumulative_ranks(amount, skew)
    pick = jax.random.randint(jax.random.fold_in(key, 1), shape, 0, int(grid[amount - 1]))
    rank = jnp.searchsorted(jnp.asarray(grid, jnp.int32), pick, side="right")
    return jax.random.permutation(jax.random.fold_in(key, 2), amount)[rank].astype(jnp.int32)


def normal_values(rng, dims, width, bound, cuts=(), kind=jnp.bfloat16):
    values = width * jax.random.normal(rng, dims, jnp.float32)
    if cuts:
        values = values * shard_levels(rng, dims, cuts, -0.22, 0.18)
    return jnp.clip(values, -bound, bound).astype(kind)


def noise_with(key, extent, deviation, most, cuts, heavy, held_as=jnp.bfloat16):
    array = deviation * jax.random.normal(key, extent, jnp.float32)
    if cuts:
        array = array * shard_levels(key, extent, cuts, -0.22, 0.18)
    return jnp.clip(with_spikes(array, jax.random.fold_in(key, 3), *heavy), -most, most).astype(held_as)


def setup_inputs(seed: int = 0, part: int = 0) -> dict:
    streams_of = jax.random.split(jax.random.key(seed), 10)
    part_keys = jax.random.split(jax.random.fold_in(streams_of[9], part), 10)
    query_cotangent = normal_values(part_keys[0], (TOKENS, MODEL_WIDTH), 1.0, 6.0, ((0, 2), (1, 8)))
    projection_input = jnp.clip(jax.random.uniform(part_keys[1], (TOKENS, MODEL_WIDTH), jnp.float32, -0.125, 0.125) * shard_levels(part_keys[1], (TOKENS, MODEL_WIDTH), ((0, 2), (1, 8)), -0.4, 0.0), -0.125, 0.125).astype(jnp.bfloat16)
    saved_lowrank = jnp.clip(jax.random.uniform(part_keys[2], (TOKENS, LARGEST_RANK), jnp.float32, -0.125, 0.125) * shard_levels(part_keys[2], (TOKENS, LARGEST_RANK), ((0, 2),), -0.4, 0.0), -0.125, 0.125).astype(jnp.bfloat16)
    query_matrix = noise_with(streams_of[3], (MODEL_WIDTH, MODEL_WIDTH), MODEL_WIDTH ** -0.5, 0.09375, ((1, 8),), (1, 0, 8, 2.0))
    adapter_shrink = normal_values(streams_of[4], (TENANT_TOTAL, MODEL_WIDTH, LARGEST_RANK), MODEL_WIDTH ** -0.5, 0.0625, ((1, 8),))
    adapter_expand = normal_values(streams_of[5], (TENANT_TOTAL, LARGEST_RANK, MODEL_WIDTH), MODEL_WIDTH ** -0.5, 0.0625, ((2, 8),))
    tenant_per_block = plant(skewed_ids(part_keys[6], (BLOCKS,), TENANT_TOTAL, 2), jax.random.fold_in(part_keys[6], 3), 0, TENANT_TOTAL - 1).astype(jnp.int32)
    tenant_adapter_rank = draw_tenant_adapter_rank(jax.random.fold_in(streams_of[9], 71), part)
    tenant_owner_index = draw_tenant_owner_index(jax.random.fold_in(streams_of[9], 71), part)
    return dict(query_cotangent=query_cotangent, projection_input=projection_input, saved_lowrank=saved_lowrank, query_matrix=query_matrix, adapter_shrink=adapter_shrink, adapter_expand=adapter_expand, tenant_per_block=tenant_per_block, tenant_adapter_rank=tenant_adapter_rank, tenant_owner_index=tenant_owner_index)


adapter_alpha = 32.0


def reference(query_cotangent, projection_input, saved_lowrank, query_matrix, adapter_shrink, adapter_expand, tenant_per_block, tenant_adapter_rank, tenant_owner_index):
    count_of_rows, width_total = query_cotangent.shape
    block_count = count_of_rows // 128
    tenant_count = tenant_adapter_rank.shape[0]
    rank_extent = adapter_shrink.shape[2]
    shard_extent = width_total // N_TENSOR
    grad_parts = query_cotangent.reshape(count_of_rows, N_TENSOR, shard_extent).transpose(1, 0, 2)
    weight_parts = query_matrix.reshape(width_total, N_TENSOR, shard_extent).transpose(1, 0, 2)

    def add_part(running, pair):
        term = lax.dot_general(pair[0], pair[1], (((1,), (1,)), ((), ())), preferred_element_type=jnp.float32)
        rounded = lax.optimization_barrier(term.astype(jnp.bfloat16))
        return running + rounded.astype(jnp.float32), None

    frozen_product, _ = lax.scan(add_part, jnp.zeros((count_of_rows, width_total), jnp.float32), (grad_parts, weight_parts))
    tenant_ids = jnp.arange(tenant_count, dtype=jnp.int32)
    rank_per_block = jnp.take(tenant_adapter_rank, tenant_per_block, axis=0).astype(jnp.float32)
    scale_per_block = adapter_alpha / rank_per_block
    block_mask = (jnp.arange(rank_extent).astype(jnp.float32)[None, :] < rank_per_block[:, None]).astype(jnp.float32)
    gradient_per_block = query_cotangent.reshape(block_count, 128, width_total).astype(jnp.float32)
    expand_per_block = jnp.take(adapter_expand, tenant_per_block, axis=0).astype(jnp.float32)
    lowrank_float = jnp.einsum("zuh,zsh->zus", gradient_per_block, expand_per_block, precision=lax.Precision.HIGHEST)
    lowrank_float = lowrank_float * (scale_per_block[:, None, None] * block_mask[:, None, :])
    lowrank_bfloat = lowrank_float.astype(jnp.bfloat16).astype(jnp.float32)
    shrink_per_block = jnp.take(adapter_shrink, tenant_per_block, axis=0).astype(jnp.float32)
    adapter_term = jnp.einsum("uwq,ueq->uwe", lowrank_bfloat, shrink_per_block, precision=lax.Precision.HIGHEST)
    input_gradient = (frozen_product + adapter_term.reshape(count_of_rows, width_total)).astype(jnp.bfloat16)
    input_per_block = projection_input.reshape(block_count, 128, width_total).astype(jnp.float32)
    shrink_piece = jnp.einsum("tme,tmj->tej", input_per_block, lowrank_bfloat, precision=lax.Precision.HIGHEST)
    saved_per_block = saved_lowrank.reshape(block_count, 128, rank_extent).astype(jnp.float32) * block_mask[:, None, :]
    expand_piece = jnp.einsum("paw,pan->pwn", saved_per_block, gradient_per_block, precision=lax.Precision.HIGHEST)
    expand_piece = expand_piece * scale_per_block[:, None, None]
    slot_order = jnp.argsort(tenant_owner_index * tenant_count + tenant_ids).astype(jnp.int32)
    slot_of = jnp.argsort(slot_order).astype(jnp.int32)
    block_slot = jnp.take(slot_of, tenant_per_block, axis=0)
    block_select = (block_slot[:, None] == tenant_ids[None, :]).astype(jnp.float32)
    grad_shrink = jnp.einsum("bs,bdr->sdr", block_select, shrink_piece, precision=lax.Precision.HIGHEST)
    grad_expand = jnp.einsum("bs,brd->srd", block_select, expand_piece, precision=lax.Precision.HIGHEST)
    return input_gradient, grad_shrink, grad_expand
```

```python
import functools

import jax
import jax.numpy as jnp
from jax import lax
from jax.experimental import pallas as pl
from jax.experimental.pallas import tpu as pltpu
from jax.sharding import PartitionSpec as P

adapter_alpha = 32.0
row_block = 128
bf16 = jnp.bfloat16
f32 = jnp.float32
contract_last = (((1,), (1,)), ((), ()))
contract_first = (((0,), (0,)), ((), ()))
vmem_bytes = 40 * 1024 * 1024


def params():
    return pltpu.CompilerParams(vmem_limit_bytes=vmem_bytes)


def product_kernel(add_count, block_count, has_link, *refs):
    position = 1
    rows, weights = refs[1], refs[2]
    position = 3
    total = lax.dot_general(
        rows[...], weights[...], contract_last, preferred_element_type=f32
    )
    for _ in range(add_count):
        total = total + refs[position][...].astype(f32)
        position += 1
    if block_count:
        low = refs[position]
        position += 1
        terms = []
        for i in range(block_count):
            terms.append(
                lax.dot_general(
                    low[i * row_block : (i + 1) * row_block, :],
                    refs[position][0],
                    contract_last,
                    preferred_element_type=f32,
                )
            )
            position += 1
        total = total + jnp.concatenate(terms, axis=0)
    refs[-1][...] = total.astype(refs[-1].dtype)


def product(scalars, gradient, weights, piece, piece_rows, width, adds, link, adapter=None):
    depth = gradient.shape[1]
    tile = min(width, 512)
    while width % tile:
        tile //= 2
    steps = width // tile
    in_specs = [
        pl.BlockSpec((piece_rows, depth), lambda j, s: (piece, 0)),
        pl.BlockSpec((tile, depth), lambda j, s: (s[0] * steps + j, 0)),
    ]
    operands = [gradient, weights]
    for array, shifted in adds:
        if shifted:
            in_specs.append(
                pl.BlockSpec((piece_rows, tile), lambda j, s: (0, s[1] * steps + j))
            )
        else:
            in_specs.append(pl.BlockSpec((piece_rows, tile), lambda j, s: (0, j)))
        operands.append(array)
    block_count = 0
    if adapter is not None:
        low, shrink = adapter
        rank = low.shape[1]
        block_count = piece_rows // row_block
        in_specs.append(pl.BlockSpec((piece_rows, rank), lambda j, s: (piece, 0)))
        operands.append(low)
        for i in range(block_count):
            in_specs.append(
                pl.BlockSpec((1, tile, rank), functools.partial(lambda j, s, i: (s[2 + i], j, 0), i=i))
            )
            operands.append(shrink)
    if link is not None:
        in_specs.append(pl.BlockSpec(memory_space=pl.ANY))
        operands.append(link)
    return pl.pallas_call(
        functools.partial(product_kernel, len(adds), block_count, link is not None),
        grid_spec=pltpu.PrefetchScalarGridSpec(
            num_scalar_prefetch=1,
            grid=(steps,),
            in_specs=in_specs,
            out_specs=pl.BlockSpec((piece_rows, tile), lambda j, s: (0, j)),
        ),
        out_shape=jax.ShapeDtypeStruct((piece_rows, width), bf16),
        compiler_params=params(),
        cost_estimate=pl.CostEstimate(
            flops=2 * piece_rows * width * depth,
            bytes_accessed=2 * (width * depth + piece_rows * depth + (1 + len(adds)) * piece_rows * width),
            transcendentals=0,
        ),
    )(scalars, *operands)


def low_kernel(tenants, rows, expand, link, out):
    out[...] = lax.dot_general(
        rows[...], expand[0], contract_last, preferred_element_type=f32
    ).astype(out.dtype)


def low_product(tenants, gradient, expand, link):
    count_of_rows, depth = gradient.shape
    rank = expand.shape[1]
    blocks = count_of_rows // row_block
    return pl.pallas_call(
        low_kernel,
        grid_spec=pltpu.PrefetchScalarGridSpec(
            num_scalar_prefetch=1,
            grid=(blocks,),
            in_specs=[
                pl.BlockSpec((row_block, depth), lambda b, s: (b, 0)),
                pl.BlockSpec((1, rank, depth), lambda b, s: (s[b], 0, 0)),
                pl.BlockSpec(memory_space=pl.ANY),
            ],
            out_specs=pl.BlockSpec((row_block, rank), lambda b, s: (b, 0)),
        ),
        out_shape=jax.ShapeDtypeStruct((count_of_rows, rank), bf16),
        compiler_params=params(),
        cost_estimate=pl.CostEstimate(
            flops=2 * count_of_rows * rank * depth,
            bytes_accessed=2 * (count_of_rows * depth + blocks * rank * depth),
            transcendentals=0,
        ),
    )(tenants, gradient, expand, link)


def factor_kernel(slots_each, blocks, slots, scales, left, right, link, own, other, other_sum):
    own[...] = jnp.zeros_like(own)
    other_sum[...] = jnp.zeros_like(other_sum)
    for b in range(blocks):
        here = pl.ds(b * row_block, row_block)
        piece = lax.dot_general(
            left[here, :], right[here, :], contract_first, preferred_element_type=f32
        )
        piece = piece * scales[b]
        slot = slots[b]

        @pl.when(slot < slots_each)
        def _():
            own[slot] += piece

        @pl.when(slot >= slots_each)
        def _():
            other_sum[slot - slots_each] += piece

    other[...] = other_sum[...].astype(other.dtype)


def factor_sums(slots, scales, left, right, slots_each, others, link):
    count_of_rows, height = left.shape
    width = right.shape[1]
    blocks = count_of_rows // row_block
    whole = pl.BlockSpec(memory_space=pltpu.VMEM)
    return pl.pallas_call(
        functools.partial(factor_kernel, slots_each, blocks),
        in_specs=[
            pl.BlockSpec(memory_space=pltpu.SMEM),
            pl.BlockSpec(memory_space=pltpu.SMEM),
            whole,
            whole,
            pl.BlockSpec(memory_space=pl.ANY),
        ],
        out_specs=[whole, whole],
        out_shape=[
            jax.ShapeDtypeStruct((slots_each, height, width), f32),
            jax.ShapeDtypeStruct((others, height, width), bf16),
        ],
        scratch_shapes=[pltpu.VMEM((others, height, width), f32)],
        compiler_params=params(),
        cost_estimate=pl.CostEstimate(
            flops=2 * count_of_rows * height * width,
            bytes_accessed=2 * count_of_rows * (height + width)
            + 4 * slots_each * height * width
            + 2 * others * height * width,
            transcendentals=0,
        ),
    )(slots, scales, left, right, link)


def per_device(
    tensor_count,
    owner_count,
    gradient,
    projection_input,
    saved_lowrank,
    weights,
    shrink,
    expand,
    tenant_per_block,
    tenant_adapter_rank,
    tenant_owner_index,
):
    count_of_rows, width = gradient.shape
    blocks = count_of_rows // row_block
    tenants = tenant_adapter_rank.shape[0]
    rank_extent = shrink.shape[2]
    nodes = tensor_count // 2
    last = nodes - 1
    place = lax.axis_index("tensor")
    node = place // 2
    side = place % 2
    owner = lax.axis_index("dp")

    halves = 2 if nodes <= 4 else 1
    pieces = 2 * halves
    piece_rows = count_of_rows // pieces
    lower = list(range(halves))
    upper = list(range(halves, pieces))

    link = [None]

    def run(scalars, piece, columns, adds, adapter=None):
        out = product(
            jnp.stack([jnp.asarray(v, jnp.int32) for v in scalars]),
            gradient, weights, piece, piece_rows, columns, adds, link[0], adapter,
        )
        link[0] = out
        return out

    def swap(x, active):
        pairs = []
        for z in active:
            pairs += [(2 * z, 2 * z + 1), (2 * z + 1, 2 * z)]
        return lax.ppermute(x, "tensor", pairs)

    def along(x, hops):
        pairs = [(2 * a + y, 2 * b + y) for a, b in hops for y in range(2)]
        return lax.ppermute(x, "tensor", pairs)

    def tasks(step, lag):
        reach = step - lag
        right = [z for z in range(nodes) if z <= reach and z < last]
        left = [z for z in range(nodes) if z >= last - reach and z > 0]
        to_right = jnp.clip(last - step + node, 0, last)
        to_left = jnp.clip(node - (last - step), 0, last)
        right_hops = [(z, z + 1) for z in right]
        left_hops = [(z, z - 1) for z in left]
        if not set(right) & set(left):
            both = jnp.where(node <= reach, to_right, to_left)
            return [(right + left, both, right_hops, left_hops)]
        return [(right, to_right, right_hops, []), (left, to_left, [], left_hops)]

    def forward(x, right_hops, left_hops):
        targets = [b for _, b in right_hops + left_hops]
        if right_hops and left_hops and len(set(targets)) == len(targets):
            both = along(x, right_hops + left_hops)
            return (both, both)
        return (
            along(x, right_hops) if right_hops else None,
            along(x, left_hops) if left_hops else None,
        )

    def addends(arrived, right_hops, left_hops):
        found = []
        if arrived is None:
            return found
        if right_hops and arrived[0] is not None:
            found.append(arrived[0])
        if left_hops and arrived[1] is not None and not (found and found[0] is arrived[1]):
            found.append(arrived[1])
        return found

    class Flow:
        def __init__(self, piece_ids, lag):
            self.piece_ids, self.lag = piece_ids, lag
            self.arrived = {p: None for p in piece_ids}
            self.swapped = {}

        def has(self, step):
            return self.lag <= step <= last - 1

        def swap(self, step):
            if not self.has(step):
                return
            for t, (active, dest, _, _) in enumerate(tasks(step, self.lag)):
                for p in self.piece_ids:
                    part = run([dest * 2 + (1 - side), 0], p, width, [])
                    self.swapped[step, t, p] = swap(part, active)

        def combine(self, step, p):
            if not self.has(step):
                return
            before = self.arrived[p]
            found = [None, None]
            for t, (active, dest, right_hops, left_hops) in enumerate(tasks(step, self.lag)):
                adds = [(self.swapped[step, t, p], False)]
                adds += [(a, False) for a in addends(before, right_hops, left_hops)]
                part = run([dest * 2 + side, 0], p, width, adds)
                got = forward(part, right_hops, left_hops)
                if right_hops:
                    found[0] = got[0]
                if left_hops:
                    found[1] = got[1]
            self.arrived[p] = tuple(found)

    class DirectFlow:
        def __init__(self):
            self.arrived = {p: None for p in lower}

        def advance(self, step, p):
            if step > last - 1:
                return
            dest = jnp.where(node == step, last, 0)
            adds = [] if self.arrived[p] is None else [(self.arrived[p], False)]
            part = run([dest, 0], p, 2 * width, adds)
            self.arrived[p] = along(part, [(step, step + 1), (last - step, last - step - 1)])

    low_flow = Flow(lower, 1)
    up_flow = Flow(upper, 0)
    direct = DirectFlow()

    tenant_ids = jnp.arange(tenants, dtype=jnp.int32)
    matches = tenant_per_block[:, None] == tenant_ids[None, :]
    rank_per_block = jnp.sum(jnp.where(matches, tenant_adapter_rank[None, :], 0), axis=1).astype(f32)
    scale_per_block = adapter_alpha / rank_per_block
    block_mask = (jnp.arange(rank_extent).astype(f32)[None, :] < rank_per_block[:, None]).astype(f32)
    key = tenant_owner_index * tenants + tenant_ids
    slot_of = jnp.sum((key[None, :] < key[:, None]).astype(jnp.int32), axis=1)
    block_slot = jnp.sum(jnp.where(matches, slot_of[None, :], 0), axis=1)
    slots_each = tenants // owner_count
    own_first = lax.rem(block_slot - owner * slots_each + tenants, tenants)

    direct.advance(0, lower[0])
    up_flow.swap(0)
    for p in lower[1:]:
        direct.advance(0, p)
    low_flow.swap(1)
    up_flow.swap(1)

    low_part = low_product(tenant_per_block, gradient, expand, link[0])
    link[0] = low_part
    half = count_of_rows // 2
    keep = lax.dynamic_slice_in_dim(low_part, side * half, half, 0)
    give = lax.dynamic_slice_in_dim(low_part, (1 - side) * half, half, 0)
    low_half = (keep.astype(f32) + swap(give, range(nodes)).astype(f32)).astype(bf16)
    low_sum = low_half.astype(f32)
    going_right = going_left = low_half
    for hop in range(1, nodes):
        going_right = along(going_right, [(z, z + 1) for z in range(hop - 1, last)])
        going_left = along(going_left, [(z, z - 1) for z in range(1, nodes - hop + 1)])
        low_sum = low_sum + going_right.astype(f32) + going_left.astype(f32)
    low_mine = low_sum.astype(bf16)
    low_other = swap(low_mine, range(nodes))
    low_whole = jnp.where(
        side == 0,
        jnp.concatenate([low_mine, low_other], axis=0),
        jnp.concatenate([low_other, low_mine], axis=0),
    )
    factor = scale_per_block[:, None, None] * block_mask[:, None, :]
    low = (low_whole.astype(f32).reshape(blocks, row_block, rank_extent) * factor).astype(bf16)
    low = low.reshape(count_of_rows, rank_extent)

    for p in upper:
        up_flow.combine(0, p)
    low_flow.swap(2)

    masked = saved_lowrank.reshape(blocks, row_block, rank_extent) * block_mask[:, None, :].astype(bf16)
    masked = masked.reshape(count_of_rows, rank_extent)
    others = slots_each * (owner_count - 1)
    ones = jnp.ones_like(scale_per_block)

    def exchange(own, other):
        total = own
        for hop in range(1, owner_count):
            theirs = other[(hop - 1) * slots_each : hop * slots_each]
            pairs = [(i, (i + hop) % owner_count) for i in range(owner_count)]
            total = total + lax.ppermute(theirs, "dp", pairs).astype(f32)
        return total

    own, other = factor_sums(
        own_first, scale_per_block, masked, gradient, slots_each, others, link[0]
    )
    link[0] = other
    grad_expand = exchange(own, other)

    own_swap = {}

    def swap_own(p):
        adds = [(direct.arrived[p], True)] if p in lower else []
        part = run([node * 2 + (1 - side), 1 - side], p, width, adds)
        own_swap[p] = swap(part, range(nodes))

    grad_shrink = None
    for step in range(1, last):
        direct.advance(step, lower[0])
        low_flow.combine(step, lower[0])
        for p in lower[1:]:
            low_flow.combine(step, p)
            direct.advance(step, p)
        up_flow.swap(step + 1)
        low_flow.swap(step + 2)
        if step == last - 1:
            for p in upper:
                swap_own(p)
            own, other = factor_sums(
                own_first, ones, projection_input, low, slots_each, others, link[0]
            )
            link[0] = other
            grad_shrink = exchange(own, other)
            for p in lower:
                swap_own(p)
        for p in upper:
            up_flow.combine(step, p)

    outs = []
    for p in range(pieces):
        flow = low_flow if p in lower else up_flow
        adds = [(own_swap[p], False)]
        if p in lower:
            adds.append((direct.arrived[p], True))
        arrived = flow.arrived[p]
        adds.append((arrived[0], False))
        if arrived[1] is not arrived[0]:
            adds.append((arrived[1], False))
        in_piece = piece_rows // row_block
        ids = [tenant_per_block[p * in_piece + i] for i in range(in_piece)]
        outs.append(run([node * 2 + side, side] + ids, p, width, adds, (low, shrink)))
    input_gradient = jnp.concatenate(outs, axis=0)
    return (input_gradient, grad_shrink, grad_expand)


def solution(mesh):
    placed = (
        P(("groups", "dp"), "tensor"),
        P(("groups", "dp"), "tensor"),
        P(("groups", "dp"), None),
        P(None, "tensor"),
        P(None, "tensor", None),
        P(None, None, "tensor"),
        P(("groups", "dp")),
        P(),
        P(),
    )
    return jax.shard_map(
        functools.partial(per_device, mesh.shape["tensor"], mesh.shape["dp"]),
        mesh=mesh,
        in_specs=placed,
        out_specs=(
            P(("groups", "dp"), "tensor"),
            P(("groups", "dp"), "tensor", None),
            P(("groups", "dp"), None, "tensor"),
        ),
        check_vma=False,
    )
```

```python
import functools

import jax
import jax.numpy as jnp
from jax import lax
from jax.experimental import pallas as pl
from jax.experimental.pallas import tpu as pltpu
from jax.sharding import PartitionSpec as P

adapter_alpha = 32.0
row_block = 128
bf16 = jnp.bfloat16
f32 = jnp.float32
contract_last = (((1,), (1,)), ((), ()))
contract_first = (((0,), (0,)), ((), ()))
vmem_bytes = 40 * 1024 * 1024
declared = pl.CostEstimate(flops=10**12, bytes_accessed=10**9, transcendentals=0)


def params():
    return pltpu.CompilerParams(vmem_limit_bytes=vmem_bytes)


def product_kernel(add_count, block_count, *refs):
    position = 1
    rows, weights = refs[1], refs[2]
    position = 3
    total = lax.dot_general(
        rows[...], weights[...], contract_last, preferred_element_type=f32
    )
    for _ in range(add_count):
        total = total + refs[position][...].astype(f32)
        position += 1
    if block_count:
        low = refs[position]
        position += 1
        terms = []
        for i in range(block_count):
            terms.append(
                lax.dot_general(
                    low[i * row_block : (i + 1) * row_block, :],
                    refs[position][0],
                    contract_last,
                    preferred_element_type=f32,
                )
            )
            position += 1
        total = total + jnp.concatenate(terms, axis=0)
    refs[-1][...] = total.astype(refs[-1].dtype)


def product(scalars, gradient, weights, piece, piece_rows, width, adds, link, adapter=None):
    depth = gradient.shape[1]
    tile = min(width, 512)
    while width % tile:
        tile //= 2
    steps = width // tile
    in_specs = [
        pl.BlockSpec((piece_rows, depth), lambda j, s: (piece, 0)),
        pl.BlockSpec((tile, depth), lambda j, s: (s[0] * steps + j, 0)),
    ]
    operands = [gradient, weights]
    for array, shifted in adds:
        if shifted:
            in_specs.append(
                pl.BlockSpec((piece_rows, tile), lambda j, s: (0, s[1] * steps + j))
            )
        else:
            in_specs.append(pl.BlockSpec((piece_rows, tile), lambda j, s: (0, j)))
        operands.append(array)
    block_count = 0
    if adapter is not None:
        low, shrink = adapter
        rank = low.shape[1]
        block_count = piece_rows // row_block
        in_specs.append(pl.BlockSpec((piece_rows, rank), lambda j, s: (piece, 0)))
        operands.append(low)
        for i in range(block_count):
            in_specs.append(
                pl.BlockSpec((1, tile, rank), functools.partial(lambda j, s, i: (s[2 + i], j, 0), i=i))
            )
            operands.append(shrink)
    for array in link:
        in_specs.append(pl.BlockSpec(memory_space=pl.ANY))
        operands.append(array)
    return pl.pallas_call(
        functools.partial(product_kernel, len(adds), block_count),
        grid_spec=pltpu.PrefetchScalarGridSpec(
            num_scalar_prefetch=1,
            grid=(steps,),
            in_specs=in_specs,
            out_specs=pl.BlockSpec((piece_rows, tile), lambda j, s: (0, j)),
        ),
        out_shape=jax.ShapeDtypeStruct((piece_rows, width), bf16),
        compiler_params=params(),
        cost_estimate=declared,
    )(scalars, *operands)


def low_kernel(tenants, rows, expand, link, out):
    out[...] = lax.dot_general(
        rows[...], expand[0], contract_last, preferred_element_type=f32
    ).astype(out.dtype)


def low_product(tenants, gradient, expand, link):
    count_of_rows, depth = gradient.shape
    rank = expand.shape[1]
    blocks = count_of_rows // row_block
    return pl.pallas_call(
        low_kernel,
        grid_spec=pltpu.PrefetchScalarGridSpec(
            num_scalar_prefetch=1,
            grid=(blocks,),
            in_specs=[
                pl.BlockSpec((row_block, depth), lambda b, s: (b, 0)),
                pl.BlockSpec((1, rank, depth), lambda b, s: (s[b], 0, 0)),
                pl.BlockSpec(memory_space=pl.ANY),
            ],
            out_specs=pl.BlockSpec((row_block, rank), lambda b, s: (b, 0)),
        ),
        out_shape=jax.ShapeDtypeStruct((count_of_rows, rank), bf16),
        compiler_params=params(),
        cost_estimate=declared,
    )(tenants, gradient, expand, link)


def factor_kernel(slots_each, blocks, slots, scales, left, right, link, own, other, other_sum):
    own[...] = jnp.zeros_like(own)
    other_sum[...] = jnp.zeros_like(other_sum)
    for b in range(blocks):
        here = pl.ds(b * row_block, row_block)
        piece = lax.dot_general(
            left[here, :], right[here, :], contract_first, preferred_element_type=f32
        )
        piece = piece * scales[b]
        slot = slots[b]

        @pl.when(slot < slots_each)
        def _():
            own[slot] += piece

        @pl.when(slot >= slots_each)
        def _():
            other_sum[slot - slots_each] += piece

    other[...] = other_sum[...].astype(other.dtype)


def factor_sums(slots, scales, left, right, slots_each, others, link):
    count_of_rows, height = left.shape
    width = right.shape[1]
    blocks = count_of_rows // row_block
    whole = pl.BlockSpec(memory_space=pltpu.VMEM)
    return pl.pallas_call(
        functools.partial(factor_kernel, slots_each, blocks),
        in_specs=[
            pl.BlockSpec(memory_space=pltpu.SMEM),
            pl.BlockSpec(memory_space=pltpu.SMEM),
            whole,
            whole,
            pl.BlockSpec(memory_space=pl.ANY),
        ],
        out_specs=[whole, whole],
        out_shape=[
            jax.ShapeDtypeStruct((slots_each, height, width), f32),
            jax.ShapeDtypeStruct((others, height, width), bf16),
        ],
        scratch_shapes=[pltpu.VMEM((others, height, width), f32)],
        compiler_params=params(),
        cost_estimate=declared,
    )(slots, scales, left, right, link)


def per_device(
    tensor_count,
    owner_count,
    gradient,
    projection_input,
    saved_lowrank,
    weights,
    shrink,
    expand,
    tenant_per_block,
    tenant_adapter_rank,
    tenant_owner_index,
):
    count_of_rows, width = gradient.shape
    blocks = count_of_rows // row_block
    tenants = tenant_adapter_rank.shape[0]
    rank_extent = shrink.shape[2]
    nodes = tensor_count // 2
    last = nodes - 1
    place = lax.axis_index("tensor")
    node = place // 2
    side = place % 2
    owner = lax.axis_index("dp")

    halves = 1
    pieces = 2 * halves
    piece_rows = count_of_rows // pieces
    lower = list(range(halves))
    upper = list(range(halves, pieces))

    link = []

    def run(scalars, piece, columns, adds, adapter=None):
        out = product(
            jnp.stack([jnp.asarray(v, jnp.int32) for v in scalars]),
            gradient, weights, piece, piece_rows, columns, adds, link, adapter,
        )
        link[:] = [out]
        return out

    def swap(x, active):
        pairs = []
        for z in active:
            pairs += [(2 * z, 2 * z + 1), (2 * z + 1, 2 * z)]
        return lax.ppermute(x, "tensor", pairs)

    def along(x, hops):
        pairs = [(2 * a + y, 2 * b + y) for a, b in hops for y in range(2)]
        return lax.ppermute(x, "tensor", pairs)

    def tasks(step, lag):
        reach = step - lag
        right = [z for z in range(nodes) if z <= reach and z < last]
        left = [z for z in range(nodes) if z >= last - reach and z > 0]
        to_right = jnp.clip(last - step + node, 0, last)
        to_left = jnp.clip(node - (last - step), 0, last)
        right_hops = [(z, z + 1) for z in right]
        left_hops = [(z, z - 1) for z in left]
        if not set(right) & set(left):
            both = jnp.where(node <= reach, to_right, to_left)
            return [(right + left, both, right_hops, left_hops)]
        return [(right, to_right, right_hops, []), (left, to_left, [], left_hops)]

    def forward(x, right_hops, left_hops):
        targets = [b for _, b in right_hops + left_hops]
        if right_hops and left_hops and len(set(targets)) == len(targets):
            both = along(x, right_hops + left_hops)
            return (both, both)
        return (
            along(x, right_hops) if right_hops else None,
            along(x, left_hops) if left_hops else None,
        )

    def addends(arrived, right_hops, left_hops):
        found = []
        if arrived is None:
            return found
        if right_hops and arrived[0] is not None:
            found.append(arrived[0])
        if left_hops and arrived[1] is not None and not (found and found[0] is arrived[1]):
            found.append(arrived[1])
        return found

    class Flow:
        def __init__(self, piece_ids, lag):
            self.piece_ids, self.lag = piece_ids, lag
            self.arrived = {p: None for p in piece_ids}
            self.swapped = {}

        def has(self, step):
            return self.lag <= step <= last - 1

        def swap(self, step):
            if not self.has(step):
                return
            for t, (active, dest, _, _) in enumerate(tasks(step, self.lag)):
                for p in self.piece_ids:
                    part = run([dest * 2 + (1 - side), 0], p, width, [])
                    self.swapped[step, t, p] = swap(part, active)

        def combine(self, step, p):
            if not self.has(step):
                return
            before = self.arrived[p]
            found = [None, None]
            for t, (active, dest, right_hops, left_hops) in enumerate(tasks(step, self.lag)):
                adds = [(self.swapped[step, t, p], False)]
                adds += [(a, False) for a in addends(before, right_hops, left_hops)]
                part = run([dest * 2 + side, 0], p, width, adds)
                got = forward(part, right_hops, left_hops)
                if right_hops:
                    found[0] = got[0]
                if left_hops:
                    found[1] = got[1]
            self.arrived[p] = tuple(found)

    class DirectFlow:
        def __init__(self):
            self.arrived = {p: None for p in lower}

        def advance(self, step, p):
            if step > last - 1:
                return
            dest = jnp.where(node == step, last, 0)
            adds = [] if self.arrived[p] is None else [(self.arrived[p], False)]
            part = run([dest, 0], p, 2 * width, adds)
            self.arrived[p] = along(part, [(step, step + 1), (last - step, last - step - 1)])

    low_flow = Flow(lower, 1)
    up_flow = Flow(upper, 0)
    direct = DirectFlow()

    tenant_ids = jnp.arange(tenants, dtype=jnp.int32)
    matches = tenant_per_block[:, None] == tenant_ids[None, :]
    rank_per_block = jnp.sum(jnp.where(matches, tenant_adapter_rank[None, :], 0), axis=1).astype(f32)
    scale_per_block = adapter_alpha / rank_per_block
    block_mask = (jnp.arange(rank_extent).astype(f32)[None, :] < rank_per_block[:, None]).astype(f32)
    key = tenant_owner_index * tenants + tenant_ids
    slot_of = jnp.sum((key[None, :] < key[:, None]).astype(jnp.int32), axis=1)
    block_slot = jnp.sum(jnp.where(matches, slot_of[None, :], 0), axis=1)
    slots_each = tenants // owner_count
    own_first = lax.rem(block_slot - owner * slots_each + tenants, tenants)

    own_swap = {}

    def swap_own(p):
        adds = [(direct.arrived[p], True)] if p in lower else []
        part = run([node * 2 + (1 - side), 1 - side], p, width, adds)
        own_swap[p] = swap(part, range(nodes))

    direct.advance(0, lower[0])
    up_flow.swap(0)
    low_flow.swap(1)
    up_flow.swap(1)
    low_flow.swap(2)

    low_part = low_product(tenant_per_block, gradient, expand, link[0])
    link[:] = [low_part]
    low_whole = lax.psum(low_part, "tensor")
    factor = scale_per_block[:, None, None] * block_mask[:, None, :]
    low = (low_whole.astype(f32).reshape(blocks, row_block, rank_extent) * factor).astype(bf16)
    low = low.reshape(count_of_rows, rank_extent)

    for p in upper:
        up_flow.combine(0, p)
    up_flow.swap(2)

    masked = saved_lowrank.reshape(blocks, row_block, rank_extent) * block_mask[:, None, :].astype(bf16)
    masked = masked.reshape(count_of_rows, rank_extent)
    others = slots_each * (owner_count - 1)
    ones = jnp.ones_like(scale_per_block)

    def exchange(own, other):
        total = own
        for hop in range(1, owner_count):
            theirs = other[(hop - 1) * slots_each : hop * slots_each]
            pairs = [(i, (i + hop) % owner_count) for i in range(owner_count)]
            total = total + lax.ppermute(theirs, "dp", pairs).astype(f32)
        return total

    own, other = factor_sums(
        own_first, scale_per_block, masked, gradient, slots_each, others, link[0]
    )
    link[:] = [other]
    grad_expand = exchange(own, other)

    for step in range(1, last):
        direct.advance(step, lower[0])
        for p in lower:
            low_flow.combine(step, p)
        up_flow.swap(step + 2)
        low_flow.swap(step + 2)
        if step == last - 1:
            for p in upper:
                swap_own(p)
        for p in upper:
            up_flow.combine(step, p)
    own, other = factor_sums(
        own_first, ones, projection_input, low, slots_each, others, link[0]
    )
    link[:] = [other]
    grad_shrink = exchange(own, other)
    link.append(grad_expand)
    link += [own_swap[p] for p in upper]
    for p in lower:
        link += [a for a in low_flow.arrived[p]]
    for p in lower:
        swap_own(p)
    link.append(grad_shrink)

    outs = {}
    for p in upper + lower:
        flow = low_flow if p in lower else up_flow
        adds = [(own_swap[p], False)]
        if p in lower:
            adds.append((direct.arrived[p], True))
        arrived = flow.arrived[p]
        adds.append((arrived[0], False))
        if arrived[1] is not arrived[0]:
            adds.append((arrived[1], False))
        in_piece = piece_rows // row_block
        ids = [tenant_per_block[p * in_piece + i] for i in range(in_piece)]
        outs[p] = run([node * 2 + side, side] + ids, p, width, adds, (low, shrink))
    input_gradient = jnp.concatenate([outs[p] for p in range(pieces)], axis=0)
    return (input_gradient, grad_shrink, grad_expand)


def solution(mesh):
    placed = (
        P(("groups", "dp"), "tensor"),
        P(("groups", "dp"), "tensor"),
        P(("groups", "dp"), None),
        P(None, "tensor"),
        P(None, "tensor", None),
        P(None, None, "tensor"),
        P(("groups", "dp")),
        P(),
        P(),
    )
    return jax.shard_map(
        functools.partial(per_device, mesh.shape["tensor"], mesh.shape["dp"]),
        mesh=mesh,
        in_specs=placed,
        out_specs=(
            P(("groups", "dp"), "tensor"),
            P(("groups", "dp"), "tensor", None),
            P(("groups", "dp"), None, "tensor"),
        ),
        check_vma=False,
    )
```

```python
import functools

import jax
import jax.numpy as jnp
from jax import lax
from jax.experimental import pallas as pl
from jax.experimental.pallas import tpu as pltpu
from jax.sharding import PartitionSpec as P

adapter_alpha = 32.0
row_block = 128
bf16 = jnp.bfloat16
f32 = jnp.float32
contract_last = (((1,), (1,)), ((), ()))
contract_first = (((0,), (0,)), ((), ()))
vmem_bytes = 40 * 1024 * 1024
declared = pl.CostEstimate(flops=10**12, bytes_accessed=10**9, transcendentals=0)


def params():
    return pltpu.CompilerParams(vmem_limit_bytes=vmem_bytes)


def product_kernel(add_count, block_count, *refs):
    position = 1
    rows, weights = refs[1], refs[2]
    position = 3
    total = lax.dot_general(
        rows[...], weights[...], contract_last, preferred_element_type=f32
    )
    for _ in range(add_count):
        total = total + refs[position][...].astype(f32)
        position += 1
    if block_count:
        low = refs[position]
        position += 1
        terms = []
        for i in range(block_count):
            terms.append(
                lax.dot_general(
                    low[i * row_block : (i + 1) * row_block, :],
                    refs[position][0],
                    contract_last,
                    preferred_element_type=f32,
                )
            )
            position += 1
        total = total + jnp.concatenate(terms, axis=0)
    refs[-1][...] = total.astype(refs[-1].dtype)


def product(scalars, gradient, weights, piece, piece_rows, width, adds, link, adapter=None, whole=None):
    depth = gradient.shape[1]
    tile = min(width, 512)
    while width % tile:
        tile //= 2
    steps = width // tile
    in_specs = [
        pl.BlockSpec((piece_rows, depth), lambda j, s: (piece, 0)),
        pl.BlockSpec((tile, depth), lambda j, s: (s[0] * steps + j, 0)),
    ]
    operands = [gradient, weights]
    for array in adds:
        in_specs.append(pl.BlockSpec((piece_rows, tile), lambda j, s: (0, j)))
        operands.append(array)
    block_count = 0
    if adapter is not None:
        low, shrink = adapter
        rank = low.shape[1]
        block_count = piece_rows // row_block
        in_specs.append(pl.BlockSpec((piece_rows, rank), lambda j, s: (piece, 0)))
        operands.append(low)
        for i in range(block_count):
            in_specs.append(
                pl.BlockSpec((1, tile, rank), functools.partial(lambda j, s, i: (s[1 + i], j, 0), i=i))
            )
            operands.append(shrink)
    for array in link:
        in_specs.append(pl.BlockSpec(memory_space=pl.ANY))
        operands.append(array)
    out_piece, out_rows, aliases = 0, piece_rows, {}
    if adapter is not None:
        out_piece, out_rows = piece, gradient.shape[0]
        if whole is not None:
            in_specs.append(pl.BlockSpec(memory_space=pl.ANY))
            operands.append(whole)
            aliases = {len(operands): 0}
    return pl.pallas_call(
        functools.partial(product_kernel, len(adds), block_count),
        grid_spec=pltpu.PrefetchScalarGridSpec(
            num_scalar_prefetch=1,
            grid=(steps,),
            in_specs=in_specs,
            out_specs=pl.BlockSpec((piece_rows, tile), lambda j, s: (out_piece, j)),
        ),
        out_shape=jax.ShapeDtypeStruct((out_rows, width), bf16),
        input_output_aliases=aliases,
        compiler_params=params(),
        cost_estimate=declared,
    )(scalars, *operands)


def low_kernel(tenants, rows, expand, link, out):
    out[...] = lax.dot_general(
        rows[...], expand[0], contract_last, preferred_element_type=f32
    ).astype(out.dtype)


def low_product(tenants, gradient, expand, link):
    count_of_rows, depth = gradient.shape
    rank = expand.shape[1]
    blocks = count_of_rows // row_block
    return pl.pallas_call(
        low_kernel,
        grid_spec=pltpu.PrefetchScalarGridSpec(
            num_scalar_prefetch=1,
            grid=(blocks,),
            in_specs=[
                pl.BlockSpec((row_block, depth), lambda b, s: (b, 0)),
                pl.BlockSpec((1, rank, depth), lambda b, s: (s[b], 0, 0)),
                pl.BlockSpec(memory_space=pl.ANY),
            ],
            out_specs=pl.BlockSpec((row_block, rank), lambda b, s: (b, 0)),
        ),
        out_shape=jax.ShapeDtypeStruct((count_of_rows, rank), bf16),
        compiler_params=params(),
        cost_estimate=declared,
    )(tenants, gradient, expand, link)


def scale_kernel(ranks, scales, low, link, out):
    columns = lax.broadcasted_iota(jnp.int32, (row_block, low.shape[1]), 1)
    for b in range(low.shape[0] // row_block):
        here = pl.ds(b * row_block, row_block)
        kept = jnp.where(columns < ranks[b], low[here, :].astype(f32) * scales[b], 0.0)
        out[here, :] = kept.astype(out.dtype)


def scaled_low(ranks, scales, low, link):
    whole = pl.BlockSpec(memory_space=pltpu.VMEM)
    return pl.pallas_call(
        scale_kernel,
        in_specs=[
            pl.BlockSpec(memory_space=pltpu.SMEM),
            pl.BlockSpec(memory_space=pltpu.SMEM),
            whole,
            pl.BlockSpec(memory_space=pl.ANY),
        ],
        out_specs=whole,
        out_shape=jax.ShapeDtypeStruct(low.shape, bf16),
        compiler_params=params(),
        cost_estimate=declared,
    )(ranks, scales, low, link)


def factor_kernel(slots_each, blocks, sources, slots, scales, *refs):
    own = refs[-1]
    own[...] = jnp.zeros_like(own)
    for source in range(sources):
        left, right = refs[2 * source], refs[2 * source + 1]
        for b in range(blocks):
            entry = source * blocks + b
            slot = slots[entry]

            @pl.when(slot < slots_each)
            def _():
                here = pl.ds(b * row_block, row_block)
                piece = lax.dot_general(
                    left[here, :], right[here, :], contract_first, preferred_element_type=f32
                )
                own[slot] += piece * scales[entry]


def factor_sums(slots, scales, sides, slots_each, link):
    count_of_rows, height = sides[0].shape
    width = sides[1].shape[1]
    blocks = count_of_rows // row_block
    whole = pl.BlockSpec(memory_space=pltpu.VMEM)
    return pl.pallas_call(
        functools.partial(factor_kernel, slots_each, blocks, len(sides) // 2),
        in_specs=[pl.BlockSpec(memory_space=pltpu.SMEM)] * 2
        + [whole] * len(sides)
        + [pl.BlockSpec(memory_space=pl.ANY)] * len(link),
        out_specs=whole,
        out_shape=jax.ShapeDtypeStruct((slots_each, height, width), f32),
        compiler_params=params(),
        cost_estimate=declared,
    )(slots, scales, *sides, *link)


def per_device(
    tensor_count,
    owner_count,
    gradient,
    projection_input,
    saved_lowrank,
    weights,
    shrink,
    expand,
    tenant_per_block,
    tenant_adapter_rank,
    tenant_owner_index,
):
    count_of_rows, width = gradient.shape
    blocks = count_of_rows // row_block
    tenants = tenant_adapter_rank.shape[0]
    rank_extent = shrink.shape[2]
    nodes = tensor_count // 2
    last = nodes - 1
    place = lax.axis_index("tensor")
    node = place // 2
    side = place % 2
    owner = lax.axis_index("dp")

    halves = 1
    pieces = 2 * halves
    piece_rows = count_of_rows // pieces
    lower = list(range(halves))
    upper = list(range(halves, pieces))

    link = []

    def run(scalars, piece, columns, adds, adapter=None, whole=None):
        out = product(
            jnp.stack([jnp.asarray(v, jnp.int32) for v in scalars]),
            gradient, weights, piece, piece_rows, columns, adds, link, adapter, whole,
        )
        link[:] = [out]
        return out

    def swap(x, active):
        pairs = []
        for z in active:
            pairs += [(2 * z, 2 * z + 1), (2 * z + 1, 2 * z)]
        return lax.ppermute(x, "tensor", pairs)

    def along(x, hops):
        pairs = [(2 * a + y, 2 * b + y) for a, b in hops for y in range(2)]
        return lax.ppermute(x, "tensor", pairs)

    def tasks(step, lag):
        reach = step - lag
        right = [z for z in range(nodes) if z <= reach and z < last]
        left = [z for z in range(nodes) if z >= last - reach and z > 0]
        to_right = jnp.clip(last - step + node, 0, last)
        to_left = jnp.clip(node - (last - step), 0, last)
        right_hops = [(z, z + 1) for z in right]
        left_hops = [(z, z - 1) for z in left]
        if not set(right) & set(left):
            both = jnp.where(node <= reach, to_right, to_left)
            return [(right + left, both, right_hops, left_hops)]
        return [(right, to_right, right_hops, []), (left, to_left, [], left_hops)]

    def forward(x, right_hops, left_hops):
        targets = [b for _, b in right_hops + left_hops]
        if right_hops and left_hops and len(set(targets)) == len(targets):
            both = along(x, right_hops + left_hops)
            return (both, both)
        return (
            along(x, right_hops) if right_hops else None,
            along(x, left_hops) if left_hops else None,
        )

    def addends(arrived, right_hops, left_hops):
        found = []
        if arrived is None:
            return found
        if right_hops and arrived[0] is not None:
            found.append(arrived[0])
        if left_hops and arrived[1] is not None and not (found and found[0] is arrived[1]):
            found.append(arrived[1])
        return found

    class Flow:
        def __init__(self, piece_ids, lag):
            self.piece_ids, self.lag = piece_ids, lag
            self.arrived = {p: None for p in piece_ids}
            self.swapped = {}

        def has(self, step):
            return self.lag <= step <= last - 1

        def swap(self, step):
            if not self.has(step):
                return
            for t, (active, dest, _, _) in enumerate(tasks(step, self.lag)):
                for p in self.piece_ids:
                    part = run([dest * 2 + (1 - side)], p, width, [])
                    self.swapped[step, t, p] = swap(part, active)

        def combine(self, step, p):
            if not self.has(step):
                return
            before = self.arrived[p]
            found = [None, None]
            for t, (active, dest, right_hops, left_hops) in enumerate(tasks(step, self.lag)):
                adds = [self.swapped[step, t, p]] + addends(before, right_hops, left_hops)
                part = run([dest * 2 + side], p, width, adds)
                got = forward(part, right_hops, left_hops)
                if right_hops:
                    found[0] = got[0]
                if left_hops:
                    found[1] = got[1]
            self.arrived[p] = tuple(found)

    class DirectFlow:
        def __init__(self):
            self.arrived = {(p, part): None for p in lower for part in (0, 1)}

        def advance(self, step, part):
            if step > last - 1:
                return
            dest = jnp.where(node == step, last, 0)
            column = side if part else 1 - side
            for p in lower:
                before = self.arrived[p, part]
                adds = [] if before is None else [before]
                out = run([dest * 2 + column], p, width, adds)
                self.arrived[p, part] = along(
                    out, [(step, step + 1), (last - step, last - step - 1)]
                )

    low_flow = Flow(lower, 1)
    up_flow = Flow(upper, 0)
    direct = DirectFlow()

    def from_owners(x):
        found = [x]
        for hop in range(1, owner_count):
            pairs = [(i, (i + hop) % owner_count) for i in range(owner_count)]
            found.append(lax.ppermute(x, "dp", pairs))
        return found

    block_tenants = jnp.concatenate(from_owners(tenant_per_block))
    tenant_ids = jnp.arange(tenants, dtype=jnp.int32)
    matches = block_tenants[:, None] == tenant_ids[None, :]
    block_ranks = jnp.sum(jnp.where(matches, tenant_adapter_rank[None, :], 0), axis=1)
    block_scales = adapter_alpha / block_ranks.astype(f32)
    key = tenant_owner_index * tenants + tenant_ids
    slot_of = jnp.sum((key[None, :] < key[:, None]).astype(jnp.int32), axis=1)
    slots_each = tenants // owner_count
    slot_here = lax.rem(slot_of - owner * slots_each + tenants, tenants)
    block_slots = jnp.sum(jnp.where(matches, slot_here[None, :], 0), axis=1)

    own_swap = {}

    def swap_own(p):
        adds = [direct.arrived[p, 0]] if p in lower else []
        part = run([node * 2 + (1 - side)], p, width, adds)
        own_swap[p] = swap(part, range(nodes))

    def adapter_space():
        part = low_product(tenant_per_block, gradient, expand, link[0])
        link[:] = [part]
        return lax.psum(jnp.concatenate(from_owners(part)), "tensor")

    def expand_gradient():
        ranks = block_ranks[:blocks]
        kept = jnp.arange(rank_extent, dtype=jnp.int32)[None, :] < ranks[:, None]
        saved = saved_lowrank.reshape(blocks, row_block, rank_extent)
        saved = saved * kept[:, None, :].astype(bf16)
        saved = from_owners(saved.reshape(count_of_rows, rank_extent))
        sides = [a for pair in zip(saved, from_owners(gradient)) for a in pair]
        out = factor_sums(block_slots, block_scales, sides, slots_each, link)
        link[:] = [out]
        return out

    def shrink_gradient(low):
        inputs = from_owners(projection_input)
        lows = [low[i * count_of_rows : (i + 1) * count_of_rows] for i in range(owner_count)]
        sides = [a for pair in zip(inputs, lows) for a in pair]
        out = factor_sums(
            block_slots, jnp.ones_like(block_scales), sides, slots_each, link
        )
        link[:] = [out]
        return out

    direct.advance(0, 0)
    up_flow.swap(0)
    direct.advance(0, 1)
    low_flow.swap(1)
    low_whole = adapter_space()
    direct.advance(1, 0)
    for p in upper:
        up_flow.combine(0, p)
    up_flow.swap(1)
    low_flow.swap(2)
    grad_expand = expand_gradient()
    direct.advance(1, 1)

    for step in range(1, last):
        direct.advance(step + 1, 0)
        for p in lower:
            low_flow.combine(step, p)
        if step == last - 1:
            for p in lower:
                swap_own(p)
        up_flow.swap(step + 1)
        for p in upper:
            up_flow.combine(step, p)
        direct.advance(step + 1, 1)
        low_flow.swap(step + 2)
        if step == last - 2:
            for p in upper:
                swap_own(p)

    low = scaled_low(block_ranks, block_scales, low_whole, link[0])
    link[:] = [low] + [direct.arrived[p, 1] for p in lower]
    link += [a for p in lower for a in low_flow.arrived[p]]
    link += [own_swap[p] for p in upper]
    grad_shrink = shrink_gradient(low)

    input_gradient = None
    for p in lower + upper:
        flow = low_flow if p in lower else up_flow
        adds = [own_swap[p]]
        if p in lower:
            adds.append(direct.arrived[p, 1])
        arrived = flow.arrived[p]
        adds.append(arrived[0])
        if arrived[1] is not arrived[0]:
            adds.append(arrived[1])
        in_piece = piece_rows // row_block
        ids = [tenant_per_block[p * in_piece + i] for i in range(in_piece)]
        input_gradient = run(
            [node * 2 + side] + ids, p, width, adds, (low, shrink), input_gradient
        )
    return (input_gradient, grad_shrink, grad_expand)


def solution(mesh):
    placed = (
        P(("groups", "dp"), "tensor"),
        P(("groups", "dp"), "tensor"),
        P(("groups", "dp"), None),
        P(None, "tensor"),
        P(None, "tensor", None),
        P(None, None, "tensor"),
        P(("groups", "dp")),
        P(),
        P(),
    )
    return jax.shard_map(
        functools.partial(per_device, mesh.shape["tensor"], mesh.shape["dp"]),
        mesh=mesh,
        in_specs=placed,
        out_specs=(
            P(("groups", "dp"), "tensor"),
            P(("groups", "dp"), "tensor", None),
            P(("groups", "dp"), None, "tensor"),
        ),
        check_vma=False,
    )
```

```python
import functools

import jax
import jax.numpy as jnp
from jax import lax
from jax.experimental import pallas as pl
from jax.experimental.pallas import tpu as pltpu
from jax.sharding import PartitionSpec as P

adapter_alpha = 32.0
row_block = 128
bf16 = jnp.bfloat16
f32 = jnp.float32
contract_last = (((1,), (1,)), ((), ()))
contract_first = (((0,), (0,)), ((), ()))
vmem_bytes = 40 * 1024 * 1024
declared = pl.CostEstimate(flops=10**12, bytes_accessed=10**9, transcendentals=0)


def params():
    return pltpu.CompilerParams(vmem_limit_bytes=vmem_bytes)


def product_kernel(modes, block_count, *refs):
    position = 1
    rows, weights = refs[1], refs[2]
    position = 3
    total = lax.dot_general(
        rows[...], weights[...], contract_last, preferred_element_type=f32
    )
    for mode in modes:
        addend = refs[position][...].astype(f32)
        if mode:
            addend = addend * refs[0][1 + mode].astype(f32)
        total = total + addend
        position += 1
    if block_count:
        low = refs[position]
        position += 1
        terms = []
        for i in range(block_count):
            terms.append(
                lax.dot_general(
                    low[i * row_block : (i + 1) * row_block, :],
                    refs[position][0],
                    contract_last,
                    preferred_element_type=f32,
                )
            )
            position += 1
        total = total + jnp.concatenate(terms, axis=0)
    refs[-1][...] = total.astype(refs[-1].dtype)


def product(scalars, gradient, weights, piece, piece_rows, width, adds, link, adapter=None, whole=None):
    depth = gradient.shape[1]
    tile = min(width, 512)
    while width % tile:
        tile //= 2
    steps = width // tile
    in_specs = [
        pl.BlockSpec((piece_rows, depth), lambda j, s: (s[1], 0)),
        pl.BlockSpec((tile, depth), lambda j, s: (s[0] * steps + j, 0)),
    ]
    operands = [gradient, weights]
    for array, _ in adds:
        in_specs.append(pl.BlockSpec((piece_rows, tile), lambda j, s: (0, j)))
        operands.append(array)
    block_count = 0
    if adapter is not None:
        low, shrink = adapter
        rank = low.shape[1]
        block_count = piece_rows // row_block
        in_specs.append(pl.BlockSpec((piece_rows, rank), lambda j, s: (piece, 0)))
        operands.append(low)
        for i in range(block_count):
            in_specs.append(
                pl.BlockSpec((1, tile, rank), functools.partial(lambda j, s, i: (s[4 + i], j, 0), i=i))
            )
            operands.append(shrink)
    for array in link:
        in_specs.append(pl.BlockSpec(memory_space=pl.ANY))
        operands.append(array)
    out_piece, out_rows, aliases = 0, piece_rows, {}
    if adapter is not None:
        out_piece, out_rows = piece, gradient.shape[0]
        if whole is not None:
            in_specs.append(pl.BlockSpec(memory_space=pl.ANY))
            operands.append(whole)
            aliases = {len(operands): 0}
    return pl.pallas_call(
        functools.partial(product_kernel, tuple(mode for _, mode in adds), block_count),
        grid_spec=pltpu.PrefetchScalarGridSpec(
            num_scalar_prefetch=1,
            grid=(steps,),
            in_specs=in_specs,
            out_specs=pl.BlockSpec((piece_rows, tile), lambda j, s: (out_piece, j)),
        ),
        out_shape=jax.ShapeDtypeStruct((out_rows, width), bf16),
        input_output_aliases=aliases,
        compiler_params=params(),
        cost_estimate=declared,
    )(scalars, *operands)


def low_kernel(tenants, rows, expand, link, out):
    out[...] = lax.dot_general(
        rows[...], expand[0], contract_last, preferred_element_type=f32
    ).astype(out.dtype)


def low_product(tenants, gradient, expand, link):
    count_of_rows, depth = gradient.shape
    rank = expand.shape[1]
    return pl.pallas_call(
        low_kernel,
        grid_spec=pltpu.PrefetchScalarGridSpec(
            num_scalar_prefetch=1,
            grid=(count_of_rows // row_block,),
            in_specs=[
                pl.BlockSpec((row_block, depth), lambda b, s: (b, 0)),
                pl.BlockSpec((1, rank, depth), lambda b, s: (s[b], 0, 0)),
                pl.BlockSpec(memory_space=pl.ANY),
            ],
            out_specs=pl.BlockSpec((row_block, rank), lambda b, s: (b, 0)),
        ),
        out_shape=jax.ShapeDtypeStruct((count_of_rows, rank), bf16),
        compiler_params=params(),
        cost_estimate=declared,
    )(tenants, gradient, expand, link)


def scale_kernel(ranks, scales, low, link, out):
    columns = lax.broadcasted_iota(jnp.int32, (row_block, low.shape[1]), 1)
    for b in range(low.shape[0] // row_block):
        here = pl.ds(b * row_block, row_block)
        kept = jnp.where(columns < ranks[b], low[here, :].astype(f32) * scales[b], 0.0)
        out[here, :] = kept.astype(out.dtype)


def scaled_low(ranks, scales, low, link):
    whole = pl.BlockSpec(memory_space=pltpu.VMEM)
    return pl.pallas_call(
        scale_kernel,
        in_specs=[pl.BlockSpec(memory_space=pltpu.SMEM)] * 2
        + [whole, pl.BlockSpec(memory_space=pl.ANY)],
        out_specs=whole,
        out_shape=jax.ShapeDtypeStruct(low.shape, bf16),
        compiler_params=params(),
        cost_estimate=declared,
    )(ranks, scales, low, link)


def factor_kernel(slots_each, slots, scales, left, right, *refs):
    own = refs[-1]
    own[...] = jnp.zeros_like(own)
    for b in range(left.shape[0] // row_block):
        slot = slots[b]

        @pl.when(slot < slots_each)
        def _():
            here = pl.ds(b * row_block, row_block)
            piece = lax.dot_general(
                left[here, :], right[here, :], contract_first, preferred_element_type=f32
            )
            own[slot] += piece * scales[b]


def factor_sums(slots, scales, left, right, slots_each, link):
    whole = pl.BlockSpec(memory_space=pltpu.VMEM)
    return pl.pallas_call(
        functools.partial(factor_kernel, slots_each),
        in_specs=[pl.BlockSpec(memory_space=pltpu.SMEM)] * 2
        + [whole] * 2
        + [pl.BlockSpec(memory_space=pl.ANY)] * len(link),
        out_specs=whole,
        out_shape=jax.ShapeDtypeStruct((slots_each, left.shape[1], right.shape[1]), f32),
        compiler_params=params(),
        cost_estimate=declared,
    )(slots, scales, left, right, *link)


def per_device(
    owner_count,
    gradient,
    projection_input,
    saved_lowrank,
    weights,
    shrink,
    expand,
    tenant_per_block,
    tenant_adapter_rank,
    tenant_owner_index,
):
    count_of_rows, width = gradient.shape
    blocks = count_of_rows // row_block
    tenants = tenant_adapter_rank.shape[0]
    rank_extent = shrink.shape[2]
    node = lax.axis_index("tensor") // 2
    side = lax.axis_index("tensor") % 2
    owner = lax.axis_index("dp")
    at_end = (node == 0) | (node == 3)
    piece_rows = count_of_rows // 2
    lower, upper = 0, 1
    link = []

    roles = (at_end, jnp.logical_not(at_end))

    def run(dest, column, piece, adds):
        scalars = (dest * 2 + column, piece) + roles
        scalars = jnp.stack([jnp.asarray(v, jnp.int32) for v in scalars])
        out = product(scalars, gradient, weights, None, piece_rows, width, adds, link)
        link[:] = [out]
        return out

    def swap(x, active):
        pairs = []
        for z in active:
            pairs += [(2 * z, 2 * z + 1), (2 * z + 1, 2 * z)]
        return lax.ppermute(x, "tensor", pairs)

    def along(x, hops):
        return lax.ppermute(
            x, "tensor", [(2 * a + y, 2 * b + y) for a, b in hops for y in range(2)]
        )

    nodes = 4
    ends, inner, every = (0, 3), (1, 2), (0, 1, 2, 3)
    from_ends = [(0, 1), (3, 2)]
    across = [(1, 2), (2, 1)]
    to_ends = [(1, 0), (2, 3)]
    first_half = node < 2
    far = jnp.where(first_half, 3, 0)
    beyond = jnp.where(first_half, 2, 1)
    nearer = jnp.where(first_half, 1, 2)
    near_end = jnp.where(first_half, 0, 3)
    same, other = side, 1 - side

    def all_owners(x):
        return lax.all_gather(x, "dp", axis=0, tiled=True)

    block_tenants = jnp.zeros((owner_count * blocks,), jnp.int32)
    for hop in range(owner_count):
        pairs = [(i, (i + hop) % owner_count) for i in range(owner_count)]
        theirs = lax.ppermute(tenant_per_block, "dp", pairs) if hop else tenant_per_block
        place = lax.rem(owner - hop + owner_count, owner_count) * blocks
        block_tenants = lax.dynamic_update_slice_in_dim(block_tenants, theirs, place, 0)
    tenant_ids = jnp.arange(tenants, dtype=jnp.int32)
    matches = block_tenants[:, None] == tenant_ids[None, :]
    block_ranks = jnp.sum(jnp.where(matches, tenant_adapter_rank[None, :], 0), axis=1)
    block_scales = adapter_alpha / block_ranks.astype(f32)
    key = tenant_owner_index * tenants + tenant_ids
    slot_of = jnp.sum((key[None, :] < key[:, None]).astype(jnp.int32), axis=1)
    slots_each = tenants // owner_count
    slot_here = lax.rem(slot_of - owner * slots_each + tenants, tenants)
    block_slots = jnp.sum(jnp.where(matches, slot_here[None, :], 0), axis=1)

    own_ranks = lax.dynamic_slice_in_dim(block_ranks, owner * blocks, blocks, 0)
    own_scales = lax.dynamic_slice_in_dim(block_scales, owner * blocks, blocks, 0)

    def adapter_space():
        part = low_product(tenant_per_block, gradient, expand, link[0])
        link[:] = [part]
        return lax.psum(part, "tensor")

    def scale_low(low):
        out = scaled_low(own_ranks, own_scales, low, link[0])
        link[:] = [out]
        return out

    def expand_gradient():
        kept = jnp.arange(rank_extent, dtype=jnp.int32)[None, :] < block_ranks[:, None]
        saved = all_owners(saved_lowrank).reshape(-1, row_block, rank_extent)
        saved = (saved * kept[:, None, :].astype(bf16)).reshape(-1, rank_extent)
        out = factor_sums(
            block_slots, block_scales, saved, all_owners(gradient), slots_each, link
        )
        link[:] = [out]
        return out

    def shrink_gradient(low):
        out = factor_sums(
            block_slots, jnp.ones_like(block_scales), all_owners(projection_input), all_owners(low),
            slots_each, link,
        )
        link[:] = [out]
        return out

    direct_a = along(run(far, other, lower, []), from_ends)
    low_whole = adapter_space()
    y1 = swap(run(jnp.where(at_end, far, near_end), other, upper, []), every)
    direct_b = along(run(far, same, lower, []), from_ends)
    y2 = swap(run(beyond, other, lower, []), ends)
    out = run(
        far,
        jnp.where(at_end, same, other),
        jnp.where(at_end, upper, lower),
        [(y1, 1), (direct_a, 0)],
    )
    upper_1, direct_a = along(out, from_ends), along(out, across)
    y3 = swap(run(jnp.where(at_end, beyond, far), other, upper, []), every)
    out = run(jnp.where(at_end, beyond, far), same, lower, [(y2, 0), (direct_b, 0)])
    lower_2, direct_b = along(out, from_ends), along(out, across)
    y4 = swap(run(jnp.where(at_end, nearer, beyond), other, lower, []), every)
    out = run(
        jnp.where(at_end, beyond, near_end),
        jnp.where(at_end, same, other),
        jnp.where(at_end, upper, lower),
        [(y3, 1), (direct_a, 0)],
    )
    both_3 = along(out, from_ends + to_ends)
    y5 = swap(run(jnp.where(at_end, nearer, beyond), other, upper, []), every)
    upper_far = along(run(far, same, upper, [(y3, 0), (upper_1, 0)]), across)
    out = run(jnp.where(at_end, nearer, near_end), same, lower, [(y4, 1), (direct_b, 0)])
    both_4 = along(out, from_ends + to_ends)
    low = scale_low(low_whole)
    y6 = swap(run(node, other, upper, []), every)
    lower_4 = along(run(beyond, same, lower, [(y4, 0), (lower_2, 0)]), across)
    out = run(
        jnp.where(at_end, nearer, near_end), same, upper, [(y5, 1), (y1, 2), (upper_far, 0)]
    )
    both_5 = along(out, from_ends + to_ends)
    y7 = swap(run(node, other, lower, [(both_3, 1)]), every)
    upper_4 = along(run(beyond, same, upper, [(y5, 0), (both_3, 0)]), across)
    link += [both_4, y6, lower_4]
    grad_expand = expand_gradient()
    grad_shrink = shrink_gradient(low)

    input_gradient = None
    in_piece = piece_rows // row_block
    for piece, adds in (
        (lower, [(y7, 0), (both_4, 0), (lower_4, 0)]),
        (upper, [(y6, 0), (both_5, 0), (upper_4, 0)]),
    ):
        scalars = [node * 2 + side, jnp.int32(piece), jnp.int32(0), jnp.int32(0)]
        scalars += [tenant_per_block[piece * in_piece + i] for i in range(in_piece)]
        input_gradient = product(
            jnp.stack(scalars).astype(jnp.int32),
            gradient, weights, piece, piece_rows, width, adds, link, (low, shrink), input_gradient,
        )
        link[:] = [input_gradient]
    return (input_gradient, grad_shrink, grad_expand)


def per_device_any(
    query_cotangent,
    projection_input,
    saved_lowrank,
    query_matrix,
    adapter_shrink,
    adapter_expand,
    tenant_per_block,
    tenant_adapter_rank,
    tenant_owner_index,
):
    count_of_rows, shard_extent = query_cotangent.shape
    block_count = count_of_rows // 128
    tenant_count = tenant_adapter_rank.shape[0]
    rank_extent = adapter_shrink.shape[2]
    frozen_product = lax.psum_scatter(
        lax.dot_general(
            query_matrix,
            query_cotangent,
            contract_last,
            preferred_element_type=jnp.float32,
        ).astype(jnp.bfloat16),
        "tensor",
        scatter_dimension=0,
        tiled=True,
    ).astype(jnp.float32)
    tenant_ids = jnp.arange(tenant_count, dtype=jnp.int32)
    matches = tenant_per_block[:, None] == tenant_ids[None, :]
    rank_per_block = jnp.sum(jnp.where(matches, tenant_adapter_rank[None, :], 0), axis=1).astype(
        jnp.float32
    )
    scale_per_block = adapter_alpha / rank_per_block
    block_mask = (
        jnp.arange(rank_extent).astype(jnp.float32)[None, :] < rank_per_block[:, None]
    ).astype(jnp.float32)
    gradient_per_block = query_cotangent.reshape(block_count, 128, shard_extent)
    expand_per_block = jnp.take(adapter_expand, tenant_per_block, axis=0)
    low_part = jnp.einsum(
        "zuh,zsh->zus", gradient_per_block, expand_per_block, preferred_element_type=jnp.float32
    )
    low_whole = lax.psum(low_part.astype(jnp.bfloat16), "tensor").astype(jnp.float32)
    lowrank_bfloat = (low_whole * (scale_per_block[:, None, None] * block_mask[:, None, :])).astype(
        jnp.bfloat16
    )
    shrink_per_block = jnp.take(adapter_shrink, tenant_per_block, axis=0)
    adapter_term = jnp.einsum(
        "uwq,ueq->uwe", lowrank_bfloat, shrink_per_block, preferred_element_type=jnp.float32
    )
    input_gradient = (frozen_product.T + adapter_term.reshape(count_of_rows, shard_extent)).astype(
        jnp.bfloat16
    )
    slot_order = jnp.argsort(tenant_owner_index * tenant_count + tenant_ids)
    slot_of = jnp.argsort(slot_order)
    block_slot = jnp.sum(jnp.where(matches, slot_of[None, :], 0), axis=1)
    block_select = (block_slot[:, None] == tenant_ids[None, :]).astype(jnp.float32)
    saved_lowrank_masked = saved_lowrank.reshape(block_count, 128, rank_extent) * block_mask[
        :, None, :
    ].astype(jnp.bfloat16)
    input_per_block = projection_input.reshape(block_count, 128, shard_extent)
    shrink_piece = jnp.einsum(
        "tme,tmj->tej", input_per_block, lowrank_bfloat, preferred_element_type=jnp.float32
    )
    expand_piece = jnp.einsum(
        "paw,pan->pwn", saved_lowrank_masked, gradient_per_block, preferred_element_type=jnp.float32
    )
    expand_piece = expand_piece * scale_per_block[:, None, None]
    shrink_slots = jnp.einsum(
        "bs,bdr->sdr", block_select, shrink_piece, precision=lax.Precision.HIGHEST
    )
    expand_slots = jnp.einsum(
        "bs,brd->srd", block_select, expand_piece, precision=lax.Precision.HIGHEST
    )
    grad_shrink, grad_expand = (
        lax.psum_scatter(
            shrink_slots.astype(jnp.bfloat16), "dp", scatter_dimension=0, tiled=True
        ).astype(jnp.float32),
        lax.psum_scatter(
            expand_slots.astype(jnp.bfloat16), "dp", scatter_dimension=0, tiled=True
        ).astype(jnp.float32),
    )
    return (input_gradient, grad_shrink, grad_expand)


def solution(mesh):
    placed = (
        P(("groups", "dp"), "tensor"),
        P(("groups", "dp"), "tensor"),
        P(("groups", "dp"), None),
        P(None, "tensor"),
        P(None, "tensor", None),
        P(None, None, "tensor"),
        P(("groups", "dp")),
        P(),
        P(),
    )
    body = per_device_any
    if mesh.shape["tensor"] == 8:
        body = functools.partial(per_device, mesh.shape["dp"])
    return jax.shard_map(
        body,
        mesh=mesh,
        in_specs=placed,
        out_specs=(
            P(("groups", "dp"), "tensor"),
            P(("groups", "dp"), "tensor", None),
            P(("groups", "dp"), None, "tensor"),
        ),
        check_vma=False,
    )
```

```python
import functools

import jax
import jax.numpy as jnp
from jax import lax
from jax.experimental import pallas as pl
from jax.experimental.pallas import tpu as pltpu
from jax.sharding import PartitionSpec as P

adapter_alpha = 32.0
row_block = 128
bf16 = jnp.bfloat16
f32 = jnp.float32
contract_last = (((1,), (1,)), ((), ()))
contract_first = (((0,), (0,)), ((), ()))
vmem_bytes = 40 * 1024 * 1024
declared = pl.CostEstimate(flops=10**12, bytes_accessed=10**9, transcendentals=0)


def params():
    return pltpu.CompilerParams(vmem_limit_bytes=vmem_bytes)


def product_kernel(modes, block_count, *refs):
    position = 1
    rows, weights = refs[1], refs[2]
    position = 3
    total = lax.dot_general(
        rows[...], weights[...], contract_last, preferred_element_type=f32
    )
    for mode in modes:
        addend = refs[position][...].astype(f32)
        if mode:
            addend = addend * refs[0][1 + mode].astype(f32)
        total = total + addend
        position += 1
    if block_count:
        low = refs[position]
        position += 1
        terms = []
        for i in range(block_count):
            terms.append(
                lax.dot_general(
                    low[i * row_block : (i + 1) * row_block, :],
                    refs[position][0],
                    contract_last,
                    preferred_element_type=f32,
                )
            )
            position += 1
        total = total + jnp.concatenate(terms, axis=0)
    refs[-1][...] = total.astype(refs[-1].dtype)


def product(scalars, gradient, weights, piece, piece_rows, width, adds, link, adapter=None):
    depth = gradient.shape[1]
    tile = min(width, 512)
    while width % tile:
        tile //= 2
    steps = width // tile
    in_specs = [
        pl.BlockSpec((piece_rows, depth), lambda j, s: (s[1], 0)),
        pl.BlockSpec((tile, depth), lambda j, s: (s[0] * steps + j, 0)),
    ]
    operands = [gradient, weights]
    for array, _ in adds:
        in_specs.append(pl.BlockSpec((piece_rows, tile), lambda j, s: (0, j)))
        operands.append(array)
    block_count = 0
    if adapter is not None:
        low, shrink = adapter
        rank = low.shape[1]
        block_count = piece_rows // row_block
        in_specs.append(pl.BlockSpec((piece_rows, rank), lambda j, s: (piece, 0)))
        operands.append(low)
        for i in range(block_count):
            in_specs.append(
                pl.BlockSpec((1, tile, rank), functools.partial(lambda j, s, i: (s[4 + i], j, 0), i=i))
            )
            operands.append(shrink)
    for array in link:
        in_specs.append(pl.BlockSpec(memory_space=pl.ANY))
        operands.append(array)
    return pl.pallas_call(
        functools.partial(product_kernel, tuple(mode for _, mode in adds), block_count),
        grid_spec=pltpu.PrefetchScalarGridSpec(
            num_scalar_prefetch=1,
            grid=(steps,),
            in_specs=in_specs,
            out_specs=pl.BlockSpec((piece_rows, tile), lambda j, s: (0, j)),
        ),
        out_shape=jax.ShapeDtypeStruct((piece_rows, width), f32 if adapter else bf16),
        compiler_params=params(),
        cost_estimate=declared,
    )(scalars, *operands)


def finish_kernel(counts, *refs):
    out = refs[-1]
    position = 0
    for piece, count in enumerate(counts):

        @pl.when(pl.program_id(0) == piece)
        def _():
            total = refs[position][...].astype(f32)
            for i in range(1, count):
                total = total + refs[position + i][...].astype(f32)
            out[...] = total.astype(out.dtype)

        position += count


def finish(groups, link):
    piece_rows, width = groups[0][0].shape
    tile = width // 2

    def place(piece):
        def index(p, j):
            return (0, jnp.where(p == piece, j, jnp.where(p < piece, 0, 1)))

        return index

    in_specs = [
        pl.BlockSpec((piece_rows, tile), place(piece))
        for piece, group in enumerate(groups)
        for _ in group
    ]
    return pl.pallas_call(
        functools.partial(finish_kernel, tuple(len(group) for group in groups)),
        grid=(len(groups), 2),
        in_specs=in_specs + [pl.BlockSpec(memory_space=pl.ANY)] * len(link),
        out_specs=pl.BlockSpec((piece_rows, tile), lambda p, j: (p, j)),
        out_shape=jax.ShapeDtypeStruct((len(groups) * piece_rows, width), bf16),
        compiler_params=params(),
        cost_estimate=declared,
    )(*[array for group in groups for array in group], *link)


def low_kernel(tenants, rows, expand, link, out):
    out[...] = lax.dot_general(
        rows[...], expand[0], contract_last, preferred_element_type=f32
    ).astype(out.dtype)


def low_product(tenants, gradient, expand, link):
    count_of_rows, depth = gradient.shape
    rank = expand.shape[1]
    return pl.pallas_call(
        low_kernel,
        grid_spec=pltpu.PrefetchScalarGridSpec(
            num_scalar_prefetch=1,
            grid=(count_of_rows // row_block,),
            in_specs=[
                pl.BlockSpec((row_block, depth), lambda b, s: (b, 0)),
                pl.BlockSpec((1, rank, depth), lambda b, s: (s[b], 0, 0)),
                pl.BlockSpec(memory_space=pl.ANY),
            ],
            out_specs=pl.BlockSpec((row_block, rank), lambda b, s: (b, 0)),
        ),
        out_shape=jax.ShapeDtypeStruct((count_of_rows, rank), bf16),
        compiler_params=params(),
        cost_estimate=declared,
    )(tenants, gradient, expand, link)


def scale_kernel(ranks, scales, low, link, out):
    columns = lax.broadcasted_iota(jnp.int32, (row_block, low.shape[1]), 1)
    for b in range(low.shape[0] // row_block):
        here = pl.ds(b * row_block, row_block)
        kept = jnp.where(columns < ranks[b], low[here, :].astype(f32) * scales[b], 0.0)
        out[here, :] = kept.astype(out.dtype)


def scaled_low(ranks, scales, low, link):
    whole = pl.BlockSpec(memory_space=pltpu.VMEM)
    return pl.pallas_call(
        scale_kernel,
        in_specs=[pl.BlockSpec(memory_space=pltpu.SMEM)] * 2
        + [whole, pl.BlockSpec(memory_space=pl.ANY)],
        out_specs=whole,
        out_shape=jax.ShapeDtypeStruct(low.shape, bf16),
        compiler_params=params(),
        cost_estimate=declared,
    )(ranks, scales, low, link)


def factor_kernel(slots_each, slots, scales, left, right, *refs):
    own = refs[-1]
    own[...] = jnp.zeros_like(own)
    for b in range(left.shape[0] // row_block):
        slot = slots[b]

        @pl.when(slot < slots_each)
        def _():
            here = pl.ds(b * row_block, row_block)
            piece = lax.dot_general(
                left[here, :], right[here, :], contract_first, preferred_element_type=f32
            )
            own[slot] += piece * scales[b]


def factor_sums(slots, scales, left, right, slots_each, link):
    whole = pl.BlockSpec(memory_space=pltpu.VMEM)
    return pl.pallas_call(
        functools.partial(factor_kernel, slots_each),
        in_specs=[pl.BlockSpec(memory_space=pltpu.SMEM)] * 2
        + [whole] * 2
        + [pl.BlockSpec(memory_space=pl.ANY)] * len(link),
        out_specs=whole,
        out_shape=jax.ShapeDtypeStruct((slots_each, left.shape[1], right.shape[1]), f32),
        compiler_params=params(),
        cost_estimate=declared,
    )(slots, scales, left, right, *link)


def per_device(
    owner_count,
    gradient,
    projection_input,
    saved_lowrank,
    weights,
    shrink,
    expand,
    tenant_per_block,
    tenant_adapter_rank,
    tenant_owner_index,
):
    count_of_rows, width = gradient.shape
    blocks = count_of_rows // row_block
    tenants = tenant_adapter_rank.shape[0]
    rank_extent = shrink.shape[2]
    node = lax.axis_index("tensor") // 2
    side = lax.axis_index("tensor") % 2
    owner = lax.axis_index("dp")
    at_end = (node == 0) | (node == 3)
    piece_rows = count_of_rows // 2
    lower, upper = 0, 1
    link = []

    roles = (at_end, jnp.logical_not(at_end))

    def run(dest, column, piece, adds):
        scalars = (dest * 2 + column, piece) + roles
        scalars = jnp.stack([jnp.asarray(v, jnp.int32) for v in scalars])
        out = product(scalars, gradient, weights, None, piece_rows, width, adds, link)
        link[:] = [out]
        return out

    def swap(x, active):
        pairs = []
        for z in active:
            pairs += [(2 * z, 2 * z + 1), (2 * z + 1, 2 * z)]
        return lax.ppermute(x, "tensor", pairs)

    def along(x, hops):
        return lax.ppermute(
            x, "tensor", [(2 * a + y, 2 * b + y) for a, b in hops for y in range(2)]
        )

    nodes = 4
    ends, inner, every = (0, 3), (1, 2), (0, 1, 2, 3)
    from_ends = [(0, 1), (3, 2)]
    across = [(1, 2), (2, 1)]
    to_ends = [(1, 0), (2, 3)]
    first_half = node < 2
    far = jnp.where(first_half, 3, 0)
    beyond = jnp.where(first_half, 2, 1)
    nearer = jnp.where(first_half, 1, 2)
    near_end = jnp.where(first_half, 0, 3)
    same, other = side, 1 - side

    def all_owners(x):
        return lax.all_gather(x, "dp", axis=0, tiled=True)

    block_tenants = jnp.zeros((owner_count * blocks,), jnp.int32)
    for hop in range(owner_count):
        pairs = [(i, (i + hop) % owner_count) for i in range(owner_count)]
        theirs = lax.ppermute(tenant_per_block, "dp", pairs) if hop else tenant_per_block
        place = lax.rem(owner - hop + owner_count, owner_count) * blocks
        block_tenants = lax.dynamic_update_slice_in_dim(block_tenants, theirs, place, 0)
    tenant_ids = jnp.arange(tenants, dtype=jnp.int32)
    matches = block_tenants[:, None] == tenant_ids[None, :]
    block_ranks = jnp.sum(jnp.where(matches, tenant_adapter_rank[None, :], 0), axis=1)
    block_scales = adapter_alpha / block_ranks.astype(f32)
    key = tenant_owner_index * tenants + tenant_ids
    slot_of = jnp.sum((key[None, :] < key[:, None]).astype(jnp.int32), axis=1)
    slots_each = tenants // owner_count
    slot_here = lax.rem(slot_of - owner * slots_each + tenants, tenants)
    block_slots = jnp.sum(jnp.where(matches, slot_here[None, :], 0), axis=1)

    own_ranks = lax.dynamic_slice_in_dim(block_ranks, owner * blocks, blocks, 0)
    own_scales = lax.dynamic_slice_in_dim(block_scales, owner * blocks, blocks, 0)

    def adapter_space():
        part = low_product(tenant_per_block, gradient, expand, link[0])
        link[:] = [part]
        return lax.psum(part, "tensor")

    def scale_low(low):
        out = scaled_low(own_ranks, own_scales, low, link[0])
        link[:] = [out]
        return out

    def expand_gradient():
        kept = jnp.arange(rank_extent, dtype=jnp.int32)[None, :] < block_ranks[:, None]
        saved = all_owners(saved_lowrank).reshape(-1, row_block, rank_extent)
        saved = (saved * kept[:, None, :].astype(bf16)).reshape(-1, rank_extent)
        out = factor_sums(
            block_slots, block_scales, saved, all_owners(gradient), slots_each, link
        )
        link[:] = [out]
        return out

    def shrink_gradient(low):
        out = factor_sums(
            block_slots, jnp.ones_like(block_scales), all_owners(projection_input), all_owners(low),
            slots_each, link,
        )
        link[:] = [out]
        return out

    y1 = swap(run(jnp.where(at_end, far, near_end), other, upper, []), every)
    direct_a = along(run(far, other, lower, []), from_ends)
    low_whole = adapter_space()
    y2 = swap(run(beyond, other, lower, []), ends)
    direct_b = along(run(far, same, lower, []), from_ends)
    out = run(
        far,
        jnp.where(at_end, same, other),
        jnp.where(at_end, upper, lower),
        [(y1, 1), (direct_a, 0)],
    )
    upper_1, direct_a = along(out, from_ends), along(out, across)
    y3 = swap(run(jnp.where(at_end, beyond, far), other, upper, []), every)
    out = run(jnp.where(at_end, beyond, far), same, lower, [(y2, 0), (direct_b, 0)])
    lower_2, direct_b = along(out, from_ends), along(out, across)
    y4 = swap(run(jnp.where(at_end, nearer, beyond), other, lower, []), every)
    out = run(
        jnp.where(at_end, beyond, near_end),
        jnp.where(at_end, same, other),
        jnp.where(at_end, upper, lower),
        [(y3, 1), (direct_a, 0)],
    )
    both_3 = along(out, from_ends + to_ends)
    grad_expand = expand_gradient()
    y5 = swap(run(jnp.where(at_end, nearer, beyond), other, upper, []), every)
    upper_far = along(run(far, same, upper, [(y3, 0), (upper_1, 0)]), across)
    out = run(jnp.where(at_end, nearer, near_end), same, lower, [(y4, 1), (direct_b, 0)])
    both_4 = along(out, from_ends + to_ends)
    low = scale_low(low_whole)
    y6 = swap(run(node, other, upper, []), every)
    lower_4 = along(run(beyond, same, lower, [(y4, 0), (lower_2, 0)]), across)
    out = run(
        jnp.where(at_end, nearer, near_end), same, upper, [(y5, 1), (y1, 2), (upper_far, 0)]
    )
    both_5 = along(out, from_ends + to_ends)
    y7 = swap(run(node, other, lower, [(both_3, 1)]), every)
    upper_4 = along(run(beyond, same, upper, [(y5, 0), (both_3, 0)]), across)
    def base(piece, adds):
        in_piece = piece_rows // row_block
        scalars = [node * 2 + side, jnp.int32(piece), jnp.int32(0), jnp.int32(0)]
        scalars += [tenant_per_block[piece * in_piece + i] for i in range(in_piece)]
        out = product(
            jnp.stack(scalars).astype(jnp.int32),
            gradient, weights, piece, piece_rows, width, adds, link, (low, shrink),
        )
        link[:] = [out]
        return out

    lower_base = base(lower, [(both_4, 0), (lower_4, 0)])
    upper_base = base(upper, [(y6, 0)])
    grad_shrink = shrink_gradient(low)
    input_gradient = finish([[lower_base, y7], [upper_base, both_5, upper_4]], link)
    return (input_gradient, grad_shrink, grad_expand)


def per_device_any(
    query_cotangent,
    projection_input,
    saved_lowrank,
    query_matrix,
    adapter_shrink,
    adapter_expand,
    tenant_per_block,
    tenant_adapter_rank,
    tenant_owner_index,
):
    count_of_rows, shard_extent = query_cotangent.shape
    block_count = count_of_rows // 128
    tenant_count = tenant_adapter_rank.shape[0]
    rank_extent = adapter_shrink.shape[2]
    frozen_product = lax.psum_scatter(
        lax.dot_general(
            query_matrix,
            query_cotangent,
            contract_last,
            preferred_element_type=jnp.float32,
        ).astype(jnp.bfloat16),
        "tensor",
        scatter_dimension=0,
        tiled=True,
    ).astype(jnp.float32)
    tenant_ids = jnp.arange(tenant_count, dtype=jnp.int32)
    matches = tenant_per_block[:, None] == tenant_ids[None, :]
    rank_per_block = jnp.sum(jnp.where(matches, tenant_adapter_rank[None, :], 0), axis=1).astype(
        jnp.float32
    )
    scale_per_block = adapter_alpha / rank_per_block
    block_mask = (
        jnp.arange(rank_extent).astype(jnp.float32)[None, :] < rank_per_block[:, None]
    ).astype(jnp.float32)
    gradient_per_block = query_cotangent.reshape(block_count, 128, shard_extent)
    expand_per_block = jnp.take(adapter_expand, tenant_per_block, axis=0)
    low_part = jnp.einsum(
        "zuh,zsh->zus", gradient_per_block, expand_per_block, preferred_element_type=jnp.float32
    )
    low_whole = lax.psum(low_part.astype(jnp.bfloat16), "tensor").astype(jnp.float32)
    lowrank_bfloat = (low_whole * (scale_per_block[:, None, None] * block_mask[:, None, :])).astype(
        jnp.bfloat16
    )
    shrink_per_block = jnp.take(adapter_shrink, tenant_per_block, axis=0)
    adapter_term = jnp.einsum(
        "uwq,ueq->uwe", lowrank_bfloat, shrink_per_block, preferred_element_type=jnp.float32
    )
    input_gradient = (frozen_product.T + adapter_term.reshape(count_of_rows, shard_extent)).astype(
        jnp.bfloat16
    )
    slot_order = jnp.argsort(tenant_owner_index * tenant_count + tenant_ids)
    slot_of = jnp.argsort(slot_order)
    block_slot = jnp.sum(jnp.where(matches, slot_of[None, :], 0), axis=1)
    block_select = (block_slot[:, None] == tenant_ids[None, :]).astype(jnp.float32)
    saved_lowrank_masked = saved_lowrank.reshape(block_count, 128, rank_extent) * block_mask[
        :, None, :
    ].astype(jnp.bfloat16)
    input_per_block = projection_input.reshape(block_count, 128, shard_extent)
    shrink_piece = jnp.einsum(
        "tme,tmj->tej", input_per_block, lowrank_bfloat, preferred_element_type=jnp.float32
    )
    expand_piece = jnp.einsum(
        "paw,pan->pwn", saved_lowrank_masked, gradient_per_block, preferred_element_type=jnp.float32
    )
    expand_piece = expand_piece * scale_per_block[:, None, None]
    shrink_slots = jnp.einsum(
        "bs,bdr->sdr", block_select, shrink_piece, precision=lax.Precision.HIGHEST
    )
    expand_slots = jnp.einsum(
        "bs,brd->srd", block_select, expand_piece, precision=lax.Precision.HIGHEST
    )
    grad_shrink, grad_expand = (
        lax.psum_scatter(
            shrink_slots.astype(jnp.bfloat16), "dp", scatter_dimension=0, tiled=True
        ).astype(jnp.float32),
        lax.psum_scatter(
            expand_slots.astype(jnp.bfloat16), "dp", scatter_dimension=0, tiled=True
        ).astype(jnp.float32),
    )
    return (input_gradient, grad_shrink, grad_expand)


def solution(mesh):
    placed = (
        P(("groups", "dp"), "tensor"),
        P(("groups", "dp"), "tensor"),
        P(("groups", "dp"), None),
        P(None, "tensor"),
        P(None, "tensor", None),
        P(None, None, "tensor"),
        P(("groups", "dp")),
        P(),
        P(),
    )
    body = per_device_any
    if mesh.shape["tensor"] == 8:
        body = functools.partial(per_device, mesh.shape["dp"])
    return jax.shard_map(
        body,
        mesh=mesh,
        in_specs=placed,
        out_specs=(
            P(("groups", "dp"), "tensor"),
            P(("groups", "dp"), "tensor", None),
            P(("groups", "dp"), None, "tensor"),
        ),
        check_vma=False,
    )
```

```python
import functools

import jax
import jax.numpy as jnp
from jax import lax
from jax.experimental import pallas as pl
from jax.experimental.pallas import tpu as pltpu
from jax.sharding import PartitionSpec as P

adapter_alpha = 32.0
row_block = 128
bf16 = jnp.bfloat16
f32 = jnp.float32
contract_last = (((1,), (1,)), ((), ()))
contract_first = (((0,), (0,)), ((), ()))
vmem_bytes = 40 * 1024 * 1024
declared = pl.CostEstimate(flops=10**12, bytes_accessed=10**9, transcendentals=0)


def params():
    return pltpu.CompilerParams(vmem_limit_bytes=vmem_bytes)


def product_kernel(modes, block_count, *refs):
    position = 1
    rows, weights = refs[1], refs[2]
    position = 3
    total = lax.dot_general(
        rows[...], weights[...], contract_last, preferred_element_type=f32
    )
    for mode in modes:
        addend = refs[position][...].astype(f32)
        if mode:
            addend = addend * refs[0][1 + mode].astype(f32)
        total = total + addend
        position += 1
    if block_count:
        low = refs[position]
        position += 1
        terms = []
        for i in range(block_count):
            terms.append(
                lax.dot_general(
                    low[i * row_block : (i + 1) * row_block, :],
                    refs[position][0],
                    contract_last,
                    preferred_element_type=f32,
                )
            )
            position += 1
        total = total + jnp.concatenate(terms, axis=0)
    refs[-1][...] = total.astype(refs[-1].dtype)


def product(scalars, gradient, weights, piece, piece_rows, width, adds, link, adapter=None):
    depth = gradient.shape[1]
    tile = min(width, 512)
    while width % tile:
        tile //= 2
    steps = width // tile
    in_specs = [
        pl.BlockSpec((piece_rows, depth), lambda j, s: (s[1], 0)),
        pl.BlockSpec((tile, depth), lambda j, s: (s[0] * steps + j, 0)),
    ]
    operands = [gradient, weights]
    for array, _ in adds:
        in_specs.append(pl.BlockSpec((piece_rows, tile), lambda j, s: (0, j)))
        operands.append(array)
    block_count = 0
    if adapter is not None:
        low, shrink = adapter
        rank = low.shape[1]
        block_count = piece_rows // row_block
        in_specs.append(pl.BlockSpec((piece_rows, rank), lambda j, s: (piece, 0)))
        operands.append(low)
        for i in range(block_count):
            in_specs.append(
                pl.BlockSpec((1, tile, rank), functools.partial(lambda j, s, i: (s[4 + i], j, 0), i=i))
            )
            operands.append(shrink)
    for array in link:
        in_specs.append(pl.BlockSpec(memory_space=pl.ANY))
        operands.append(array)
    return pl.pallas_call(
        functools.partial(product_kernel, tuple(mode for _, mode in adds), block_count),
        grid_spec=pltpu.PrefetchScalarGridSpec(
            num_scalar_prefetch=1,
            grid=(steps,),
            in_specs=in_specs,
            out_specs=pl.BlockSpec((piece_rows, tile), lambda j, s: (0, j)),
        ),
        out_shape=jax.ShapeDtypeStruct((piece_rows, width), bf16),
        compiler_params=params(),
        cost_estimate=declared,
    )(scalars, *operands)


def finish_kernel(counts, *refs):
    out = refs[-1]
    position = 0
    for piece, count in enumerate(counts):

        @pl.when(pl.program_id(0) == piece)
        def _():
            total = refs[position][...].astype(f32)
            for i in range(1, count):
                total = total + refs[position + i][...].astype(f32)
            out[...] = total.astype(out.dtype)

        position += count


def finish(groups, link):
    piece_rows, width = groups[0][0].shape
    tile = width // 2

    def place(piece):
        def index(p, j):
            return (0, jnp.where(p == piece, j, jnp.where(p < piece, 0, 1)))

        return index

    in_specs = [
        pl.BlockSpec((piece_rows, tile), place(piece))
        for piece, group in enumerate(groups)
        for _ in group
    ]
    return pl.pallas_call(
        functools.partial(finish_kernel, tuple(len(group) for group in groups)),
        grid=(len(groups), 2),
        in_specs=in_specs + [pl.BlockSpec(memory_space=pl.ANY)] * len(link),
        out_specs=pl.BlockSpec((piece_rows, tile), lambda p, j: (p, j)),
        out_shape=jax.ShapeDtypeStruct((len(groups) * piece_rows, width), bf16),
        compiler_params=params(),
        cost_estimate=declared,
    )(*[array for group in groups for array in group], *link)


def low_kernel(tenants, rows, expand, link, out):
    out[...] = lax.dot_general(
        rows[...], expand[0], contract_last, preferred_element_type=f32
    ).astype(out.dtype)


def low_product(tenants, gradient, expand, link):
    count_of_rows, depth = gradient.shape
    rank = expand.shape[1]
    return pl.pallas_call(
        low_kernel,
        grid_spec=pltpu.PrefetchScalarGridSpec(
            num_scalar_prefetch=1,
            grid=(count_of_rows // row_block,),
            in_specs=[
                pl.BlockSpec((row_block, depth), lambda b, s: (b, 0)),
                pl.BlockSpec((1, rank, depth), lambda b, s: (s[b], 0, 0)),
                pl.BlockSpec(memory_space=pl.ANY),
            ],
            out_specs=pl.BlockSpec((row_block, rank), lambda b, s: (b, 0)),
        ),
        out_shape=jax.ShapeDtypeStruct((count_of_rows, rank), bf16),
        compiler_params=params(),
        cost_estimate=declared,
    )(tenants, gradient, expand, link)


def scale_kernel(ranks, scales, low, link, out):
    columns = lax.broadcasted_iota(jnp.int32, (row_block, low.shape[1]), 1)
    for b in range(low.shape[0] // row_block):
        here = pl.ds(b * row_block, row_block)
        kept = jnp.where(columns < ranks[b], low[here, :].astype(f32) * scales[b], 0.0)
        out[here, :] = kept.astype(out.dtype)


def scaled_low(ranks, scales, low, link):
    whole = pl.BlockSpec(memory_space=pltpu.VMEM)
    return pl.pallas_call(
        scale_kernel,
        in_specs=[pl.BlockSpec(memory_space=pltpu.SMEM)] * 2
        + [whole, pl.BlockSpec(memory_space=pl.ANY)],
        out_specs=whole,
        out_shape=jax.ShapeDtypeStruct(low.shape, bf16),
        compiler_params=params(),
        cost_estimate=declared,
    )(ranks, scales, low, link)


def factor_kernel(slots_each, slots, scales, left, right, *refs):
    own = refs[-1]
    own[...] = jnp.zeros_like(own)
    for b in range(left.shape[0] // row_block):
        slot = slots[b]

        @pl.when(slot < slots_each)
        def _():
            here = pl.ds(b * row_block, row_block)
            piece = lax.dot_general(
                left[here, :], right[here, :], contract_first, preferred_element_type=f32
            )
            own[slot] += piece * scales[b]


def factor_sums(slots, scales, left, right, slots_each, link):
    whole = pl.BlockSpec(memory_space=pltpu.VMEM)
    return pl.pallas_call(
        functools.partial(factor_kernel, slots_each),
        in_specs=[pl.BlockSpec(memory_space=pltpu.SMEM)] * 2
        + [whole] * 2
        + [pl.BlockSpec(memory_space=pl.ANY)] * len(link),
        out_specs=whole,
        out_shape=jax.ShapeDtypeStruct((slots_each, left.shape[1], right.shape[1]), f32),
        compiler_params=params(),
        cost_estimate=declared,
    )(slots, scales, left, right, *link)


def per_device(
    owner_count,
    gradient,
    projection_input,
    saved_lowrank,
    weights,
    shrink,
    expand,
    tenant_per_block,
    tenant_adapter_rank,
    tenant_owner_index,
):
    count_of_rows, width = gradient.shape
    blocks = count_of_rows // row_block
    tenants = tenant_adapter_rank.shape[0]
    rank_extent = shrink.shape[2]
    node = lax.axis_index("tensor") // 2
    side = lax.axis_index("tensor") % 2
    owner = lax.axis_index("dp")
    at_end = (node == 0) | (node == 3)
    piece_rows = count_of_rows // 2
    lower, upper = 0, 1
    link = []

    roles = (at_end, jnp.logical_not(at_end))

    def run(dest, column, piece, adds):
        scalars = (dest * 2 + column, piece) + roles
        scalars = jnp.stack([jnp.asarray(v, jnp.int32) for v in scalars])
        out = product(scalars, gradient, weights, None, piece_rows, width, adds, link)
        link[:] = [out]
        return out

    def swap(x, active):
        pairs = []
        for z in active:
            pairs += [(2 * z, 2 * z + 1), (2 * z + 1, 2 * z)]
        pairs += [(2 * z + y, 2 * z + y) for z in every if z not in active for y in range(2)]
        return lax.ppermute(x, "tensor", pairs)

    def along(x, hops):
        return lax.ppermute(
            x, "tensor", [(2 * a + y, 2 * b + y) for a, b in hops for y in range(2)]
        )

    nodes = 4
    ends, inner, every = (0, 3), (1, 2), (0, 1, 2, 3)
    from_ends = [(0, 1), (3, 2)]
    across_only = [(1, 2), (2, 1)]
    to_ends = [(1, 0), (2, 3)]
    pairwise = from_ends + to_ends
    across = across_only + [(0, 0), (3, 3)]
    first_half = node < 2
    far = jnp.where(first_half, 3, 0)
    beyond = jnp.where(first_half, 2, 1)
    nearer = jnp.where(first_half, 1, 2)
    near_end = jnp.where(first_half, 0, 3)
    same, other = side, 1 - side

    def all_owners(x):
        return lax.all_gather(x, "dp", axis=0, tiled=True)

    block_tenants = jnp.zeros((owner_count * blocks,), jnp.int32)
    for hop in range(owner_count):
        pairs = [(i, (i + hop) % owner_count) for i in range(owner_count)]
        theirs = lax.ppermute(tenant_per_block, "dp", pairs) if hop else tenant_per_block
        place = lax.rem(owner - hop + owner_count, owner_count) * blocks
        block_tenants = lax.dynamic_update_slice_in_dim(block_tenants, theirs, place, 0)
    tenant_ids = jnp.arange(tenants, dtype=jnp.int32)
    matches = block_tenants[:, None] == tenant_ids[None, :]
    block_ranks = jnp.sum(jnp.where(matches, tenant_adapter_rank[None, :], 0), axis=1)
    block_scales = adapter_alpha / block_ranks.astype(f32)
    key = tenant_owner_index * tenants + tenant_ids
    slot_of = jnp.sum((key[None, :] < key[:, None]).astype(jnp.int32), axis=1)
    slots_each = tenants // owner_count
    slot_here = lax.rem(slot_of - owner * slots_each + tenants, tenants)
    block_slots = jnp.sum(jnp.where(matches, slot_here[None, :], 0), axis=1)

    own_ranks = lax.dynamic_slice_in_dim(block_ranks, owner * blocks, blocks, 0)
    own_scales = lax.dynamic_slice_in_dim(block_scales, owner * blocks, blocks, 0)

    def adapter_space():
        part = low_product(tenant_per_block, gradient, expand, link[0])
        link[:] = [part]
        return lax.psum(part, "tensor")

    def scale_low(low):
        out = scaled_low(own_ranks, own_scales, low, link[0])
        link[:] = [out]
        return out

    def expand_gradient():
        kept = jnp.arange(rank_extent, dtype=jnp.int32)[None, :] < block_ranks[:, None]
        saved = all_owners(saved_lowrank).reshape(-1, row_block, rank_extent)
        saved = (saved * kept[:, None, :].astype(bf16)).reshape(-1, rank_extent)
        out = factor_sums(
            block_slots, block_scales, saved, all_owners(gradient), slots_each, link
        )
        link[:] = [out]
        return out

    def shrink_gradient(low):
        out = factor_sums(
            block_slots, jnp.ones_like(block_scales), all_owners(projection_input), all_owners(low),
            slots_each, link,
        )
        link[:] = [out]
        return out

    y1 = swap(run(jnp.where(at_end, far, near_end), other, upper, []), every)
    direct_a = along(run(far, other, lower, []), pairwise)
    low_whole = adapter_space()
    y2 = swap(run(beyond, other, lower, []), ends)
    direct_b = along(run(far, same, lower, []), pairwise)
    out = run(
        far,
        jnp.where(at_end, same, other),
        jnp.where(at_end, upper, lower),
        [(y1, 1), (direct_a, 2)],
    )
    upper_1, direct_a = along(out, pairwise), along(out, across)
    y3 = swap(run(jnp.where(at_end, beyond, far), other, upper, []), every)
    out = run(jnp.where(at_end, beyond, far), same, lower, [(y2, 1), (direct_b, 2)])
    lower_2, direct_b = along(out, pairwise), along(out, across)
    y4 = swap(run(jnp.where(at_end, nearer, beyond), other, lower, []), every)
    out = run(
        jnp.where(at_end, beyond, near_end),
        jnp.where(at_end, same, other),
        jnp.where(at_end, upper, lower),
        [(y3, 1), (direct_a, 2)],
    )
    both_3 = along(out, pairwise)
    grad_expand = expand_gradient()
    y5 = swap(run(jnp.where(at_end, nearer, beyond), other, upper, []), every)
    upper_far = along(run(far, same, upper, [(y3, 0), (upper_1, 0)]), across)
    out = run(jnp.where(at_end, nearer, near_end), same, lower, [(y4, 1), (direct_b, 2)])
    both_4 = along(out, pairwise)
    low = scale_low(low_whole)
    y6 = swap(run(node, other, upper, []), every)
    lower_4 = along(run(beyond, same, lower, [(y4, 0), (lower_2, 0)]), across)
    out = run(
        jnp.where(at_end, nearer, near_end), same, upper, [(y5, 1), (y1, 2), (upper_far, 2)]
    )
    both_5 = along(out, pairwise)
    y7 = swap(run(node, other, lower, [(both_3, 1)]), every)
    upper_4 = along(run(beyond, same, upper, [(y5, 0), (both_3, 0)]), across_only)
    def base(piece, adds):
        in_piece = piece_rows // row_block
        scalars = [node * 2 + side, jnp.int32(piece)] + [jnp.asarray(r, jnp.int32) for r in roles]
        scalars += [tenant_per_block[piece * in_piece + i] for i in range(in_piece)]
        out = product(
            jnp.stack(scalars).astype(jnp.int32),
            gradient, weights, piece, piece_rows, width, adds, link, (low, shrink),
        )
        link[:] = [out]
        return out

    lower_base = base(lower, [(both_4, 0), (lower_4, 2)])
    upper_base = base(upper, [(y6, 0)])
    grad_shrink = shrink_gradient(low)
    input_gradient = finish([[lower_base, y7], [upper_base, both_5, upper_4]], link)
    return (input_gradient, grad_shrink, grad_expand)


def per_device_any(
    query_cotangent,
    projection_input,
    saved_lowrank,
    query_matrix,
    adapter_shrink,
    adapter_expand,
    tenant_per_block,
    tenant_adapter_rank,
    tenant_owner_index,
):
    count_of_rows, shard_extent = query_cotangent.shape
    block_count = count_of_rows // 128
    tenant_count = tenant_adapter_rank.shape[0]
    rank_extent = adapter_shrink.shape[2]
    frozen_product = lax.psum_scatter(
        lax.dot_general(
            query_matrix,
            query_cotangent,
            contract_last,
            preferred_element_type=jnp.float32,
        ).astype(jnp.bfloat16),
        "tensor",
        scatter_dimension=0,
        tiled=True,
    ).astype(jnp.float32)
    tenant_ids = jnp.arange(tenant_count, dtype=jnp.int32)
    matches = tenant_per_block[:, None] == tenant_ids[None, :]
    rank_per_block = jnp.sum(jnp.where(matches, tenant_adapter_rank[None, :], 0), axis=1).astype(
        jnp.float32
    )
    scale_per_block = adapter_alpha / rank_per_block
    block_mask = (
        jnp.arange(rank_extent).astype(jnp.float32)[None, :] < rank_per_block[:, None]
    ).astype(jnp.float32)
    gradient_per_block = query_cotangent.reshape(block_count, 128, shard_extent)
    expand_per_block = jnp.take(adapter_expand, tenant_per_block, axis=0)
    low_part = jnp.einsum(
        "zuh,zsh->zus", gradient_per_block, expand_per_block, preferred_element_type=jnp.float32
    )
    low_whole = lax.psum(low_part.astype(jnp.bfloat16), "tensor").astype(jnp.float32)
    lowrank_bfloat = (low_whole * (scale_per_block[:, None, None] * block_mask[:, None, :])).astype(
        jnp.bfloat16
    )
    shrink_per_block = jnp.take(adapter_shrink, tenant_per_block, axis=0)
    adapter_term = jnp.einsum(
        "uwq,ueq->uwe", lowrank_bfloat, shrink_per_block, preferred_element_type=jnp.float32
    )
    input_gradient = (frozen_product.T + adapter_term.reshape(count_of_rows, shard_extent)).astype(
        jnp.bfloat16
    )
    slot_order = jnp.argsort(tenant_owner_index * tenant_count + tenant_ids)
    slot_of = jnp.argsort(slot_order)
    block_slot = jnp.sum(jnp.where(matches, slot_of[None, :], 0), axis=1)
    block_select = (block_slot[:, None] == tenant_ids[None, :]).astype(jnp.float32)
    saved_lowrank_masked = saved_lowrank.reshape(block_count, 128, rank_extent) * block_mask[
        :, None, :
    ].astype(jnp.bfloat16)
    input_per_block = projection_input.reshape(block_count, 128, shard_extent)
    shrink_piece = jnp.einsum(
        "tme,tmj->tej", input_per_block, lowrank_bfloat, preferred_element_type=jnp.float32
    )
    expand_piece = jnp.einsum(
        "paw,pan->pwn", saved_lowrank_masked, gradient_per_block, preferred_element_type=jnp.float32
    )
    expand_piece = expand_piece * scale_per_block[:, None, None]
    shrink_slots = jnp.einsum(
        "bs,bdr->sdr", block_select, shrink_piece, precision=lax.Precision.HIGHEST
    )
    expand_slots = jnp.einsum(
        "bs,brd->srd", block_select, expand_piece, precision=lax.Precision.HIGHEST
    )
    grad_shrink, grad_expand = (
        lax.psum_scatter(
            shrink_slots.astype(jnp.bfloat16), "dp", scatter_dimension=0, tiled=True
        ).astype(jnp.float32),
        lax.psum_scatter(
            expand_slots.astype(jnp.bfloat16), "dp", scatter_dimension=0, tiled=True
        ).astype(jnp.float32),
    )
    return (input_gradient, grad_shrink, grad_expand)


def solution(mesh):
    placed = (
        P(("groups", "dp"), "tensor"),
        P(("groups", "dp"), "tensor"),
        P(("groups", "dp"), None),
        P(None, "tensor"),
        P(None, "tensor", None),
        P(None, None, "tensor"),
        P(("groups", "dp")),
        P(),
        P(),
    )
    body = per_device_any
    if mesh.shape["tensor"] == 8:
        body = functools.partial(per_device, mesh.shape["dp"])
    return jax.shard_map(
        body,
        mesh=mesh,
        in_specs=placed,
        out_specs=(
            P(("groups", "dp"), "tensor"),
            P(("groups", "dp"), "tensor", None),
            P(("groups", "dp"), None, "tensor"),
        ),
        check_vma=False,
    )
```

```python
import functools

import jax
import jax.numpy as jnp
from jax import lax
from jax.experimental import pallas as pl
from jax.experimental.pallas import tpu as pltpu
from jax.sharding import PartitionSpec as P

adapter_alpha = 32.0
row_block = 128
bf16 = jnp.bfloat16
f32 = jnp.float32
contract_last = (((1,), (1,)), ((), ()))
contract_first = (((0,), (0,)), ((), ()))
vmem_bytes = 40 * 1024 * 1024
declared = pl.CostEstimate(flops=10**12, bytes_accessed=10**9, transcendentals=0)


def params():
    return pltpu.CompilerParams(vmem_limit_bytes=vmem_bytes)


def product_kernel(modes, block_count, *refs):
    position = 1
    rows, weights = refs[1], refs[2]
    position = 3
    total = lax.dot_general(
        rows[...], weights[...], contract_last, preferred_element_type=f32
    )
    for mode in modes:
        addend = refs[position][...].astype(f32)
        if mode:
            addend = addend * refs[0][1 + mode].astype(f32)
        total = total + addend
        position += 1
    if block_count:
        low = refs[position]
        position += 1
        terms = []
        for i in range(block_count):
            terms.append(
                lax.dot_general(
                    low[i * row_block : (i + 1) * row_block, :],
                    refs[position][0],
                    contract_last,
                    preferred_element_type=f32,
                )
            )
            position += 1
        total = total + jnp.concatenate(terms, axis=0)
    refs[-1][...] = total.astype(refs[-1].dtype)


def product(scalars, gradient, weights, piece, piece_rows, width, adds, link, adapter=None):
    depth = gradient.shape[1]
    tile = min(width, 512)
    while width % tile:
        tile //= 2
    steps = width // tile
    in_specs = [
        pl.BlockSpec((piece_rows, depth), lambda j, s: (s[1], 0)),
        pl.BlockSpec((tile, depth), lambda j, s: (s[0] * steps + j, 0)),
    ]
    operands = [gradient, weights]
    for array, _ in adds:
        in_specs.append(pl.BlockSpec((piece_rows, tile), lambda j, s: (0, j)))
        operands.append(array)
    block_count = 0
    if adapter is not None:
        low, shrink = adapter
        rank = low.shape[1]
        block_count = piece_rows // row_block
        in_specs.append(pl.BlockSpec((piece_rows, rank), lambda j, s: (piece, 0)))
        operands.append(low)
        for i in range(block_count):
            in_specs.append(
                pl.BlockSpec((1, tile, rank), functools.partial(lambda j, s, i: (s[4 + i], j, 0), i=i))
            )
            operands.append(shrink)
    for array in link:
        in_specs.append(pl.BlockSpec(memory_space=pl.ANY))
        operands.append(array)
    return pl.pallas_call(
        functools.partial(product_kernel, tuple(mode for _, mode in adds), block_count),
        grid_spec=pltpu.PrefetchScalarGridSpec(
            num_scalar_prefetch=1,
            grid=(steps,),
            in_specs=in_specs,
            out_specs=pl.BlockSpec((piece_rows, tile), lambda j, s: (0, j)),
        ),
        out_shape=jax.ShapeDtypeStruct((piece_rows, width), bf16),
        compiler_params=params(),
        cost_estimate=declared,
    )(scalars, *operands)


def finish_kernel(counts, *refs):
    out = refs[-1]
    position = 0
    for piece, count in enumerate(counts):

        @pl.when(pl.program_id(0) == piece)
        def _():
            total = refs[position][...].astype(f32)
            for i in range(1, count):
                total = total + refs[position + i][...].astype(f32)
            out[...] = total.astype(out.dtype)

        position += count


def finish(groups, link):
    piece_rows, width = groups[0][0].shape
    tile = width // 2

    def place(piece):
        def index(p, j):
            return (0, jnp.where(p == piece, j, jnp.where(p < piece, 0, 1)))

        return index

    in_specs = [
        pl.BlockSpec((piece_rows, tile), place(piece))
        for piece, group in enumerate(groups)
        for _ in group
    ]
    return pl.pallas_call(
        functools.partial(finish_kernel, tuple(len(group) for group in groups)),
        grid=(len(groups), 2),
        in_specs=in_specs + [pl.BlockSpec(memory_space=pl.ANY)] * len(link),
        out_specs=pl.BlockSpec((piece_rows, tile), lambda p, j: (p, j)),
        out_shape=jax.ShapeDtypeStruct((len(groups) * piece_rows, width), bf16),
        compiler_params=params(),
        cost_estimate=declared,
    )(*[array for group in groups for array in group], *link)


def low_kernel(tenants, rows, expand, link, out):
    out[...] = lax.dot_general(
        rows[...], expand[0], contract_last, preferred_element_type=f32
    ).astype(out.dtype)


def low_product(tenants, gradient, expand, link):
    count_of_rows, depth = gradient.shape
    rank = expand.shape[1]
    return pl.pallas_call(
        low_kernel,
        grid_spec=pltpu.PrefetchScalarGridSpec(
            num_scalar_prefetch=1,
            grid=(count_of_rows // row_block,),
            in_specs=[
                pl.BlockSpec((row_block, depth), lambda b, s: (b, 0)),
                pl.BlockSpec((1, rank, depth), lambda b, s: (s[b], 0, 0)),
                pl.BlockSpec(memory_space=pl.ANY),
            ],
            out_specs=pl.BlockSpec((row_block, rank), lambda b, s: (b, 0)),
        ),
        out_shape=jax.ShapeDtypeStruct((count_of_rows, rank), bf16),
        compiler_params=params(),
        cost_estimate=declared,
    )(tenants, gradient, expand, link)


def scale_kernel(ranks, scales, low, link, out):
    columns = lax.broadcasted_iota(jnp.int32, (row_block, low.shape[1]), 1)
    for b in range(low.shape[0] // row_block):
        here = pl.ds(b * row_block, row_block)
        kept = jnp.where(columns < ranks[b], low[here, :].astype(f32) * scales[b], 0.0)
        out[here, :] = kept.astype(out.dtype)


def scaled_low(ranks, scales, low, link):
    whole = pl.BlockSpec(memory_space=pltpu.VMEM)
    return pl.pallas_call(
        scale_kernel,
        in_specs=[pl.BlockSpec(memory_space=pltpu.SMEM)] * 2
        + [whole, pl.BlockSpec(memory_space=pl.ANY)],
        out_specs=whole,
        out_shape=jax.ShapeDtypeStruct(low.shape, bf16),
        compiler_params=params(),
        cost_estimate=declared,
    )(ranks, scales, low, link)


def factor_kernel(slots_each, slots, scales, left, right, *refs):
    own = refs[-1]
    own[...] = jnp.zeros_like(own)
    for b in range(left.shape[0] // row_block):
        slot = slots[b]

        @pl.when(slot < slots_each)
        def _():
            here = pl.ds(b * row_block, row_block)
            piece = lax.dot_general(
                left[here, :], right[here, :], contract_first, preferred_element_type=f32
            )
            own[slot] += piece * scales[b]


def factor_sums(slots, scales, left, right, slots_each, link):
    whole = pl.BlockSpec(memory_space=pltpu.VMEM)
    return pl.pallas_call(
        functools.partial(factor_kernel, slots_each),
        in_specs=[pl.BlockSpec(memory_space=pltpu.SMEM)] * 2
        + [whole] * 2
        + [pl.BlockSpec(memory_space=pl.ANY)] * len(link),
        out_specs=whole,
        out_shape=jax.ShapeDtypeStruct((slots_each, left.shape[1], right.shape[1]), f32),
        compiler_params=params(),
        cost_estimate=declared,
    )(slots, scales, left, right, *link)


def per_device(
    owner_count,
    gradient,
    projection_input,
    saved_lowrank,
    weights,
    shrink,
    expand,
    tenant_per_block,
    tenant_adapter_rank,
    tenant_owner_index,
):
    count_of_rows, width = gradient.shape
    blocks = count_of_rows // row_block
    tenants = tenant_adapter_rank.shape[0]
    rank_extent = shrink.shape[2]
    node = lax.axis_index("tensor") // 2
    side = lax.axis_index("tensor") % 2
    owner = lax.axis_index("dp")
    at_end = (node == 0) | (node == 3)
    piece_rows = count_of_rows // 2
    lower, upper = 0, 1
    link = []

    roles = (at_end, jnp.logical_not(at_end))

    def run(dest, column, piece, adds):
        scalars = (dest * 2 + column, piece) + roles
        scalars = jnp.stack([jnp.asarray(v, jnp.int32) for v in scalars])
        out = product(scalars, gradient, weights, None, piece_rows, width, adds, link)
        link[:] = [out]
        return out

    def swap(x, active):
        pairs = []
        for z in active:
            pairs += [(2 * z, 2 * z + 1), (2 * z + 1, 2 * z)]
        return lax.ppermute(x, "tensor", pairs)

    def along(x, hops):
        return lax.ppermute(
            x, "tensor", [(2 * a + y, 2 * b + y) for a, b in hops for y in range(2)]
        )

    nodes = 4
    every = (0, 1, 2, 3)
    from_ends = [(0, 1), (3, 2)]
    across = [(1, 2), (2, 1)]
    to_ends = [(1, 0), (2, 3)]
    pairwise = from_ends + to_ends
    def exchange(x):
        pairs = []
        for group in range(2):
            for y in range(2):
                pairs += [(group * 8 + 2 * a + y, group * 8 + 2 * b + y) for a, b in across]
                pairs += [(group * 8 + 2 * z + y, (1 - group) * 8 + 2 * z + y) for z in (0, 3)]
        return lax.ppermute(x, ("groups", "tensor"), pairs)

    first_half = node < 2
    far = jnp.where(first_half, 3, 0)
    beyond = jnp.where(first_half, 2, 1)
    nearer = jnp.where(first_half, 1, 2)
    near_end = jnp.where(first_half, 0, 3)
    same, other = side, 1 - side

    def all_owners(x):
        return lax.all_gather(x, "dp", axis=0, tiled=True)

    block_tenants = jnp.zeros((owner_count * blocks,), jnp.int32)
    for hop in range(owner_count):
        pairs = [(i, (i + hop) % owner_count) for i in range(owner_count)]
        theirs = lax.ppermute(tenant_per_block, "dp", pairs) if hop else tenant_per_block
        place = lax.rem(owner - hop + owner_count, owner_count) * blocks
        block_tenants = lax.dynamic_update_slice_in_dim(block_tenants, theirs, place, 0)
    tenant_ids = jnp.arange(tenants, dtype=jnp.int32)
    matches = block_tenants[:, None] == tenant_ids[None, :]
    block_ranks = jnp.sum(jnp.where(matches, tenant_adapter_rank[None, :], 0), axis=1)
    block_scales = adapter_alpha / block_ranks.astype(f32)
    key = tenant_owner_index * tenants + tenant_ids
    slot_of = jnp.sum((key[None, :] < key[:, None]).astype(jnp.int32), axis=1)
    slots_each = tenants // owner_count
    slot_here = lax.rem(slot_of - owner * slots_each + tenants, tenants)
    block_slots = jnp.sum(jnp.where(matches, slot_here[None, :], 0), axis=1)

    own_ranks = lax.dynamic_slice_in_dim(block_ranks, owner * blocks, blocks, 0)
    own_scales = lax.dynamic_slice_in_dim(block_scales, owner * blocks, blocks, 0)

    def adapter_space():
        part = low_product(tenant_per_block, gradient, expand, link[0])
        link[:] = [part]
        return lax.psum(part, "tensor")

    def scale_low(low):
        out = scaled_low(own_ranks, own_scales, low, link[0])
        link[:] = [out]
        return out

    def expand_gradient():
        kept = jnp.arange(rank_extent, dtype=jnp.int32)[None, :] < block_ranks[:, None]
        saved = all_owners(saved_lowrank).reshape(-1, row_block, rank_extent)
        saved = (saved * kept[:, None, :].astype(bf16)).reshape(-1, rank_extent)
        out = factor_sums(
            block_slots, block_scales, saved, all_owners(gradient), slots_each, link
        )
        link[:] = [out]
        return out

    def shrink_gradient(low):
        out = factor_sums(
            block_slots, jnp.ones_like(block_scales), all_owners(projection_input), all_owners(low),
            slots_each, link,
        )
        link[:] = [out]
        return out

    y1 = swap(run(jnp.where(at_end, far, near_end), other, upper, []), every)
    direct_a = along(run(far, other, lower, []), pairwise)
    low_whole = adapter_space()
    y2 = swap(run(beyond, other, lower, []), every)
    direct_b = along(run(far, same, lower, []), pairwise)
    out = run(
        far,
        jnp.where(at_end, same, other),
        jnp.where(at_end, upper, lower),
        [(y1, 1), (direct_a, 2)],
    )
    upper_1, direct_a = along(out, pairwise), exchange(out)
    y3 = swap(run(jnp.where(at_end, beyond, far), other, upper, []), every)
    out = run(jnp.where(at_end, beyond, far), same, lower, [(y2, 1), (direct_b, 2)])
    lower_2, direct_b = along(out, pairwise), exchange(out)
    y4 = swap(run(jnp.where(at_end, nearer, beyond), other, lower, []), every)
    out = run(
        jnp.where(at_end, beyond, near_end),
        jnp.where(at_end, same, other),
        jnp.where(at_end, upper, lower),
        [(y3, 1), (direct_a, 2)],
    )
    both_3 = along(out, pairwise)
    grad_expand = expand_gradient()
    y5 = swap(run(jnp.where(at_end, nearer, beyond), other, upper, []), every)
    upper_far = exchange(run(far, same, upper, [(y3, 0), (upper_1, 0)]))
    out = run(jnp.where(at_end, nearer, near_end), same, lower, [(y4, 1), (direct_b, 2)])
    both_4 = along(out, pairwise)
    low = scale_low(low_whole)
    y6 = swap(run(node, other, upper, []), every)
    lower_4 = exchange(run(beyond, same, lower, [(y4, 0), (lower_2, 0)]))
    out = run(
        jnp.where(at_end, nearer, near_end), same, upper, [(y5, 1), (y1, 2), (upper_far, 2)]
    )
    both_5 = along(out, pairwise)
    y7 = swap(run(node, other, lower, [(both_3, 1)]), every)
    upper_4 = along(run(beyond, same, upper, [(y5, 0), (both_3, 0)]), across)
    def base(piece, adds):
        in_piece = piece_rows // row_block
        scalars = [node * 2 + side, jnp.int32(piece)] + [jnp.asarray(r, jnp.int32) for r in roles]
        scalars += [tenant_per_block[piece * in_piece + i] for i in range(in_piece)]
        out = product(
            jnp.stack(scalars).astype(jnp.int32),
            gradient, weights, piece, piece_rows, width, adds, link, (low, shrink),
        )
        link[:] = [out]
        return out

    lower_base = base(lower, [(both_4, 0), (lower_4, 2)])
    upper_base = base(upper, [(y6, 0)])
    grad_shrink = shrink_gradient(low)
    input_gradient = finish([[lower_base, y7], [upper_base, both_5, upper_4]], link)
    return (input_gradient, grad_shrink, grad_expand)


def per_device_any(
    query_cotangent,
    projection_input,
    saved_lowrank,
    query_matrix,
    adapter_shrink,
    adapter_expand,
    tenant_per_block,
    tenant_adapter_rank,
    tenant_owner_index,
):
    count_of_rows, shard_extent = query_cotangent.shape
    block_count = count_of_rows // 128
    tenant_count = tenant_adapter_rank.shape[0]
    rank_extent = adapter_shrink.shape[2]
    frozen_product = lax.psum_scatter(
        lax.dot_general(
            query_matrix,
            query_cotangent,
            contract_last,
            preferred_element_type=jnp.float32,
        ).astype(jnp.bfloat16),
        "tensor",
        scatter_dimension=0,
        tiled=True,
    ).astype(jnp.float32)
    tenant_ids = jnp.arange(tenant_count, dtype=jnp.int32)
    matches = tenant_per_block[:, None] == tenant_ids[None, :]
    rank_per_block = jnp.sum(jnp.where(matches, tenant_adapter_rank[None, :], 0), axis=1).astype(
        jnp.float32
    )
    scale_per_block = adapter_alpha / rank_per_block
    block_mask = (
        jnp.arange(rank_extent).astype(jnp.float32)[None, :] < rank_per_block[:, None]
    ).astype(jnp.float32)
    gradient_per_block = query_cotangent.reshape(block_count, 128, shard_extent)
    expand_per_block = jnp.take(adapter_expand, tenant_per_block, axis=0)
    low_part = jnp.einsum(
        "zuh,zsh->zus", gradient_per_block, expand_per_block, preferred_element_type=jnp.float32
    )
    low_whole = lax.psum(low_part.astype(jnp.bfloat16), "tensor").astype(jnp.float32)
    lowrank_bfloat = (low_whole * (scale_per_block[:, None, None] * block_mask[:, None, :])).astype(
        jnp.bfloat16
    )
    shrink_per_block = jnp.take(adapter_shrink, tenant_per_block, axis=0)
    adapter_term = jnp.einsum(
        "uwq,ueq->uwe", lowrank_bfloat, shrink_per_block, preferred_element_type=jnp.float32
    )
    input_gradient = (frozen_product.T + adapter_term.reshape(count_of_rows, shard_extent)).astype(
        jnp.bfloat16
    )
    slot_order = jnp.argsort(tenant_owner_index * tenant_count + tenant_ids)
    slot_of = jnp.argsort(slot_order)
    block_slot = jnp.sum(jnp.where(matches, slot_of[None, :], 0), axis=1)
    block_select = (block_slot[:, None] == tenant_ids[None, :]).astype(jnp.float32)
    saved_lowrank_masked = saved_lowrank.reshape(block_count, 128, rank_extent) * block_mask[
        :, None, :
    ].astype(jnp.bfloat16)
    input_per_block = projection_input.reshape(block_count, 128, shard_extent)
    shrink_piece = jnp.einsum(
        "tme,tmj->tej", input_per_block, lowrank_bfloat, preferred_element_type=jnp.float32
    )
    expand_piece = jnp.einsum(
        "paw,pan->pwn", saved_lowrank_masked, gradient_per_block, preferred_element_type=jnp.float32
    )
    expand_piece = expand_piece * scale_per_block[:, None, None]
    shrink_slots = jnp.einsum(
        "bs,bdr->sdr", block_select, shrink_piece, precision=lax.Precision.HIGHEST
    )
    expand_slots = jnp.einsum(
        "bs,brd->srd", block_select, expand_piece, precision=lax.Precision.HIGHEST
    )
    grad_shrink, grad_expand = (
        lax.psum_scatter(
            shrink_slots.astype(jnp.bfloat16), "dp", scatter_dimension=0, tiled=True
        ).astype(jnp.float32),
        lax.psum_scatter(
            expand_slots.astype(jnp.bfloat16), "dp", scatter_dimension=0, tiled=True
        ).astype(jnp.float32),
    )
    return (input_gradient, grad_shrink, grad_expand)


def solution(mesh):
    placed = (
        P(("groups", "dp"), "tensor"),
        P(("groups", "dp"), "tensor"),
        P(("groups", "dp"), None),
        P(None, "tensor"),
        P(None, "tensor", None),
        P(None, None, "tensor"),
        P(("groups", "dp")),
        P(),
        P(),
    )
    body = per_device_any
    if mesh.shape["tensor"] == 8 and mesh.shape["groups"] == 2:
        body = functools.partial(per_device, mesh.shape["dp"])
    return jax.shard_map(
        body,
        mesh=mesh,
        in_specs=placed,
        out_specs=(
            P(("groups", "dp"), "tensor"),
            P(("groups", "dp"), "tensor", None),
            P(("groups", "dp"), None, "tensor"),
        ),
        check_vma=False,
    )
```

```python
import functools

import jax
import jax.numpy as jnp
from jax import lax
from jax.experimental import pallas as pl
from jax.experimental.pallas import tpu as pltpu
from jax.sharding import PartitionSpec as P

adapter_alpha = 32.0
row_block = 128
bf16 = jnp.bfloat16
f32 = jnp.float32
contract_last = (((1,), (1,)), ((), ()))
contract_first = (((0,), (0,)), ((), ()))
vmem_bytes = 40 * 1024 * 1024
declared = pl.CostEstimate(flops=10**12, bytes_accessed=10**9, transcendentals=0)


def params():
    return pltpu.CompilerParams(vmem_limit_bytes=vmem_bytes)


def product_kernel(modes, block_count, *refs):
    position = 1
    rows, weights = refs[1], refs[2]
    position = 3
    total = lax.dot_general(
        rows[...], weights[...], contract_last, preferred_element_type=f32
    )
    for mode in modes:
        addend = refs[position][...].astype(f32)
        if mode:
            addend = addend * refs[0][1 + mode].astype(f32)
        total = total + addend
        position += 1
    if block_count:
        low = refs[position]
        position += 1
        terms = []
        for i in range(block_count):
            terms.append(
                lax.dot_general(
                    low[i * row_block : (i + 1) * row_block, :],
                    refs[position][0],
                    contract_last,
                    preferred_element_type=f32,
                )
            )
            position += 1
        total = total + jnp.concatenate(terms, axis=0)
    refs[-1][...] = total.astype(refs[-1].dtype)


def product(scalars, gradient, weights, piece, piece_rows, width, adds, link, adapter=None):
    depth = gradient.shape[1]
    tile = min(width, 512)
    while width % tile:
        tile //= 2
    steps = width // tile
    in_specs = [
        pl.BlockSpec((piece_rows, depth), lambda j, s: (s[1], 0)),
        pl.BlockSpec((tile, depth), lambda j, s: (s[0] * steps + j, 0)),
    ]
    operands = [gradient, weights]
    for array, _ in adds:
        in_specs.append(pl.BlockSpec((piece_rows, tile), lambda j, s: (0, j)))
        operands.append(array)
    block_count = 0
    if adapter is not None:
        low, shrink = adapter
        rank = low.shape[1]
        block_count = piece_rows // row_block
        in_specs.append(pl.BlockSpec((piece_rows, rank), lambda j, s: (piece, 0)))
        operands.append(low)
        for i in range(block_count):
            in_specs.append(
                pl.BlockSpec((1, tile, rank), functools.partial(lambda j, s, i: (s[4 + i], j, 0), i=i))
            )
            operands.append(shrink)
    for array in link:
        in_specs.append(pl.BlockSpec(memory_space=pl.ANY))
        operands.append(array)
    return pl.pallas_call(
        functools.partial(product_kernel, tuple(mode for _, mode in adds), block_count),
        grid_spec=pltpu.PrefetchScalarGridSpec(
            num_scalar_prefetch=1,
            grid=(steps,),
            in_specs=in_specs,
            out_specs=pl.BlockSpec((piece_rows, tile), lambda j, s: (0, j)),
        ),
        out_shape=jax.ShapeDtypeStruct((piece_rows, width), bf16),
        compiler_params=params(),
        cost_estimate=declared,
    )(scalars, *operands)


def pair_kernel(scalars, rows, weights, first, second):
    part = lax.dot_general(
        rows[...], weights[...], contract_last, preferred_element_type=f32
    ).astype(bf16)

    @pl.when(pl.program_id(0) == 0)
    def _():
        first[...] = part

    @pl.when(pl.program_id(0) == 1)
    def _():
        second[...] = part


def product_pair(scalars, gradient, weights, piece_rows, width):
    depth = gradient.shape[1]
    tile = width // 2
    piece = jax.ShapeDtypeStruct((piece_rows, width), bf16)
    return pl.pallas_call(
        pair_kernel,
        grid_spec=pltpu.PrefetchScalarGridSpec(
            num_scalar_prefetch=1,
            grid=(2, 2),
            in_specs=[
                pl.BlockSpec((piece_rows, depth), lambda t, j, s: (s[2 * t + 1], 0)),
                pl.BlockSpec((tile, depth), lambda t, j, s: (s[2 * t] * 2 + j, 0)),
            ],
            out_specs=[
                pl.BlockSpec((piece_rows, tile), lambda t, j, s: (0, jnp.where(t == 0, j, 1))),
                pl.BlockSpec((piece_rows, tile), lambda t, j, s: (0, jnp.where(t == 1, j, 0))),
            ],
        ),
        out_shape=[piece, piece],
        compiler_params=params(),
        cost_estimate=declared,
    )(scalars, gradient, weights)


def finish_kernel(counts, *refs):
    out = refs[-1]
    position = 0
    for piece, count in enumerate(counts):

        @pl.when(pl.program_id(0) == piece)
        def _():
            total = refs[position][...].astype(f32)
            for i in range(1, count):
                total = total + refs[position + i][...].astype(f32)
            out[...] = total.astype(out.dtype)

        position += count


def finish(groups, link):
    piece_rows, width = groups[0][0].shape
    tile = width // 2

    def place(piece):
        def index(p, j):
            return (0, jnp.where(p == piece, j, jnp.where(p < piece, 0, 1)))

        return index

    in_specs = [
        pl.BlockSpec((piece_rows, tile), place(piece))
        for piece, group in enumerate(groups)
        for _ in group
    ]
    return pl.pallas_call(
        functools.partial(finish_kernel, tuple(len(group) for group in groups)),
        grid=(len(groups), 2),
        in_specs=in_specs + [pl.BlockSpec(memory_space=pl.ANY)] * len(link),
        out_specs=pl.BlockSpec((piece_rows, tile), lambda p, j: (p, j)),
        out_shape=jax.ShapeDtypeStruct((len(groups) * piece_rows, width), bf16),
        compiler_params=params(),
        cost_estimate=declared,
    )(*[array for group in groups for array in group], *link)


def low_kernel(tenants, rows, expand, link, out):
    out[...] = lax.dot_general(
        rows[...], expand[0], contract_last, preferred_element_type=f32
    ).astype(out.dtype)


def low_product(tenants, gradient, expand, link):
    count_of_rows, depth = gradient.shape
    rank = expand.shape[1]
    return pl.pallas_call(
        low_kernel,
        grid_spec=pltpu.PrefetchScalarGridSpec(
            num_scalar_prefetch=1,
            grid=(count_of_rows // row_block,),
            in_specs=[
                pl.BlockSpec((row_block, depth), lambda b, s: (b, 0)),
                pl.BlockSpec((1, rank, depth), lambda b, s: (s[b], 0, 0)),
                pl.BlockSpec(memory_space=pl.ANY),
            ],
            out_specs=pl.BlockSpec((row_block, rank), lambda b, s: (b, 0)),
        ),
        out_shape=jax.ShapeDtypeStruct((count_of_rows, rank), bf16),
        compiler_params=params(),
        cost_estimate=declared,
    )(tenants, gradient, expand, link)


def scale_kernel(ranks, scales, low, link, out):
    columns = lax.broadcasted_iota(jnp.int32, (row_block, low.shape[1]), 1)
    for b in range(low.shape[0] // row_block):
        here = pl.ds(b * row_block, row_block)
        kept = jnp.where(columns < ranks[b], low[here, :].astype(f32) * scales[b], 0.0)
        out[here, :] = kept.astype(out.dtype)


def scaled_low(ranks, scales, low, link):
    whole = pl.BlockSpec(memory_space=pltpu.VMEM)
    return pl.pallas_call(
        scale_kernel,
        in_specs=[pl.BlockSpec(memory_space=pltpu.SMEM)] * 2
        + [whole, pl.BlockSpec(memory_space=pl.ANY)],
        out_specs=whole,
        out_shape=jax.ShapeDtypeStruct(low.shape, bf16),
        compiler_params=params(),
        cost_estimate=declared,
    )(ranks, scales, low, link)


def factor_kernel(slots_each, slots, scales, left, right, *refs):
    own = refs[-1]
    own[...] = jnp.zeros_like(own)
    for b in range(left.shape[0] // row_block):
        slot = slots[b]

        @pl.when(slot < slots_each)
        def _():
            here = pl.ds(b * row_block, row_block)
            piece = lax.dot_general(
                left[here, :], right[here, :], contract_first, preferred_element_type=f32
            )
            own[slot] += piece * scales[b]


def factor_sums(slots, scales, left, right, slots_each, link):
    whole = pl.BlockSpec(memory_space=pltpu.VMEM)
    return pl.pallas_call(
        functools.partial(factor_kernel, slots_each),
        in_specs=[pl.BlockSpec(memory_space=pltpu.SMEM)] * 2
        + [whole] * 2
        + [pl.BlockSpec(memory_space=pl.ANY)] * len(link),
        out_specs=whole,
        out_shape=jax.ShapeDtypeStruct((slots_each, left.shape[1], right.shape[1]), f32),
        compiler_params=params(),
        cost_estimate=declared,
    )(slots, scales, left, right, *link)


def per_device(
    owner_count,
    gradient,
    projection_input,
    saved_lowrank,
    weights,
    shrink,
    expand,
    tenant_per_block,
    tenant_adapter_rank,
    tenant_owner_index,
):
    count_of_rows, width = gradient.shape
    blocks = count_of_rows // row_block
    tenants = tenant_adapter_rank.shape[0]
    rank_extent = shrink.shape[2]
    node = lax.axis_index("tensor") // 2
    side = lax.axis_index("tensor") % 2
    owner = lax.axis_index("dp")
    at_end = (node == 0) | (node == 3)
    piece_rows = count_of_rows // 2
    lower, upper = 0, 1
    link = []

    roles = (at_end, jnp.logical_not(at_end))

    def run(dest, column, piece, adds):
        scalars = (dest * 2 + column, piece) + roles
        scalars = jnp.stack([jnp.asarray(v, jnp.int32) for v in scalars])
        out = product(scalars, gradient, weights, None, piece_rows, width, adds, link)
        link[:] = [out]
        return out

    def swap(x, active):
        pairs = []
        for z in active:
            pairs += [(2 * z, 2 * z + 1), (2 * z + 1, 2 * z)]
        return lax.ppermute(x, "tensor", pairs)

    def along(x, hops):
        return lax.ppermute(
            x, "tensor", [(2 * a + y, 2 * b + y) for a, b in hops for y in range(2)]
        )

    nodes = 4
    every = (0, 1, 2, 3)
    from_ends = [(0, 1), (3, 2)]
    across = [(1, 2), (2, 1)]
    to_ends = [(1, 0), (2, 3)]
    pairwise = from_ends + to_ends
    def exchange(x):
        pairs = []
        for group in range(2):
            for y in range(2):
                pairs += [(group * 8 + 2 * a + y, group * 8 + 2 * b + y) for a, b in across]
                pairs += [(group * 8 + 2 * z + y, (1 - group) * 8 + 2 * z + y) for z in (0, 3)]
        return lax.ppermute(x, ("groups", "tensor"), pairs)

    first_half = node < 2
    far = jnp.where(first_half, 3, 0)
    beyond = jnp.where(first_half, 2, 1)
    nearer = jnp.where(first_half, 1, 2)
    near_end = jnp.where(first_half, 0, 3)
    same, other = side, 1 - side

    def all_owners(x):
        return lax.all_gather(x, "dp", axis=0, tiled=True)

    block_tenants = jnp.zeros((owner_count * blocks,), jnp.int32)
    for hop in range(owner_count):
        pairs = [(i, (i + hop) % owner_count) for i in range(owner_count)]
        theirs = lax.ppermute(tenant_per_block, "dp", pairs) if hop else tenant_per_block
        place = lax.rem(owner - hop + owner_count, owner_count) * blocks
        block_tenants = lax.dynamic_update_slice_in_dim(block_tenants, theirs, place, 0)
    tenant_ids = jnp.arange(tenants, dtype=jnp.int32)
    matches = block_tenants[:, None] == tenant_ids[None, :]
    block_ranks = jnp.sum(jnp.where(matches, tenant_adapter_rank[None, :], 0), axis=1)
    block_scales = adapter_alpha / block_ranks.astype(f32)
    key = tenant_owner_index * tenants + tenant_ids
    slot_of = jnp.sum((key[None, :] < key[:, None]).astype(jnp.int32), axis=1)
    slots_each = tenants // owner_count
    slot_here = lax.rem(slot_of - owner * slots_each + tenants, tenants)
    block_slots = jnp.sum(jnp.where(matches, slot_here[None, :], 0), axis=1)

    own_ranks = lax.dynamic_slice_in_dim(block_ranks, owner * blocks, blocks, 0)
    own_scales = lax.dynamic_slice_in_dim(block_scales, owner * blocks, blocks, 0)

    def adapter_space():
        part = low_product(tenant_per_block, gradient, expand, link[0])
        link[:] = [part]
        return lax.psum(part, "tensor")

    def scale_low(low):
        out = scaled_low(own_ranks, own_scales, low, link[0])
        link[:] = [out]
        return out

    def expand_gradient():
        kept = jnp.arange(rank_extent, dtype=jnp.int32)[None, :] < block_ranks[:, None]
        saved = all_owners(saved_lowrank).reshape(-1, row_block, rank_extent)
        saved = (saved * kept[:, None, :].astype(bf16)).reshape(-1, rank_extent)
        out = factor_sums(
            block_slots, block_scales, saved, all_owners(gradient), slots_each, link
        )
        link[:] = [out]
        return out

    def shrink_gradient(low):
        out = factor_sums(
            block_slots, jnp.ones_like(block_scales), all_owners(projection_input), all_owners(low),
            slots_each, link,
        )
        link[:] = [out]
        return out

    firsts = (jnp.where(at_end, far, near_end) * 2 + other, upper, far * 2 + other, lower)
    out_y, out_z = product_pair(
        jnp.stack([jnp.asarray(v, jnp.int32) for v in firsts]),
        gradient, weights, piece_rows, width,
    )
    y1, direct_a = swap(out_y, every), along(out_z, pairwise)
    link[:] = [out_z]
    low_whole = adapter_space()
    y2 = swap(run(beyond, other, lower, []), every)
    direct_b = along(run(far, same, lower, []), pairwise)
    out = run(
        far,
        jnp.where(at_end, same, other),
        jnp.where(at_end, upper, lower),
        [(y1, 1), (direct_a, 2)],
    )
    upper_1, direct_a = along(out, pairwise), exchange(out)
    y3 = swap(run(jnp.where(at_end, beyond, far), other, upper, []), every)
    out = run(jnp.where(at_end, beyond, far), same, lower, [(y2, 1), (direct_b, 2)])
    lower_2, direct_b = along(out, pairwise), exchange(out)
    y4 = swap(run(jnp.where(at_end, nearer, beyond), other, lower, []), every)
    out = run(
        jnp.where(at_end, beyond, near_end),
        jnp.where(at_end, same, other),
        jnp.where(at_end, upper, lower),
        [(y3, 1), (direct_a, 2)],
    )
    both_3 = along(out, pairwise)
    grad_expand = expand_gradient()
    y5 = swap(run(jnp.where(at_end, nearer, beyond), other, upper, []), every)
    upper_far = exchange(run(far, same, upper, [(y3, 0), (upper_1, 0)]))
    out = run(jnp.where(at_end, nearer, near_end), same, lower, [(y4, 1), (direct_b, 2)])
    both_4 = along(out, pairwise)
    low = scale_low(low_whole)
    y6 = swap(run(node, other, upper, []), every)
    lower_4 = exchange(run(beyond, same, lower, [(y4, 0), (lower_2, 0)]))
    out = run(
        jnp.where(at_end, nearer, near_end), same, upper, [(y5, 1), (y1, 2), (upper_far, 2)]
    )
    both_5 = along(out, pairwise)
    y7 = swap(run(node, other, lower, [(both_3, 1)]), every)
    upper_4 = along(run(beyond, same, upper, [(y5, 0), (both_3, 0)]), across)
    link += [both_4, lower_4]
    grad_shrink = shrink_gradient(low)
    def base(piece, adds):
        in_piece = piece_rows // row_block
        scalars = [node * 2 + side, jnp.int32(piece)] + [jnp.asarray(r, jnp.int32) for r in roles]
        scalars += [tenant_per_block[piece * in_piece + i] for i in range(in_piece)]
        out = product(
            jnp.stack(scalars).astype(jnp.int32),
            gradient, weights, piece, piece_rows, width, adds, link, (low, shrink),
        )
        link[:] = [out]
        return out

    lower_base = base(lower, [(both_4, 0), (lower_4, 2)])
    upper_base = base(upper, [(y6, 0)])
    input_gradient = finish([[lower_base, y7], [upper_base, both_5, upper_4]], [])
    return (input_gradient, grad_shrink, grad_expand)


def per_device_any(
    query_cotangent,
    projection_input,
    saved_lowrank,
    query_matrix,
    adapter_shrink,
    adapter_expand,
    tenant_per_block,
    tenant_adapter_rank,
    tenant_owner_index,
):
    count_of_rows, shard_extent = query_cotangent.shape
    block_count = count_of_rows // 128
    tenant_count = tenant_adapter_rank.shape[0]
    rank_extent = adapter_shrink.shape[2]
    frozen_product = lax.psum_scatter(
        lax.dot_general(
            query_matrix,
            query_cotangent,
            contract_last,
            preferred_element_type=jnp.float32,
        ).astype(jnp.bfloat16),
        "tensor",
        scatter_dimension=0,
        tiled=True,
    ).astype(jnp.float32)
    tenant_ids = jnp.arange(tenant_count, dtype=jnp.int32)
    matches = tenant_per_block[:, None] == tenant_ids[None, :]
    rank_per_block = jnp.sum(jnp.where(matches, tenant_adapter_rank[None, :], 0), axis=1).astype(
        jnp.float32
    )
    scale_per_block = adapter_alpha / rank_per_block
    block_mask = (
        jnp.arange(rank_extent).astype(jnp.float32)[None, :] < rank_per_block[:, None]
    ).astype(jnp.float32)
    gradient_per_block = query_cotangent.reshape(block_count, 128, shard_extent)
    expand_per_block = jnp.take(adapter_expand, tenant_per_block, axis=0)
    low_part = jnp.einsum(
        "zuh,zsh->zus", gradient_per_block, expand_per_block, preferred_element_type=jnp.float32
    )
    low_whole = lax.psum(low_part.astype(jnp.bfloat16), "tensor").astype(jnp.float32)
    lowrank_bfloat = (low_whole * (scale_per_block[:, None, None] * block_mask[:, None, :])).astype(
        jnp.bfloat16
    )
    shrink_per_block = jnp.take(adapter_shrink, tenant_per_block, axis=0)
    adapter_term = jnp.einsum(
        "uwq,ueq->uwe", lowrank_bfloat, shrink_per_block, preferred_element_type=jnp.float32
    )
    input_gradient = (frozen_product.T + adapter_term.reshape(count_of_rows, shard_extent)).astype(
        jnp.bfloat16
    )
    slot_order = jnp.argsort(tenant_owner_index * tenant_count + tenant_ids)
    slot_of = jnp.argsort(slot_order)
    block_slot = jnp.sum(jnp.where(matches, slot_of[None, :], 0), axis=1)
    block_select = (block_slot[:, None] == tenant_ids[None, :]).astype(jnp.float32)
    saved_lowrank_masked = saved_lowrank.reshape(block_count, 128, rank_extent) * block_mask[
        :, None, :
    ].astype(jnp.bfloat16)
    input_per_block = projection_input.reshape(block_count, 128, shard_extent)
    shrink_piece = jnp.einsum(
        "tme,tmj->tej", input_per_block, lowrank_bfloat, preferred_element_type=jnp.float32
    )
    expand_piece = jnp.einsum(
        "paw,pan->pwn", saved_lowrank_masked, gradient_per_block, preferred_element_type=jnp.float32
    )
    expand_piece = expand_piece * scale_per_block[:, None, None]
    shrink_slots = jnp.einsum(
        "bs,bdr->sdr", block_select, shrink_piece, precision=lax.Precision.HIGHEST
    )
    expand_slots = jnp.einsum(
        "bs,brd->srd", block_select, expand_piece, precision=lax.Precision.HIGHEST
    )
    grad_shrink, grad_expand = (
        lax.psum_scatter(
            shrink_slots.astype(jnp.bfloat16), "dp", scatter_dimension=0, tiled=True
        ).astype(jnp.float32),
        lax.psum_scatter(
            expand_slots.astype(jnp.bfloat16), "dp", scatter_dimension=0, tiled=True
        ).astype(jnp.float32),
    )
    return (input_gradient, grad_shrink, grad_expand)


def solution(mesh):
    placed = (
        P(("groups", "dp"), "tensor"),
        P(("groups", "dp"), "tensor"),
        P(("groups", "dp"), None),
        P(None, "tensor"),
        P(None, "tensor", None),
        P(None, None, "tensor"),
        P(("groups", "dp")),
        P(),
        P(),
    )
    body = per_device_any
    if mesh.shape["tensor"] == 8 and mesh.shape["groups"] == 2:
        body = functools.partial(per_device, mesh.shape["dp"])
    return jax.shard_map(
        body,
        mesh=mesh,
        in_specs=placed,
        out_specs=(
            P(("groups", "dp"), "tensor"),
            P(("groups", "dp"), "tensor", None),
            P(("groups", "dp"), None, "tensor"),
        ),
        check_vma=False,
    )
```

```python
import functools

import jax
import jax.numpy as jnp
from jax import lax
from jax.experimental import pallas as pl
from jax.experimental.pallas import tpu as pltpu
from jax.sharding import PartitionSpec as P

adapter_alpha = 32.0
row_block = 128
bf16 = jnp.bfloat16
f32 = jnp.float32
contract_last = (((1,), (1,)), ((), ()))
contract_first = (((0,), (0,)), ((), ()))
vmem_bytes = 40 * 1024 * 1024
declared = pl.CostEstimate(flops=10**12, bytes_accessed=10**9, transcendentals=0)


def params():
    return pltpu.CompilerParams(vmem_limit_bytes=vmem_bytes)


def product_kernel(modes, block_count, *refs):
    position = 1
    rows, weights = refs[1], refs[2]
    position = 3
    total = lax.dot_general(
        rows[...], weights[...], contract_last, preferred_element_type=f32
    )
    for mode in modes:
        addend = refs[position][...].astype(f32)
        if mode:
            addend = addend * refs[0][1 + mode].astype(f32)
        total = total + addend
        position += 1
    if block_count:
        low = refs[position]
        position += 1
        terms = []
        for i in range(block_count):
            terms.append(
                lax.dot_general(
                    low[i * row_block : (i + 1) * row_block, :],
                    refs[position][0],
                    contract_last,
                    preferred_element_type=f32,
                )
            )
            position += 1
        total = total + jnp.concatenate(terms, axis=0)
    refs[-1][...] = total.astype(refs[-1].dtype)


def product(scalars, gradient, weights, piece, piece_rows, width, adds, link, adapter=None):
    depth = gradient.shape[1]
    tile = min(width, 512)
    while width % tile:
        tile //= 2
    steps = width // tile
    in_specs = [
        pl.BlockSpec((piece_rows, depth), lambda j, s: (s[1], 0)),
        pl.BlockSpec((tile, depth), lambda j, s: (s[0] * steps + j, 0)),
    ]
    operands = [gradient, weights]
    for array, _ in adds:
        in_specs.append(pl.BlockSpec((piece_rows, tile), lambda j, s: (0, j)))
        operands.append(array)
    block_count = 0
    if adapter is not None:
        low, shrink = adapter
        rank = low.shape[1]
        block_count = piece_rows // row_block
        in_specs.append(pl.BlockSpec((piece_rows, rank), lambda j, s: (piece, 0)))
        operands.append(low)
        for i in range(block_count):
            in_specs.append(
                pl.BlockSpec((1, tile, rank), functools.partial(lambda j, s, i: (s[4 + i], j, 0), i=i))
            )
            operands.append(shrink)
    for array in link:
        in_specs.append(pl.BlockSpec(memory_space=pl.ANY))
        operands.append(array)
    return pl.pallas_call(
        functools.partial(product_kernel, tuple(mode for _, mode in adds), block_count),
        grid_spec=pltpu.PrefetchScalarGridSpec(
            num_scalar_prefetch=1,
            grid=(steps,),
            in_specs=in_specs,
            out_specs=pl.BlockSpec((piece_rows, tile), lambda j, s: (0, j)),
        ),
        out_shape=jax.ShapeDtypeStruct((piece_rows, width), bf16),
        compiler_params=params(),
        cost_estimate=declared,
    )(scalars, *operands)


def pair_kernel(scalars, rows, weights, first, second):
    part = lax.dot_general(
        rows[...], weights[...], contract_last, preferred_element_type=f32
    ).astype(bf16)

    @pl.when(pl.program_id(0) == 0)
    def _():
        first[...] = part

    @pl.when(pl.program_id(0) == 1)
    def _():
        second[...] = part


def product_pair(scalars, gradient, weights, piece_rows, width):
    depth = gradient.shape[1]
    tile = width // 2
    piece = jax.ShapeDtypeStruct((piece_rows, width), bf16)
    return pl.pallas_call(
        pair_kernel,
        grid_spec=pltpu.PrefetchScalarGridSpec(
            num_scalar_prefetch=1,
            grid=(2, 2),
            in_specs=[
                pl.BlockSpec((piece_rows, depth), lambda t, j, s: (s[2 * t + 1], 0)),
                pl.BlockSpec((tile, depth), lambda t, j, s: (s[2 * t] * 2 + j, 0)),
            ],
            out_specs=[
                pl.BlockSpec((piece_rows, tile), lambda t, j, s: (0, jnp.where(t == 0, j, 1))),
                pl.BlockSpec((piece_rows, tile), lambda t, j, s: (0, jnp.where(t == 1, j, 0))),
            ],
        ),
        out_shape=[piece, piece],
        compiler_params=params(),
        cost_estimate=declared,
    )(scalars, gradient, weights)


def finish_kernel(counts, inner, *refs):
    out, staged, done = refs[-3:]
    rows = refs[0].shape[0]
    part = rows // 2
    copies = []
    position = 0
    for piece, count in enumerate(counts):
        for half in range(2):
            here = slice(half * part, (half + 1) * part)
            total = refs[position][here, :].astype(f32)
            for i in range(1, count):
                addend = refs[position + i][here, :].astype(f32)
                if piece and i == count - 1:
                    addend = addend * inner[0].astype(f32)
                total = total + addend
            index = 2 * piece + half
            staged[index] = total.astype(staged.dtype)
            copy = pltpu.make_async_copy(
                staged.at[index], out.at[pl.ds(index * part, part), :], done.at[index]
            )
            copy.start()
            copies.append(copy)
        position += count
    for copy in copies:
        copy.wait()


def finish(inner, groups):
    rows, width = groups[0][0].shape
    arrays = [array for group in groups for array in group]
    parts = 2 * len(groups)
    return pl.pallas_call(
        functools.partial(finish_kernel, tuple(len(group) for group in groups)),
        in_specs=[pl.BlockSpec(memory_space=pltpu.SMEM)]
        + [pl.BlockSpec(memory_space=pltpu.VMEM)] * len(arrays),
        out_specs=pl.BlockSpec(memory_space=pl.ANY),
        out_shape=jax.ShapeDtypeStruct((len(groups) * rows, width), bf16),
        scratch_shapes=[
            pltpu.VMEM((parts, rows // 2, width), bf16),
            pltpu.SemaphoreType.DMA((parts,)),
        ],
        compiler_params=params(),
        cost_estimate=declared,
    )(inner, *arrays)


def low_kernel(tenants, rows, expand, link, out):
    out[...] = lax.dot_general(
        rows[...], expand[0], contract_last, preferred_element_type=f32
    ).astype(out.dtype)


def low_product(tenants, gradient, expand, link):
    count_of_rows, depth = gradient.shape
    rank = expand.shape[1]
    return pl.pallas_call(
        low_kernel,
        grid_spec=pltpu.PrefetchScalarGridSpec(
            num_scalar_prefetch=1,
            grid=(count_of_rows // row_block,),
            in_specs=[
                pl.BlockSpec((row_block, depth), lambda b, s: (b, 0)),
                pl.BlockSpec((1, rank, depth), lambda b, s: (s[b], 0, 0)),
                pl.BlockSpec(memory_space=pl.ANY),
            ],
            out_specs=pl.BlockSpec((row_block, rank), lambda b, s: (b, 0)),
        ),
        out_shape=jax.ShapeDtypeStruct((count_of_rows, rank), bf16),
        compiler_params=params(),
        cost_estimate=declared,
    )(tenants, gradient, expand, link)


def scale_kernel(ranks, scales, low, link, out):
    columns = lax.broadcasted_iota(jnp.int32, (row_block, low.shape[1]), 1)
    for b in range(low.shape[0] // row_block):
        here = pl.ds(b * row_block, row_block)
        kept = jnp.where(columns < ranks[b], low[here, :].astype(f32) * scales[b], 0.0)
        out[here, :] = kept.astype(out.dtype)


def scaled_low(ranks, scales, low, link):
    whole = pl.BlockSpec(memory_space=pltpu.VMEM)
    return pl.pallas_call(
        scale_kernel,
        in_specs=[pl.BlockSpec(memory_space=pltpu.SMEM)] * 2
        + [whole, pl.BlockSpec(memory_space=pl.ANY)],
        out_specs=whole,
        out_shape=jax.ShapeDtypeStruct(low.shape, bf16),
        compiler_params=params(),
        cost_estimate=declared,
    )(ranks, scales, low, link)


def factor_kernel(slots_each, slots, scales, left, right, *refs):
    own = refs[-1]
    own[...] = jnp.zeros_like(own)
    for b in range(left.shape[0] // row_block):
        slot = slots[b]

        @pl.when(slot < slots_each)
        def _():
            here = pl.ds(b * row_block, row_block)
            piece = lax.dot_general(
                left[here, :], right[here, :], contract_first, preferred_element_type=f32
            )
            own[slot] += piece * scales[b]


def factor_sums(slots, scales, left, right, slots_each, link):
    whole = pl.BlockSpec(memory_space=pltpu.VMEM)
    return pl.pallas_call(
        functools.partial(factor_kernel, slots_each),
        in_specs=[pl.BlockSpec(memory_space=pltpu.SMEM)] * 2
        + [whole] * 2
        + [pl.BlockSpec(memory_space=pl.ANY)] * len(link),
        out_specs=whole,
        out_shape=jax.ShapeDtypeStruct((slots_each, left.shape[1], right.shape[1]), f32),
        compiler_params=params(),
        cost_estimate=declared,
    )(slots, scales, left, right, *link)


def per_device(
    owner_count,
    gradient,
    projection_input,
    saved_lowrank,
    weights,
    shrink,
    expand,
    tenant_per_block,
    tenant_adapter_rank,
    tenant_owner_index,
):
    count_of_rows, width = gradient.shape
    blocks = count_of_rows // row_block
    tenants = tenant_adapter_rank.shape[0]
    rank_extent = shrink.shape[2]
    node = lax.axis_index("tensor") // 2
    side = lax.axis_index("tensor") % 2
    owner = lax.axis_index("dp")
    at_end = (node == 0) | (node == 3)
    piece_rows = count_of_rows // 2
    lower, upper = 0, 1
    link = []

    roles = (at_end, jnp.logical_not(at_end))

    def run(dest, column, piece, adds):
        scalars = (dest * 2 + column, piece) + roles
        scalars = jnp.stack([jnp.asarray(v, jnp.int32) for v in scalars])
        out = product(scalars, gradient, weights, None, piece_rows, width, adds, link)
        link[:] = [out]
        return out

    def swap(x, active):
        pairs = []
        for z in active:
            pairs += [(2 * z, 2 * z + 1), (2 * z + 1, 2 * z)]
        return lax.ppermute(x, "tensor", pairs)

    def along(x, hops):
        return lax.ppermute(
            x, "tensor", [(2 * a + y, 2 * b + y) for a, b in hops for y in range(2)]
        )

    nodes = 4
    every = (0, 1, 2, 3)
    from_ends = [(0, 1), (3, 2)]
    across = [(1, 2), (2, 1)]
    to_ends = [(1, 0), (2, 3)]
    pairwise = from_ends + to_ends
    def exchange(x):
        pairs = []
        for group in range(2):
            for y in range(2):
                pairs += [(group * 8 + 2 * a + y, group * 8 + 2 * b + y) for a, b in across]
                pairs += [(group * 8 + 2 * z + y, (1 - group) * 8 + 2 * z + y) for z in (0, 3)]
        return lax.ppermute(x, ("groups", "tensor"), pairs)

    first_half = node < 2
    far = jnp.where(first_half, 3, 0)
    beyond = jnp.where(first_half, 2, 1)
    nearer = jnp.where(first_half, 1, 2)
    near_end = jnp.where(first_half, 0, 3)
    same, other = side, 1 - side

    def all_owners(x):
        return lax.all_gather(x, "dp", axis=0, tiled=True)

    block_tenants = jnp.zeros((owner_count * blocks,), jnp.int32)
    for hop in range(owner_count):
        pairs = [(i, (i + hop) % owner_count) for i in range(owner_count)]
        theirs = lax.ppermute(tenant_per_block, "dp", pairs) if hop else tenant_per_block
        place = lax.rem(owner - hop + owner_count, owner_count) * blocks
        block_tenants = lax.dynamic_update_slice_in_dim(block_tenants, theirs, place, 0)
    tenant_ids = jnp.arange(tenants, dtype=jnp.int32)
    matches = block_tenants[:, None] == tenant_ids[None, :]
    block_ranks = jnp.sum(jnp.where(matches, tenant_adapter_rank[None, :], 0), axis=1)
    block_scales = adapter_alpha / block_ranks.astype(f32)
    key = tenant_owner_index * tenants + tenant_ids
    slot_of = jnp.sum((key[None, :] < key[:, None]).astype(jnp.int32), axis=1)
    slots_each = tenants // owner_count
    slot_here = lax.rem(slot_of - owner * slots_each + tenants, tenants)
    block_slots = jnp.sum(jnp.where(matches, slot_here[None, :], 0), axis=1)

    own_ranks = lax.dynamic_slice_in_dim(block_ranks, owner * blocks, blocks, 0)
    own_scales = lax.dynamic_slice_in_dim(block_scales, owner * blocks, blocks, 0)

    def adapter_space():
        part = low_product(tenant_per_block, gradient, expand, link[0])
        link[:] = [part]
        return lax.psum(part, "tensor")

    def scale_low(low):
        out = scaled_low(own_ranks, own_scales, low, link[0])
        link[:] = [out]
        return out

    def expand_gradient():
        kept = jnp.arange(rank_extent, dtype=jnp.int32)[None, :] < block_ranks[:, None]
        saved = all_owners(saved_lowrank).reshape(-1, row_block, rank_extent)
        saved = (saved * kept[:, None, :].astype(bf16)).reshape(-1, rank_extent)
        out = factor_sums(
            block_slots, block_scales, saved, all_owners(gradient), slots_each, link
        )
        link[:] = [out]
        return out

    def shrink_gradient(low):
        out = factor_sums(
            block_slots, jnp.ones_like(block_scales), all_owners(projection_input), all_owners(low),
            slots_each, link,
        )
        link[:] = [out]
        return out

    firsts = (jnp.where(at_end, far, near_end) * 2 + other, upper, far * 2 + other, lower)
    out_y, out_z = product_pair(
        jnp.stack([jnp.asarray(v, jnp.int32) for v in firsts]),
        gradient, weights, piece_rows, width,
    )
    y1, direct_a = swap(out_y, every), along(out_z, pairwise)
    link[:] = [out_z]
    low_whole = adapter_space()
    y2 = swap(run(beyond, other, lower, []), every)
    direct_b = along(run(far, same, lower, []), pairwise)
    out = run(
        far,
        jnp.where(at_end, same, other),
        jnp.where(at_end, upper, lower),
        [(y1, 1), (direct_a, 2)],
    )
    upper_1, direct_a = along(out, pairwise), exchange(out)
    y3 = swap(run(jnp.where(at_end, beyond, far), other, upper, []), every)
    out = run(jnp.where(at_end, beyond, far), same, lower, [(y2, 1), (direct_b, 2)])
    lower_2, direct_b = along(out, pairwise), exchange(out)
    y4 = swap(run(jnp.where(at_end, nearer, beyond), other, lower, []), every)
    out = run(
        jnp.where(at_end, beyond, near_end),
        jnp.where(at_end, same, other),
        jnp.where(at_end, upper, lower),
        [(y3, 1), (direct_a, 2)],
    )
    both_3 = along(out, pairwise)
    grad_expand = expand_gradient()
    y5 = swap(run(jnp.where(at_end, nearer, beyond), other, upper, []), every)
    upper_far = exchange(run(far, same, upper, [(y3, 0), (upper_1, 0)]))
    out = run(jnp.where(at_end, nearer, near_end), same, lower, [(y4, 1), (direct_b, 2)])
    both_4 = along(out, pairwise)
    low = scale_low(low_whole)
    y6 = swap(run(node, other, upper, []), every)
    lower_4 = exchange(run(beyond, same, lower, [(y4, 0), (lower_2, 0)]))
    out = run(
        jnp.where(at_end, nearer, near_end), same, upper, [(y5, 1), (y1, 2), (upper_far, 2)]
    )
    both_5 = along(out, pairwise)
    y7 = swap(run(node, other, lower, [(both_3, 1)]), every)
    upper_4 = exchange(run(beyond, same, upper, [(y5, 0), (both_3, 0)]))
    link += [both_4, lower_4]
    grad_shrink = shrink_gradient(low)
    def base(piece, adds):
        in_piece = piece_rows // row_block
        scalars = [node * 2 + side, jnp.int32(piece)] + [jnp.asarray(r, jnp.int32) for r in roles]
        scalars += [tenant_per_block[piece * in_piece + i] for i in range(in_piece)]
        out = product(
            jnp.stack(scalars).astype(jnp.int32),
            gradient, weights, piece, piece_rows, width, adds, link, (low, shrink),
        )
        link[:] = [out]
        return out

    lower_base = base(lower, [(both_4, 0), (lower_4, 2)])
    upper_base = base(upper, [(y6, 0)])
    inner = jnp.reshape(roles[1].astype(jnp.int32), (1,))
    input_gradient = finish(inner, [[lower_base, y7], [upper_base, both_5, upper_4]])
    return (input_gradient, grad_shrink, grad_expand)


def per_device_any(
    query_cotangent,
    projection_input,
    saved_lowrank,
    query_matrix,
    adapter_shrink,
    adapter_expand,
    tenant_per_block,
    tenant_adapter_rank,
    tenant_owner_index,
):
    count_of_rows, shard_extent = query_cotangent.shape
    block_count = count_of_rows // 128
    tenant_count = tenant_adapter_rank.shape[0]
    rank_extent = adapter_shrink.shape[2]
    frozen_product = lax.psum_scatter(
        lax.dot_general(
            query_matrix,
            query_cotangent,
            contract_last,
            preferred_element_type=jnp.float32,
        ).astype(jnp.bfloat16),
        "tensor",
        scatter_dimension=0,
        tiled=True,
    ).astype(jnp.float32)
    tenant_ids = jnp.arange(tenant_count, dtype=jnp.int32)
    matches = tenant_per_block[:, None] == tenant_ids[None, :]
    rank_per_block = jnp.sum(jnp.where(matches, tenant_adapter_rank[None, :], 0), axis=1).astype(
        jnp.float32
    )
    scale_per_block = adapter_alpha / rank_per_block
    block_mask = (
        jnp.arange(rank_extent).astype(jnp.float32)[None, :] < rank_per_block[:, None]
    ).astype(jnp.float32)
    gradient_per_block = query_cotangent.reshape(block_count, 128, shard_extent)
    expand_per_block = jnp.take(adapter_expand, tenant_per_block, axis=0)
    low_part = jnp.einsum(
        "zuh,zsh->zus", gradient_per_block, expand_per_block, preferred_element_type=jnp.float32
    )
    low_whole = lax.psum(low_part.astype(jnp.bfloat16), "tensor").astype(jnp.float32)
    lowrank_bfloat = (low_whole * (scale_per_block[:, None, None] * block_mask[:, None, :])).astype(
        jnp.bfloat16
    )
    shrink_per_block = jnp.take(adapter_shrink, tenant_per_block, axis=0)
    adapter_term = jnp.einsum(
        "uwq,ueq->uwe", lowrank_bfloat, shrink_per_block, preferred_element_type=jnp.float32
    )
    input_gradient = (frozen_product.T + adapter_term.reshape(count_of_rows, shard_extent)).astype(
        jnp.bfloat16
    )
    slot_order = jnp.argsort(tenant_owner_index * tenant_count + tenant_ids)
    slot_of = jnp.argsort(slot_order)
    block_slot = jnp.sum(jnp.where(matches, slot_of[None, :], 0), axis=1)
    block_select = (block_slot[:, None] == tenant_ids[None, :]).astype(jnp.float32)
    saved_lowrank_masked = saved_lowrank.reshape(block_count, 128, rank_extent) * block_mask[
        :, None, :
    ].astype(jnp.bfloat16)
    input_per_block = projection_input.reshape(block_count, 128, shard_extent)
    shrink_piece = jnp.einsum(
        "tme,tmj->tej", input_per_block, lowrank_bfloat, preferred_element_type=jnp.float32
    )
    expand_piece = jnp.einsum(
        "paw,pan->pwn", saved_lowrank_masked, gradient_per_block, preferred_element_type=jnp.float32
    )
    expand_piece = expand_piece * scale_per_block[:, None, None]
    shrink_slots = jnp.einsum(
        "bs,bdr->sdr", block_select, shrink_piece, precision=lax.Precision.HIGHEST
    )
    expand_slots = jnp.einsum(
        "bs,brd->srd", block_select, expand_piece, precision=lax.Precision.HIGHEST
    )
    grad_shrink, grad_expand = (
        lax.psum_scatter(
            shrink_slots.astype(jnp.bfloat16), "dp", scatter_dimension=0, tiled=True
        ).astype(jnp.float32),
        lax.psum_scatter(
            expand_slots.astype(jnp.bfloat16), "dp", scatter_dimension=0, tiled=True
        ).astype(jnp.float32),
    )
    return (input_gradient, grad_shrink, grad_expand)


def solution(mesh):
    placed = (
        P(("groups", "dp"), "tensor"),
        P(("groups", "dp"), "tensor"),
        P(("groups", "dp"), None),
        P(None, "tensor"),
        P(None, "tensor", None),
        P(None, None, "tensor"),
        P(("groups", "dp")),
        P(),
        P(),
    )
    body = per_device_any
    if mesh.shape["tensor"] == 8 and mesh.shape["groups"] == 2:
        body = functools.partial(per_device, mesh.shape["dp"])
    return jax.shard_map(
        body,
        mesh=mesh,
        in_specs=placed,
        out_specs=(
            P(("groups", "dp"), "tensor"),
            P(("groups", "dp"), "tensor", None),
            P(("groups", "dp"), None, "tensor"),
        ),
        check_vma=False,
    )
```

```python
import functools

import jax
import jax.numpy as jnp
from jax import lax
from jax.experimental import pallas as pl
from jax.experimental.pallas import tpu as pltpu
from jax.sharding import PartitionSpec as P

adapter_alpha = 32.0
row_block = 128
bf16 = jnp.bfloat16
f32 = jnp.float32
contract_last = (((1,), (1,)), ((), ()))
contract_first = (((0,), (0,)), ((), ()))
vmem_bytes = 40 * 1024 * 1024
declared = pl.CostEstimate(flops=10**12, bytes_accessed=10**9, transcendentals=0)


def params():
    return pltpu.CompilerParams(vmem_limit_bytes=vmem_bytes)


def product_kernel(modes, block_count, *refs):
    position = 1
    rows, weights = refs[1], refs[2]
    position = 3
    total = lax.dot_general(
        rows[...], weights[...], contract_last, preferred_element_type=f32
    )
    for mode in modes:
        addend = refs[position][...].astype(f32)
        if mode:
            addend = addend * refs[0][1 + mode].astype(f32)
        total = total + addend
        position += 1
    if block_count:
        low = refs[position]
        position += 1
        terms = []
        for i in range(block_count):
            terms.append(
                lax.dot_general(
                    low[i * row_block : (i + 1) * row_block, :],
                    refs[position][0],
                    contract_last,
                    preferred_element_type=f32,
                )
            )
            position += 1
        total = total + jnp.concatenate(terms, axis=0)
    refs[-1][...] = total.astype(refs[-1].dtype)


def product(scalars, gradient, weights, piece, piece_rows, width, adds, link, adapter=None):
    depth = gradient.shape[1]
    tile = min(width, 512)
    while width % tile:
        tile //= 2
    steps = width // tile
    in_specs = [
        pl.BlockSpec((piece_rows, depth), lambda j, s: (s[1], 0)),
        pl.BlockSpec((tile, depth), lambda j, s: (s[0] * steps + j, 0)),
    ]
    operands = [gradient, weights]
    for array, _ in adds:
        in_specs.append(pl.BlockSpec((piece_rows, tile), lambda j, s: (0, j)))
        operands.append(array)
    block_count = 0
    if adapter is not None:
        low, shrink = adapter
        rank = low.shape[1]
        block_count = piece_rows // row_block
        in_specs.append(pl.BlockSpec((piece_rows, rank), lambda j, s: (piece, 0)))
        operands.append(low)
        for i in range(block_count):
            in_specs.append(
                pl.BlockSpec((1, tile, rank), functools.partial(lambda j, s, i: (s[4 + i], j, 0), i=i))
            )
            operands.append(shrink)
    for array in link:
        in_specs.append(pl.BlockSpec(memory_space=pl.ANY))
        operands.append(array)
    return pl.pallas_call(
        functools.partial(product_kernel, tuple(mode for _, mode in adds), block_count),
        grid_spec=pltpu.PrefetchScalarGridSpec(
            num_scalar_prefetch=1,
            grid=(steps,),
            in_specs=in_specs,
            out_specs=pl.BlockSpec((piece_rows, tile), lambda j, s: (0, j)),
        ),
        out_shape=jax.ShapeDtypeStruct((piece_rows, width), bf16),
        compiler_params=params(),
        cost_estimate=declared,
    )(scalars, *operands)


def pair_kernel(scalars, rows, weights, first, second):
    part = lax.dot_general(
        rows[...], weights[...], contract_last, preferred_element_type=f32
    ).astype(bf16)

    @pl.when(pl.program_id(0) == 0)
    def _():
        first[...] = part

    @pl.when(pl.program_id(0) == 1)
    def _():
        second[...] = part


def product_pair(scalars, gradient, weights, piece_rows, width):
    depth = gradient.shape[1]
    tile = width // 2
    piece = jax.ShapeDtypeStruct((piece_rows, width), bf16)
    return pl.pallas_call(
        pair_kernel,
        grid_spec=pltpu.PrefetchScalarGridSpec(
            num_scalar_prefetch=1,
            grid=(2, 2),
            in_specs=[
                pl.BlockSpec((piece_rows, depth), lambda t, j, s: (s[2 * t + 1], 0)),
                pl.BlockSpec((tile, depth), lambda t, j, s: (s[2 * t] * 2 + j, 0)),
            ],
            out_specs=[
                pl.BlockSpec((piece_rows, tile), lambda t, j, s: (0, jnp.where(t == 0, j, 1))),
                pl.BlockSpec((piece_rows, tile), lambda t, j, s: (0, jnp.where(t == 1, j, 0))),
            ],
        ),
        out_shape=[piece, piece],
        compiler_params=params(),
        cost_estimate=declared,
    )(scalars, gradient, weights)


def finish_kernel(counts, inner, *refs):
    out, staged, done = refs[-3:]
    rows = refs[0].shape[0]
    part = rows // 2
    copies = []
    position = 0
    for piece, count in enumerate(counts):
        for half in range(2):
            here = slice(half * part, (half + 1) * part)
            total = refs[position][here, :].astype(f32)
            for i in range(1, count):
                addend = refs[position + i][here, :].astype(f32)
                if piece and i == count - 1:
                    addend = addend * inner[0].astype(f32)
                total = total + addend
            index = 2 * piece + half
            staged[index] = total.astype(staged.dtype)
            copy = pltpu.make_async_copy(
                staged.at[index], out.at[pl.ds(index * part, part), :], done.at[index]
            )
            copy.start()
            copies.append(copy)
        position += count
    for copy in copies:
        copy.wait()


def finish(inner, groups):
    rows, width = groups[0][0].shape
    arrays = [array for group in groups for array in group]
    parts = 2 * len(groups)
    return pl.pallas_call(
        functools.partial(finish_kernel, tuple(len(group) for group in groups)),
        in_specs=[pl.BlockSpec(memory_space=pltpu.SMEM)]
        + [pl.BlockSpec(memory_space=pltpu.VMEM)] * len(arrays),
        out_specs=pl.BlockSpec(memory_space=pl.ANY),
        out_shape=jax.ShapeDtypeStruct((len(groups) * rows, width), bf16),
        scratch_shapes=[
            pltpu.VMEM((parts, rows // 2, width), bf16),
            pltpu.SemaphoreType.DMA((parts,)),
        ],
        compiler_params=params(),
        cost_estimate=declared,
    )(inner, *arrays)


def low_kernel(tenants, rows, expand, link, out):
    out[...] = lax.dot_general(
        rows[...], expand[0], contract_last, preferred_element_type=f32
    ).astype(out.dtype)


def low_product(tenants, gradient, expand, link):
    count_of_rows, depth = gradient.shape
    rank = expand.shape[1]
    return pl.pallas_call(
        low_kernel,
        grid_spec=pltpu.PrefetchScalarGridSpec(
            num_scalar_prefetch=1,
            grid=(count_of_rows // row_block,),
            in_specs=[
                pl.BlockSpec((row_block, depth), lambda b, s: (b, 0)),
                pl.BlockSpec((1, rank, depth), lambda b, s: (s[b], 0, 0)),
                pl.BlockSpec(memory_space=pl.ANY),
            ],
            out_specs=pl.BlockSpec((row_block, rank), lambda b, s: (b, 0)),
        ),
        out_shape=jax.ShapeDtypeStruct((count_of_rows, rank), bf16),
        compiler_params=params(),
        cost_estimate=declared,
    )(tenants, gradient, expand, link)


def scale_kernel(ranks, scales, low, link, out):
    columns = lax.broadcasted_iota(jnp.int32, (row_block, low.shape[1]), 1)
    for b in range(low.shape[0] // row_block):
        here = pl.ds(b * row_block, row_block)
        kept = jnp.where(columns < ranks[b], low[here, :].astype(f32) * scales[b], 0.0)
        out[here, :] = kept.astype(out.dtype)


def scaled_low(ranks, scales, low, link):
    whole = pl.BlockSpec(memory_space=pltpu.VMEM)
    return pl.pallas_call(
        scale_kernel,
        in_specs=[pl.BlockSpec(memory_space=pltpu.SMEM)] * 2
        + [whole, pl.BlockSpec(memory_space=pl.ANY)],
        out_specs=whole,
        out_shape=jax.ShapeDtypeStruct(low.shape, bf16),
        compiler_params=params(),
        cost_estimate=declared,
    )(ranks, scales, low, link)


def factor_kernel(slots_each, slots, scales, left, right, *refs):
    own = refs[-1]
    own[...] = jnp.zeros_like(own)
    for b in range(left.shape[0] // row_block):
        slot = slots[b]

        @pl.when(slot < slots_each)
        def _():
            here = pl.ds(b * row_block, row_block)
            piece = lax.dot_general(
                left[here, :], right[here, :], contract_first, preferred_element_type=f32
            )
            own[slot] += piece * scales[b]


def factor_sums(slots, scales, left, right, slots_each, link):
    whole = pl.BlockSpec(memory_space=pltpu.VMEM)
    return pl.pallas_call(
        functools.partial(factor_kernel, slots_each),
        in_specs=[pl.BlockSpec(memory_space=pltpu.SMEM)] * 2
        + [whole] * 2
        + [pl.BlockSpec(memory_space=pl.ANY)] * len(link),
        out_specs=whole,
        out_shape=jax.ShapeDtypeStruct((slots_each, left.shape[1], right.shape[1]), f32),
        compiler_params=params(),
        cost_estimate=declared,
    )(slots, scales, left, right, *link)


def per_device(
    owner_count,
    gradient,
    projection_input,
    saved_lowrank,
    weights,
    shrink,
    expand,
    tenant_per_block,
    tenant_adapter_rank,
    tenant_owner_index,
):
    count_of_rows, width = gradient.shape
    blocks = count_of_rows // row_block
    tenants = tenant_adapter_rank.shape[0]
    rank_extent = shrink.shape[2]
    node = lax.axis_index("tensor") // 2
    side = lax.axis_index("tensor") % 2
    owner = lax.axis_index("dp")
    at_end = (node == 0) | (node == 3)
    piece_rows = count_of_rows // 2
    lower, upper = 0, 1
    link = []

    roles = (at_end, jnp.logical_not(at_end))

    def run(dest, column, piece, adds):
        scalars = (dest * 2 + column, piece) + roles
        scalars = jnp.stack([jnp.asarray(v, jnp.int32) for v in scalars])
        out = product(scalars, gradient, weights, None, piece_rows, width, adds, link)
        link[:] = [out]
        return out

    def swap(x, active):
        pairs = []
        for z in active:
            pairs += [(2 * z, 2 * z + 1), (2 * z + 1, 2 * z)]
        return lax.ppermute(x, "tensor", pairs)

    def along(x, hops):
        return lax.ppermute(
            x, "tensor", [(2 * a + y, 2 * b + y) for a, b in hops for y in range(2)]
        )

    nodes = 4
    every = (0, 1, 2, 3)
    from_ends = [(0, 1), (3, 2)]
    across = [(1, 2), (2, 1)]
    to_ends = [(1, 0), (2, 3)]
    pairwise = from_ends + to_ends
    def exchange(x):
        pairs = []
        for group in range(2):
            for y in range(2):
                pairs += [(group * 8 + 2 * a + y, group * 8 + 2 * b + y) for a, b in across]
                pairs += [(group * 8 + 2 * z + y, (1 - group) * 8 + 2 * z + y) for z in (0, 3)]
        return lax.ppermute(x, ("groups", "tensor"), pairs)

    first_half = node < 2
    far = jnp.where(first_half, 3, 0)
    beyond = jnp.where(first_half, 2, 1)
    nearer = jnp.where(first_half, 1, 2)
    near_end = jnp.where(first_half, 0, 3)
    same, other = side, 1 - side

    def all_owners(x):
        return lax.all_gather(x, "dp", axis=0, tiled=True)

    block_tenants = jnp.zeros((owner_count * blocks,), jnp.int32)
    for hop in range(owner_count):
        pairs = [(i, (i + hop) % owner_count) for i in range(owner_count)]
        theirs = lax.ppermute(tenant_per_block, "dp", pairs) if hop else tenant_per_block
        place = lax.rem(owner - hop + owner_count, owner_count) * blocks
        block_tenants = lax.dynamic_update_slice_in_dim(block_tenants, theirs, place, 0)
    tenant_ids = jnp.arange(tenants, dtype=jnp.int32)
    matches = block_tenants[:, None] == tenant_ids[None, :]
    block_ranks = jnp.sum(jnp.where(matches, tenant_adapter_rank[None, :], 0), axis=1)
    block_scales = adapter_alpha / block_ranks.astype(f32)
    key = tenant_owner_index * tenants + tenant_ids
    slot_of = jnp.sum((key[None, :] < key[:, None]).astype(jnp.int32), axis=1)
    slots_each = tenants // owner_count
    slot_here = lax.rem(slot_of - owner * slots_each + tenants, tenants)
    block_slots = jnp.sum(jnp.where(matches, slot_here[None, :], 0), axis=1)

    own_ranks = lax.dynamic_slice_in_dim(block_ranks, owner * blocks, blocks, 0)
    own_scales = lax.dynamic_slice_in_dim(block_scales, owner * blocks, blocks, 0)

    def adapter_space():
        part = low_product(tenant_per_block, gradient, expand, link[0])
        link[:] = [part]
        return lax.psum(part, "tensor")

    def scale_low(low):
        out = scaled_low(own_ranks, own_scales, low, link[0])
        link[:] = [out]
        return out

    def expand_gradient():
        kept = jnp.arange(rank_extent, dtype=jnp.int32)[None, :] < block_ranks[:, None]
        saved = all_owners(saved_lowrank).reshape(-1, row_block, rank_extent)
        saved = (saved * kept[:, None, :].astype(bf16)).reshape(-1, rank_extent)
        out = factor_sums(
            block_slots, block_scales, saved, all_owners(gradient), slots_each, link
        )
        link[:] = [out]
        return out

    def shrink_gradient(low):
        out = factor_sums(
            block_slots, jnp.ones_like(block_scales), all_owners(projection_input), all_owners(low),
            slots_each, link,
        )
        link[:] = [out]
        return out

    firsts = (jnp.where(at_end, far, near_end) * 2 + other, upper, far * 2 + other, lower)
    out_y, out_z = product_pair(
        jnp.stack([jnp.asarray(v, jnp.int32) for v in firsts]),
        gradient, weights, piece_rows, width,
    )
    y1, direct_a = swap(out_y, every), along(out_z, pairwise)
    link[:] = [out_z]
    low_whole = adapter_space()
    y2 = swap(run(beyond, other, lower, []), every)
    direct_b = along(run(far, same, lower, []), pairwise)
    out = run(
        far,
        jnp.where(at_end, same, other),
        jnp.where(at_end, upper, lower),
        [(y1, 1), (direct_a, 2)],
    )
    upper_1, direct_a = along(out, pairwise), exchange(out)
    y3 = swap(run(jnp.where(at_end, beyond, far), other, upper, []), every)
    out = run(jnp.where(at_end, beyond, far), same, lower, [(y2, 1), (direct_b, 2)])
    lower_2, direct_b = along(out, pairwise), exchange(out)
    y4 = swap(run(jnp.where(at_end, nearer, beyond), other, lower, []), every)
    out = run(
        jnp.where(at_end, beyond, near_end),
        jnp.where(at_end, same, other),
        jnp.where(at_end, upper, lower),
        [(y3, 1), (direct_a, 2)],
    )
    both_3 = along(out, pairwise)
    upper_far = exchange(run(far, same, upper, [(y3, 0), (upper_1, 0)]))
    grad_expand = expand_gradient()
    y5 = swap(run(jnp.where(at_end, nearer, beyond), other, upper, []), every)
    out = run(jnp.where(at_end, nearer, near_end), same, lower, [(y4, 1), (direct_b, 2)])
    both_4 = along(out, pairwise)
    lower_4 = exchange(run(beyond, same, lower, [(y4, 0), (lower_2, 0)]))
    low = scale_low(low_whole)
    y6 = swap(run(node, other, upper, []), every)
    out = run(
        jnp.where(at_end, nearer, near_end), same, upper, [(y5, 1), (y1, 2), (upper_far, 2)]
    )
    both_5 = along(out, pairwise)
    y7 = swap(run(node, other, lower, [(both_3, 1)]), every)
    upper_4 = exchange(run(beyond, same, upper, [(y5, 0), (both_3, 0)]))
    link += [both_4, lower_4]
    grad_shrink = shrink_gradient(low)
    def base(piece, adds):
        in_piece = piece_rows // row_block
        scalars = [node * 2 + side, jnp.int32(piece)] + [jnp.asarray(r, jnp.int32) for r in roles]
        scalars += [tenant_per_block[piece * in_piece + i] for i in range(in_piece)]
        out = product(
            jnp.stack(scalars).astype(jnp.int32),
            gradient, weights, piece, piece_rows, width, adds, link, (low, shrink),
        )
        link[:] = [out]
        return out

    lower_base = base(lower, [(both_4, 0), (lower_4, 2)])
    upper_base = base(upper, [(y6, 0)])
    inner = jnp.reshape(roles[1].astype(jnp.int32), (1,))
    input_gradient = finish(inner, [[lower_base, y7], [upper_base, both_5, upper_4]])
    return (input_gradient, grad_shrink, grad_expand)


def per_device_any(
    query_cotangent,
    projection_input,
    saved_lowrank,
    query_matrix,
    adapter_shrink,
    adapter_expand,
    tenant_per_block,
    tenant_adapter_rank,
    tenant_owner_index,
):
    count_of_rows, shard_extent = query_cotangent.shape
    block_count = count_of_rows // 128
    tenant_count = tenant_adapter_rank.shape[0]
    rank_extent = adapter_shrink.shape[2]
    frozen_product = lax.psum_scatter(
        lax.dot_general(
            query_matrix,
            query_cotangent,
            contract_last,
            preferred_element_type=jnp.float32,
        ).astype(jnp.bfloat16),
        "tensor",
        scatter_dimension=0,
        tiled=True,
    ).astype(jnp.float32)
    tenant_ids = jnp.arange(tenant_count, dtype=jnp.int32)
    matches = tenant_per_block[:, None] == tenant_ids[None, :]
    rank_per_block = jnp.sum(jnp.where(matches, tenant_adapter_rank[None, :], 0), axis=1).astype(
        jnp.float32
    )
    scale_per_block = adapter_alpha / rank_per_block
    block_mask = (
        jnp.arange(rank_extent).astype(jnp.float32)[None, :] < rank_per_block[:, None]
    ).astype(jnp.float32)
    gradient_per_block = query_cotangent.reshape(block_count, 128, shard_extent)
    expand_per_block = jnp.take(adapter_expand, tenant_per_block, axis=0)
    low_part = jnp.einsum(
        "zuh,zsh->zus", gradient_per_block, expand_per_block, preferred_element_type=jnp.float32
    )
    low_whole = lax.psum(low_part.astype(jnp.bfloat16), "tensor").astype(jnp.float32)
    lowrank_bfloat = (low_whole * (scale_per_block[:, None, None] * block_mask[:, None, :])).astype(
        jnp.bfloat16
    )
    shrink_per_block = jnp.take(adapter_shrink, tenant_per_block, axis=0)
    adapter_term = jnp.einsum(
        "uwq,ueq->uwe", lowrank_bfloat, shrink_per_block, preferred_element_type=jnp.float32
    )
    input_gradient = (frozen_product.T + adapter_term.reshape(count_of_rows, shard_extent)).astype(
        jnp.bfloat16
    )
    slot_order = jnp.argsort(tenant_owner_index * tenant_count + tenant_ids)
    slot_of = jnp.argsort(slot_order)
    block_slot = jnp.sum(jnp.where(matches, slot_of[None, :], 0), axis=1)
    block_select = (block_slot[:, None] == tenant_ids[None, :]).astype(jnp.float32)
    saved_lowrank_masked = saved_lowrank.reshape(block_count, 128, rank_extent) * block_mask[
        :, None, :
    ].astype(jnp.bfloat16)
    input_per_block = projection_input.reshape(block_count, 128, shard_extent)
    shrink_piece = jnp.einsum(
        "tme,tmj->tej", input_per_block, lowrank_bfloat, preferred_element_type=jnp.float32
    )
    expand_piece = jnp.einsum(
        "paw,pan->pwn", saved_lowrank_masked, gradient_per_block, preferred_element_type=jnp.float32
    )
    expand_piece = expand_piece * scale_per_block[:, None, None]
    shrink_slots = jnp.einsum(
        "bs,bdr->sdr", block_select, shrink_piece, precision=lax.Precision.HIGHEST
    )
    expand_slots = jnp.einsum(
        "bs,brd->srd", block_select, expand_piece, precision=lax.Precision.HIGHEST
    )
    grad_shrink, grad_expand = (
        lax.psum_scatter(
            shrink_slots.astype(jnp.bfloat16), "dp", scatter_dimension=0, tiled=True
        ).astype(jnp.float32),
        lax.psum_scatter(
            expand_slots.astype(jnp.bfloat16), "dp", scatter_dimension=0, tiled=True
        ).astype(jnp.float32),
    )
    return (input_gradient, grad_shrink, grad_expand)


def solution(mesh):
    placed = (
        P(("groups", "dp"), "tensor"),
        P(("groups", "dp"), "tensor"),
        P(("groups", "dp"), None),
        P(None, "tensor"),
        P(None, "tensor", None),
        P(None, None, "tensor"),
        P(("groups", "dp")),
        P(),
        P(),
    )
    body = per_device_any
    if mesh.shape["tensor"] == 8 and mesh.shape["groups"] == 2:
        body = functools.partial(per_device, mesh.shape["dp"])
    return jax.shard_map(
        body,
        mesh=mesh,
        in_specs=placed,
        out_specs=(
            P(("groups", "dp"), "tensor"),
            P(("groups", "dp"), "tensor", None),
            P(("groups", "dp"), None, "tensor"),
        ),
        check_vma=False,
    )
```

```python
import functools

import jax
import jax.numpy as jnp
from jax import lax
from jax.experimental import pallas as pl
from jax.experimental.pallas import tpu as pltpu
from jax.sharding import PartitionSpec as P

adapter_alpha = 32.0
row_block = 128
bf16 = jnp.bfloat16
f32 = jnp.float32
contract_last = (((1,), (1,)), ((), ()))
contract_first = (((0,), (0,)), ((), ()))
vmem_bytes = 40 * 1024 * 1024
declared = pl.CostEstimate(flops=10**12, bytes_accessed=10**9, transcendentals=0)


def params():
    return pltpu.CompilerParams(vmem_limit_bytes=vmem_bytes)


def product_kernel(modes, block_count, *refs):
    position = 1
    rows, weights = refs[1], refs[2]
    position = 3
    total = lax.dot_general(
        rows[...], weights[...], contract_last, preferred_element_type=f32
    )
    for mode in modes:
        addend = refs[position][...].astype(f32)
        if mode:
            addend = addend * refs[0][1 + mode].astype(f32)
        total = total + addend
        position += 1
    if block_count:
        low = refs[position]
        position += 1
        terms = []
        for i in range(block_count):
            terms.append(
                lax.dot_general(
                    low[i * row_block : (i + 1) * row_block, :],
                    refs[position][0],
                    contract_last,
                    preferred_element_type=f32,
                )
            )
            position += 1
        total = total + jnp.concatenate(terms, axis=0)
    refs[-1][...] = total.astype(refs[-1].dtype)


def product(scalars, gradient, weights, piece, piece_rows, width, adds, link, adapter=None):
    depth = gradient.shape[1]
    tile = min(width, 512)
    while width % tile:
        tile //= 2
    steps = width // tile
    in_specs = [
        pl.BlockSpec((piece_rows, depth), lambda j, s: (s[1], 0)),
        pl.BlockSpec((tile, depth), lambda j, s: (s[0] * steps + j, 0)),
    ]
    operands = [gradient, weights]
    for array, _ in adds:
        in_specs.append(pl.BlockSpec((piece_rows, tile), lambda j, s: (0, j)))
        operands.append(array)
    block_count = 0
    if adapter is not None:
        low, shrink = adapter
        rank = low.shape[1]
        block_count = piece_rows // row_block
        in_specs.append(pl.BlockSpec((piece_rows, rank), lambda j, s: (piece, 0)))
        operands.append(low)
        for i in range(block_count):
            in_specs.append(
                pl.BlockSpec((1, tile, rank), functools.partial(lambda j, s, i: (s[4 + i], j, 0), i=i))
            )
            operands.append(shrink)
    for array in link:
        in_specs.append(pl.BlockSpec(memory_space=pl.ANY))
        operands.append(array)
    return pl.pallas_call(
        functools.partial(product_kernel, tuple(mode for _, mode in adds), block_count),
        grid_spec=pltpu.PrefetchScalarGridSpec(
            num_scalar_prefetch=1,
            grid=(steps,),
            in_specs=in_specs,
            out_specs=pl.BlockSpec((piece_rows, tile), lambda j, s: (0, j)),
        ),
        out_shape=jax.ShapeDtypeStruct((piece_rows, width), bf16),
        compiler_params=params(),
        cost_estimate=declared,
    )(scalars, *operands)


def pair_kernel(scalars, rows, weights, first, second):
    part = lax.dot_general(
        rows[...], weights[...], contract_last, preferred_element_type=f32
    ).astype(bf16)

    @pl.when(pl.program_id(0) == 0)
    def _():
        first[...] = part

    @pl.when(pl.program_id(0) == 1)
    def _():
        second[...] = part


def product_pair(scalars, gradient, weights, piece_rows, width):
    depth = gradient.shape[1]
    tile = width // 2
    piece = jax.ShapeDtypeStruct((piece_rows, width), bf16)
    return pl.pallas_call(
        pair_kernel,
        grid_spec=pltpu.PrefetchScalarGridSpec(
            num_scalar_prefetch=1,
            grid=(2, 2),
            in_specs=[
                pl.BlockSpec((piece_rows, depth), lambda t, j, s: (s[2 * t + 1], 0)),
                pl.BlockSpec((tile, depth), lambda t, j, s: (s[2 * t] * 2 + j, 0)),
            ],
            out_specs=[
                pl.BlockSpec((piece_rows, tile), lambda t, j, s: (0, jnp.where(t == 0, j, 1))),
                pl.BlockSpec((piece_rows, tile), lambda t, j, s: (0, jnp.where(t == 1, j, 0))),
            ],
        ),
        out_shape=[piece, piece],
        compiler_params=params(),
        cost_estimate=declared,
    )(scalars, gradient, weights)


def finish_kernel(counts, inner, *refs):
    out, staged, done = refs[-3:]
    rows = refs[0].shape[0]
    part = rows // 2
    copies = []
    position = 0
    for piece, count in enumerate(counts):
        for half in range(2):
            here = slice(half * part, (half + 1) * part)
            total = refs[position][here, :].astype(f32)
            for i in range(1, count):
                addend = refs[position + i][here, :].astype(f32)
                if piece and i == count - 1:
                    addend = addend * inner[0].astype(f32)
                total = total + addend
            index = 2 * piece + half
            staged[index] = total.astype(staged.dtype)
            copy = pltpu.make_async_copy(
                staged.at[index], out.at[pl.ds(index * part, part), :], done.at[index]
            )
            copy.start()
            copies.append(copy)
        position += count
    for copy in copies:
        copy.wait()


def finish(inner, groups):
    rows, width = groups[0][0].shape
    arrays = [array for group in groups for array in group]
    parts = 2 * len(groups)
    return pl.pallas_call(
        functools.partial(finish_kernel, tuple(len(group) for group in groups)),
        in_specs=[pl.BlockSpec(memory_space=pltpu.SMEM)]
        + [pl.BlockSpec(memory_space=pltpu.VMEM)] * len(arrays),
        out_specs=pl.BlockSpec(memory_space=pl.ANY),
        out_shape=jax.ShapeDtypeStruct((len(groups) * rows, width), bf16),
        scratch_shapes=[
            pltpu.VMEM((parts, rows // 2, width), bf16),
            pltpu.SemaphoreType.DMA((parts,)),
        ],
        compiler_params=params(),
        cost_estimate=declared,
    )(inner, *arrays)


def low_kernel(tenants, rows, expand, link, out):
    out[...] = lax.dot_general(
        rows[...], expand[0], contract_last, preferred_element_type=f32
    ).astype(out.dtype)


def low_product(tenants, gradient, expand, link):
    count_of_rows, depth = gradient.shape
    rank = expand.shape[1]
    return pl.pallas_call(
        low_kernel,
        grid_spec=pltpu.PrefetchScalarGridSpec(
            num_scalar_prefetch=1,
            grid=(count_of_rows // row_block,),
            in_specs=[
                pl.BlockSpec((row_block, depth), lambda b, s: (b, 0)),
                pl.BlockSpec((1, rank, depth), lambda b, s: (s[b], 0, 0)),
                pl.BlockSpec(memory_space=pl.ANY),
            ],
            out_specs=pl.BlockSpec((row_block, rank), lambda b, s: (b, 0)),
        ),
        out_shape=jax.ShapeDtypeStruct((count_of_rows, rank), bf16),
        compiler_params=params(),
        cost_estimate=declared,
    )(tenants, gradient, expand, link)


def scale_kernel(ranks, scales, low, link, out):
    columns = lax.broadcasted_iota(jnp.int32, (row_block, low.shape[1]), 1)
    for b in range(low.shape[0] // row_block):
        here = pl.ds(b * row_block, row_block)
        kept = jnp.where(columns < ranks[b], low[here, :].astype(f32) * scales[b], 0.0)
        out[here, :] = kept.astype(out.dtype)


def scaled_low(ranks, scales, low, link):
    whole = pl.BlockSpec(memory_space=pltpu.VMEM)
    return pl.pallas_call(
        scale_kernel,
        in_specs=[pl.BlockSpec(memory_space=pltpu.SMEM)] * 2
        + [whole, pl.BlockSpec(memory_space=pl.ANY)],
        out_specs=whole,
        out_shape=jax.ShapeDtypeStruct(low.shape, bf16),
        compiler_params=params(),
        cost_estimate=declared,
    )(ranks, scales, low, link)


def factor_kernel(slots_each, slots, scales, left, right, *refs):
    own = refs[-1]
    own[...] = jnp.zeros_like(own)
    for b in range(left.shape[0] // row_block):
        slot = slots[b]

        @pl.when(slot < slots_each)
        def _():
            here = pl.ds(b * row_block, row_block)
            piece = lax.dot_general(
                left[here, :], right[here, :], contract_first, preferred_element_type=f32
            )
            own[slot] += piece * scales[b]


def factor_sums(slots, scales, left, right, slots_each, link):
    whole = pl.BlockSpec(memory_space=pltpu.VMEM)
    return pl.pallas_call(
        functools.partial(factor_kernel, slots_each),
        in_specs=[pl.BlockSpec(memory_space=pltpu.SMEM)] * 2
        + [whole] * 2
        + [pl.BlockSpec(memory_space=pl.ANY)] * len(link),
        out_specs=whole,
        out_shape=jax.ShapeDtypeStruct((slots_each, left.shape[1], right.shape[1]), f32),
        compiler_params=params(),
        cost_estimate=declared,
    )(slots, scales, left, right, *link)


def per_device(
    owner_count,
    gradient,
    projection_input,
    saved_lowrank,
    weights,
    shrink,
    expand,
    tenant_per_block,
    tenant_adapter_rank,
    tenant_owner_index,
):
    count_of_rows, width = gradient.shape
    blocks = count_of_rows // row_block
    tenants = tenant_adapter_rank.shape[0]
    rank_extent = shrink.shape[2]
    node = lax.axis_index("tensor") // 2
    side = lax.axis_index("tensor") % 2
    owner = lax.axis_index("dp")
    at_end = (node == 0) | (node == 3)
    piece_rows = count_of_rows // 2
    lower, upper = 0, 1
    link = []

    roles = (at_end, jnp.logical_not(at_end))

    def run(dest, column, piece, adds):
        scalars = (dest * 2 + column, piece) + roles
        scalars = jnp.stack([jnp.asarray(v, jnp.int32) for v in scalars])
        out = product(scalars, gradient, weights, None, piece_rows, width, adds, link)
        link[:] = [out]
        return out

    def swap(x, active):
        pairs = []
        for z in active:
            pairs += [(2 * z, 2 * z + 1), (2 * z + 1, 2 * z)]
        return lax.ppermute(x, "tensor", pairs)

    def along(x, hops):
        return lax.ppermute(
            x, "tensor", [(2 * a + y, 2 * b + y) for a, b in hops for y in range(2)]
        )

    nodes = 4
    every = (0, 1, 2, 3)
    from_ends = [(0, 1), (3, 2)]
    across = [(1, 2), (2, 1)]
    to_ends = [(1, 0), (2, 3)]
    pairwise = from_ends + to_ends
    def exchange(x):
        pairs = []
        for group in range(2):
            for y in range(2):
                pairs += [(group * 8 + 2 * a + y, group * 8 + 2 * b + y) for a, b in across]
                pairs += [(group * 8 + 2 * z + y, (1 - group) * 8 + 2 * z + y) for z in (0, 3)]
        return lax.ppermute(x, ("groups", "tensor"), pairs)

    first_half = node < 2
    far = jnp.where(first_half, 3, 0)
    beyond = jnp.where(first_half, 2, 1)
    nearer = jnp.where(first_half, 1, 2)
    near_end = jnp.where(first_half, 0, 3)
    same, other = side, 1 - side

    def all_owners(x):
        return lax.all_gather(x, "dp", axis=0, tiled=True)

    block_tenants = jnp.zeros((owner_count * blocks,), jnp.int32)
    for hop in range(owner_count):
        pairs = [(i, (i + hop) % owner_count) for i in range(owner_count)]
        theirs = lax.ppermute(tenant_per_block, "dp", pairs) if hop else tenant_per_block
        place = lax.rem(owner - hop + owner_count, owner_count) * blocks
        block_tenants = lax.dynamic_update_slice_in_dim(block_tenants, theirs, place, 0)
    tenant_ids = jnp.arange(tenants, dtype=jnp.int32)
    matches = block_tenants[:, None] == tenant_ids[None, :]
    block_ranks = jnp.sum(jnp.where(matches, tenant_adapter_rank[None, :], 0), axis=1)
    block_scales = adapter_alpha / block_ranks.astype(f32)
    key = tenant_owner_index * tenants + tenant_ids
    slot_of = jnp.sum((key[None, :] < key[:, None]).astype(jnp.int32), axis=1)
    slots_each = tenants // owner_count
    slot_here = lax.rem(slot_of - owner * slots_each + tenants, tenants)
    block_slots = jnp.sum(jnp.where(matches, slot_here[None, :], 0), axis=1)

    own_ranks = lax.dynamic_slice_in_dim(block_ranks, owner * blocks, blocks, 0)
    own_scales = lax.dynamic_slice_in_dim(block_scales, owner * blocks, blocks, 0)

    def adapter_space():
        part = low_product(tenant_per_block, gradient, expand, link[0])
        link[:] = [part]
        return lax.psum(part, "tensor")

    def scale_low(low):
        out = scaled_low(own_ranks, own_scales, low, link[0])
        link[:] = [out]
        return out

    def expand_gradient():
        kept = jnp.arange(rank_extent, dtype=jnp.int32)[None, :] < block_ranks[:, None]
        saved = all_owners(saved_lowrank).reshape(-1, row_block, rank_extent)
        saved = (saved * kept[:, None, :].astype(bf16)).reshape(-1, rank_extent)
        out = factor_sums(
            block_slots, block_scales, saved, all_owners(gradient), slots_each, link
        )
        link[:] = [out]
        return out

    def shrink_gradient(low):
        out = factor_sums(
            block_slots, jnp.ones_like(block_scales), all_owners(projection_input), all_owners(low),
            slots_each, link,
        )
        link[:] = [out]
        return out

    firsts = (jnp.where(at_end, far, near_end) * 2 + other, upper, far * 2 + other, lower)
    out_y, out_z = product_pair(
        jnp.stack([jnp.asarray(v, jnp.int32) for v in firsts]),
        gradient, weights, piece_rows, width,
    )
    y1, direct_a = swap(out_y, every), along(out_z, pairwise)
    link[:] = [out_z]
    low_whole = adapter_space()
    y2 = swap(run(beyond, other, lower, []), every)
    direct_b = along(run(far, same, lower, []), pairwise)
    out = run(
        far,
        jnp.where(at_end, same, other),
        jnp.where(at_end, upper, lower),
        [(y1, 1), (direct_a, 2)],
    )
    upper_1, direct_a = along(out, pairwise), exchange(out)
    y3 = swap(run(jnp.where(at_end, beyond, far), other, upper, []), every)
    out = run(jnp.where(at_end, beyond, far), same, lower, [(y2, 1), (direct_b, 2)])
    lower_2, direct_b = along(out, pairwise), exchange(out)
    y4 = swap(run(jnp.where(at_end, nearer, beyond), other, lower, []), every)
    out = run(
        jnp.where(at_end, beyond, near_end),
        jnp.where(at_end, same, other),
        jnp.where(at_end, upper, lower),
        [(y3, 1), (direct_a, 2)],
    )
    both_3 = along(out, pairwise)
    upper_far = exchange(run(far, same, upper, [(y3, 0), (upper_1, 0)]))
    y5 = swap(run(jnp.where(at_end, nearer, beyond), other, upper, []), every)
    grad_expand = expand_gradient()
    out = run(jnp.where(at_end, nearer, near_end), same, lower, [(y4, 1), (direct_b, 2)])
    both_4 = along(out, pairwise)
    lower_4 = exchange(run(beyond, same, lower, [(y4, 0), (lower_2, 0)]))
    low = scale_low(low_whole)
    y6 = swap(run(node, other, upper, []), every)
    out = run(
        jnp.where(at_end, nearer, near_end), same, upper, [(y5, 1), (y1, 2), (upper_far, 2)]
    )
    both_5 = along(out, pairwise)
    y7 = swap(run(node, other, lower, [(both_3, 1)]), every)
    upper_4 = exchange(run(beyond, same, upper, [(y5, 0), (both_3, 0)]))
    link += [both_4, lower_4]
    grad_shrink = shrink_gradient(low)
    def base(piece, adds):
        in_piece = piece_rows // row_block
        scalars = [node * 2 + side, jnp.int32(piece)] + [jnp.asarray(r, jnp.int32) for r in roles]
        scalars += [tenant_per_block[piece * in_piece + i] for i in range(in_piece)]
        out = product(
            jnp.stack(scalars).astype(jnp.int32),
            gradient, weights, piece, piece_rows, width, adds, link, (low, shrink),
        )
        link[:] = [out]
        return out

    lower_base = base(lower, [(both_4, 0), (lower_4, 2)])
    upper_base = base(upper, [(y6, 0)])
    inner = jnp.reshape(roles[1].astype(jnp.int32), (1,))
    input_gradient = finish(inner, [[lower_base, y7], [upper_base, both_5, upper_4]])
    return (input_gradient, grad_shrink, grad_expand)


def per_device_any(
    query_cotangent,
    projection_input,
    saved_lowrank,
    query_matrix,
    adapter_shrink,
    adapter_expand,
    tenant_per_block,
    tenant_adapter_rank,
    tenant_owner_index,
):
    count_of_rows, shard_extent = query_cotangent.shape
    block_count = count_of_rows // 128
    tenant_count = tenant_adapter_rank.shape[0]
    rank_extent = adapter_shrink.shape[2]
    frozen_product = lax.psum_scatter(
        lax.dot_general(
            query_matrix,
            query_cotangent,
            contract_last,
            preferred_element_type=jnp.float32,
        ).astype(jnp.bfloat16),
        "tensor",
        scatter_dimension=0,
        tiled=True,
    ).astype(jnp.float32)
    tenant_ids = jnp.arange(tenant_count, dtype=jnp.int32)
    matches = tenant_per_block[:, None] == tenant_ids[None, :]
    rank_per_block = jnp.sum(jnp.where(matches, tenant_adapter_rank[None, :], 0), axis=1).astype(
        jnp.float32
    )
    scale_per_block = adapter_alpha / rank_per_block
    block_mask = (
        jnp.arange(rank_extent).astype(jnp.float32)[None, :] < rank_per_block[:, None]
    ).astype(jnp.float32)
    gradient_per_block = query_cotangent.reshape(block_count, 128, shard_extent)
    expand_per_block = jnp.take(adapter_expand, tenant_per_block, axis=0)
    low_part = jnp.einsum(
        "zuh,zsh->zus", gradient_per_block, expand_per_block, preferred_element_type=jnp.float32
    )
    low_whole = lax.psum(low_part.astype(jnp.bfloat16), "tensor").astype(jnp.float32)
    lowrank_bfloat = (low_whole * (scale_per_block[:, None, None] * block_mask[:, None, :])).astype(
        jnp.bfloat16
    )
    shrink_per_block = jnp.take(adapter_shrink, tenant_per_block, axis=0)
    adapter_term = jnp.einsum(
        "uwq,ueq->uwe", lowrank_bfloat, shrink_per_block, preferred_element_type=jnp.float32
    )
    input_gradient = (frozen_product.T + adapter_term.reshape(count_of_rows, shard_extent)).astype(
        jnp.bfloat16
    )
    slot_order = jnp.argsort(tenant_owner_index * tenant_count + tenant_ids)
    slot_of = jnp.argsort(slot_order)
    block_slot = jnp.sum(jnp.where(matches, slot_of[None, :], 0), axis=1)
    block_select = (block_slot[:, None] == tenant_ids[None, :]).astype(jnp.float32)
    saved_lowrank_masked = saved_lowrank.reshape(block_count, 128, rank_extent) * block_mask[
        :, None, :
    ].astype(jnp.bfloat16)
    input_per_block = projection_input.reshape(block_count, 128, shard_extent)
    shrink_piece = jnp.einsum(
        "tme,tmj->tej", input_per_block, lowrank_bfloat, preferred_element_type=jnp.float32
    )
    expand_piece = jnp.einsum(
        "paw,pan->pwn", saved_lowrank_masked, gradient_per_block, preferred_element_type=jnp.float32
    )
    expand_piece = expand_piece * scale_per_block[:, None, None]
    shrink_slots = jnp.einsum(
        "bs,bdr->sdr", block_select, shrink_piece, precision=lax.Precision.HIGHEST
    )
    expand_slots = jnp.einsum(
        "bs,brd->srd", block_select, expand_piece, precision=lax.Precision.HIGHEST
    )
    grad_shrink, grad_expand = (
        lax.psum_scatter(
            shrink_slots.astype(jnp.bfloat16), "dp", scatter_dimension=0, tiled=True
        ).astype(jnp.float32),
        lax.psum_scatter(
            expand_slots.astype(jnp.bfloat16), "dp", scatter_dimension=0, tiled=True
        ).astype(jnp.float32),
    )
    return (input_gradient, grad_shrink, grad_expand)


def solution(mesh):
    placed = (
        P(("groups", "dp"), "tensor"),
        P(("groups", "dp"), "tensor"),
        P(("groups", "dp"), None),
        P(None, "tensor"),
        P(None, "tensor", None),
        P(None, None, "tensor"),
        P(("groups", "dp")),
        P(),
        P(),
    )
    body = per_device_any
    if mesh.shape["tensor"] == 8 and mesh.shape["groups"] == 2:
        body = functools.partial(per_device, mesh.shape["dp"])
    return jax.shard_map(
        body,
        mesh=mesh,
        in_specs=placed,
        out_specs=(
            P(("groups", "dp"), "tensor"),
            P(("groups", "dp"), "tensor", None),
            P(("groups", "dp"), None, "tensor"),
        ),
        check_vma=False,
    )
```

```python
import functools

import jax
import jax.numpy as jnp
from jax import lax
from jax.experimental import pallas as pl
from jax.experimental.pallas import tpu as pltpu
from jax.sharding import PartitionSpec as P

adapter_alpha = 32.0
row_block = 128
bf16 = jnp.bfloat16
f32 = jnp.float32
contract_last = (((1,), (1,)), ((), ()))
contract_first = (((0,), (0,)), ((), ()))
vmem_bytes = 58 * 1024 * 1024
declared = pl.CostEstimate(flops=10**12, bytes_accessed=10**9, transcendentals=0)


def params():
    return pltpu.CompilerParams(vmem_limit_bytes=vmem_bytes)


def product_kernel(modes, block_count, *refs):
    position = 1
    rows, weights = refs[1], refs[2]
    position = 3
    total = lax.dot_general(
        rows[...], weights[...], contract_last, preferred_element_type=f32
    )
    for mode in modes:
        addend = refs[position][...].astype(f32)
        if mode:
            addend = addend * refs[0][1 + mode].astype(f32)
        total = total + addend
        position += 1
    if block_count:
        low = refs[position]
        position += 1
        terms = []
        for i in range(block_count):
            terms.append(
                lax.dot_general(
                    low[i * row_block : (i + 1) * row_block, :],
                    refs[position][0],
                    contract_last,
                    preferred_element_type=f32,
                )
            )
            position += 1
        total = total + jnp.concatenate(terms, axis=0)
    refs[-1][...] = total.astype(refs[-1].dtype)


def product(scalars, gradient, weights, piece, piece_rows, width, adds, link, adapter=None):
    depth = gradient.shape[1]
    tile = min(width, 512)
    while width % tile:
        tile //= 2
    steps = width // tile
    in_specs = [
        pl.BlockSpec((piece_rows, depth), lambda j, s: (s[1], 0)),
        pl.BlockSpec((tile, depth), lambda j, s: (s[0] * steps + j, 0)),
    ]
    operands = [gradient, weights]
    for array, _ in adds:
        in_specs.append(pl.BlockSpec((piece_rows, tile), lambda j, s: (0, j)))
        operands.append(array)
    block_count = 0
    if adapter is not None:
        low, shrink = adapter
        rank = low.shape[1]
        block_count = piece_rows // row_block
        in_specs.append(pl.BlockSpec((piece_rows, rank), lambda j, s: (piece, 0)))
        operands.append(low)
        for i in range(block_count):
            in_specs.append(
                pl.BlockSpec((1, tile, rank), functools.partial(lambda j, s, i: (s[4 + i], j, 0), i=i))
            )
            operands.append(shrink)
    for array in link:
        in_specs.append(pl.BlockSpec(memory_space=pl.ANY))
        operands.append(array)
    return pl.pallas_call(
        functools.partial(product_kernel, tuple(mode for _, mode in adds), block_count),
        grid_spec=pltpu.PrefetchScalarGridSpec(
            num_scalar_prefetch=1,
            grid=(steps,),
            in_specs=in_specs,
            out_specs=pl.BlockSpec((piece_rows, tile), lambda j, s: (0, j)),
        ),
        out_shape=jax.ShapeDtypeStruct((piece_rows, width), bf16),
        compiler_params=params(),
        cost_estimate=declared,
    )(scalars, *operands)


def pair_kernel(scalars, rows, weights, first, second):
    part = lax.dot_general(
        rows[...], weights[...], contract_last, preferred_element_type=f32
    ).astype(bf16)

    @pl.when(pl.program_id(0) == 0)
    def _():
        first[...] = part

    @pl.when(pl.program_id(0) == 1)
    def _():
        second[...] = part


def product_pair(scalars, gradient, weights, piece_rows, width):
    depth = gradient.shape[1]
    tile = width // 2
    piece = jax.ShapeDtypeStruct((piece_rows, width), bf16)
    return pl.pallas_call(
        pair_kernel,
        grid_spec=pltpu.PrefetchScalarGridSpec(
            num_scalar_prefetch=1,
            grid=(2, 2),
            in_specs=[
                pl.BlockSpec((piece_rows, depth), lambda t, j, s: (s[2 * t + 1], 0)),
                pl.BlockSpec((tile, depth), lambda t, j, s: (s[2 * t] * 2 + j, 0)),
            ],
            out_specs=[
                pl.BlockSpec((piece_rows, tile), lambda t, j, s: (0, jnp.where(t == 0, j, 1))),
                pl.BlockSpec((piece_rows, tile), lambda t, j, s: (0, jnp.where(t == 1, j, 0))),
            ],
        ),
        out_shape=[piece, piece],
        compiler_params=params(),
        cost_estimate=declared,
    )(scalars, gradient, weights)


def finish_kernel(counts, inner, *refs):
    out, staged, done = refs[-3:]
    rows = refs[0].shape[0]
    part = rows // 2
    copies = []
    position = 0
    for piece, count in enumerate(counts):
        for half in range(2):
            here = slice(half * part, (half + 1) * part)
            total = refs[position][here, :].astype(f32)
            for i in range(1, count):
                addend = refs[position + i][here, :].astype(f32)
                if piece and i == count - 1:
                    addend = addend * inner[0].astype(f32)
                total = total + addend
            index = 2 * piece + half
            staged[index] = total.astype(staged.dtype)
            copy = pltpu.make_async_copy(
                staged.at[index], out.at[pl.ds(index * part, part), :], done.at[index]
            )
            copy.start()
            copies.append(copy)
        position += count
    for copy in copies:
        copy.wait()


def finish(inner, groups):
    rows, width = groups[0][0].shape
    arrays = [array for group in groups for array in group]
    parts = 2 * len(groups)
    return pl.pallas_call(
        functools.partial(finish_kernel, tuple(len(group) for group in groups)),
        in_specs=[pl.BlockSpec(memory_space=pltpu.SMEM)]
        + [pl.BlockSpec(memory_space=pltpu.VMEM)] * len(arrays),
        out_specs=pl.BlockSpec(memory_space=pl.ANY),
        out_shape=jax.ShapeDtypeStruct((len(groups) * rows, width), bf16),
        scratch_shapes=[
            pltpu.VMEM((parts, rows // 2, width), bf16),
            pltpu.SemaphoreType.DMA((parts,)),
        ],
        compiler_params=params(),
        cost_estimate=declared,
    )(inner, *arrays)


def low_kernel(tenants, rows, expand, link, out):
    out[...] = lax.dot_general(
        rows[...], expand[0], contract_last, preferred_element_type=f32
    ).astype(out.dtype)


def low_product(tenants, gradient, expand, link):
    count_of_rows, depth = gradient.shape
    rank = expand.shape[1]
    return pl.pallas_call(
        low_kernel,
        grid_spec=pltpu.PrefetchScalarGridSpec(
            num_scalar_prefetch=1,
            grid=(count_of_rows // row_block,),
            in_specs=[
                pl.BlockSpec((row_block, depth), lambda b, s: (b, 0)),
                pl.BlockSpec((1, rank, depth), lambda b, s: (s[b], 0, 0)),
                pl.BlockSpec(memory_space=pl.ANY),
            ],
            out_specs=pl.BlockSpec((row_block, rank), lambda b, s: (b, 0)),
        ),
        out_shape=jax.ShapeDtypeStruct((count_of_rows, rank), bf16),
        compiler_params=params(),
        cost_estimate=declared,
    )(tenants, gradient, expand, link)


def scale_kernel(ranks, scales, low, link, out):
    columns = lax.broadcasted_iota(jnp.int32, (row_block, low.shape[1]), 1)
    for b in range(low.shape[0] // row_block):
        here = pl.ds(b * row_block, row_block)
        kept = jnp.where(columns < ranks[b], low[here, :].astype(f32) * scales[b], 0.0)
        out[here, :] = kept.astype(out.dtype)


def scaled_low(ranks, scales, low, link):
    whole = pl.BlockSpec(memory_space=pltpu.VMEM)
    return pl.pallas_call(
        scale_kernel,
        in_specs=[pl.BlockSpec(memory_space=pltpu.SMEM)] * 2
        + [whole, pl.BlockSpec(memory_space=pl.ANY)],
        out_specs=whole,
        out_shape=jax.ShapeDtypeStruct(low.shape, bf16),
        compiler_params=params(),
        cost_estimate=declared,
    )(ranks, scales, low, link)


def factor_kernel(slots_each, slots, scales, left, right, *refs):
    own = refs[-1]
    own[...] = jnp.zeros_like(own)
    for b in range(left.shape[0] // row_block):
        slot = slots[b]

        @pl.when(slot < slots_each)
        def _():
            here = pl.ds(b * row_block, row_block)
            piece = lax.dot_general(
                left[here, :], right[here, :], contract_first, preferred_element_type=f32
            )
            own[slot] += piece * scales[b]


def factor_sums(slots, scales, left, right, slots_each, link):
    whole = pl.BlockSpec(memory_space=pltpu.VMEM)
    return pl.pallas_call(
        functools.partial(factor_kernel, slots_each),
        in_specs=[pl.BlockSpec(memory_space=pltpu.SMEM)] * 2
        + [whole] * 2
        + [pl.BlockSpec(memory_space=pl.ANY)] * len(link),
        out_specs=whole,
        out_shape=jax.ShapeDtypeStruct((slots_each, left.shape[1], right.shape[1]), f32),
        compiler_params=params(),
        cost_estimate=declared,
    )(slots, scales, left, right, *link)


def per_device(
    owner_count,
    gradient,
    projection_input,
    saved_lowrank,
    weights,
    shrink,
    expand,
    tenant_per_block,
    tenant_adapter_rank,
    tenant_owner_index,
):
    count_of_rows, width = gradient.shape
    blocks = count_of_rows // row_block
    tenants = tenant_adapter_rank.shape[0]
    rank_extent = shrink.shape[2]
    node = lax.axis_index("tensor") // 2
    side = lax.axis_index("tensor") % 2
    owner = lax.axis_index("dp")
    at_end = (node == 0) | (node == 3)
    piece_rows = count_of_rows // 2
    lower, upper = 0, 1
    link = []

    roles = (at_end, jnp.logical_not(at_end))

    def run(dest, column, piece, adds):
        scalars = (dest * 2 + column, piece) + roles
        scalars = jnp.stack([jnp.asarray(v, jnp.int32) for v in scalars])
        out = product(scalars, gradient, weights, None, piece_rows, width, adds, link)
        link[:] = [out]
        return out

    def swap(x, active):
        pairs = []
        for z in active:
            pairs += [(2 * z, 2 * z + 1), (2 * z + 1, 2 * z)]
        return lax.ppermute(x, "tensor", pairs)

    def along(x, hops):
        return lax.ppermute(
            x, "tensor", [(2 * a + y, 2 * b + y) for a, b in hops for y in range(2)]
        )

    nodes = 4
    every = (0, 1, 2, 3)
    from_ends = [(0, 1), (3, 2)]
    across = [(1, 2), (2, 1)]
    to_ends = [(1, 0), (2, 3)]
    pairwise = from_ends + to_ends
    def exchange(x):
        pairs = []
        for group in range(2):
            for y in range(2):
                pairs += [(group * 8 + 2 * a + y, group * 8 + 2 * b + y) for a, b in across]
                pairs += [(group * 8 + 2 * z + y, (1 - group) * 8 + 2 * z + y) for z in (0, 3)]
        return lax.ppermute(x, ("groups", "tensor"), pairs)

    first_half = node < 2
    far = jnp.where(first_half, 3, 0)
    beyond = jnp.where(first_half, 2, 1)
    nearer = jnp.where(first_half, 1, 2)
    near_end = jnp.where(first_half, 0, 3)
    same, other = side, 1 - side

    def all_owners(x):
        return lax.all_gather(x, "dp", axis=0, tiled=True)

    block_tenants = jnp.zeros((owner_count * blocks,), jnp.int32)
    for hop in range(owner_count):
        pairs = [(i, (i + hop) % owner_count) for i in range(owner_count)]
        theirs = lax.ppermute(tenant_per_block, "dp", pairs) if hop else tenant_per_block
        place = lax.rem(owner - hop + owner_count, owner_count) * blocks
        block_tenants = lax.dynamic_update_slice_in_dim(block_tenants, theirs, place, 0)
    tenant_ids = jnp.arange(tenants, dtype=jnp.int32)
    matches = block_tenants[:, None] == tenant_ids[None, :]
    block_ranks = jnp.sum(jnp.where(matches, tenant_adapter_rank[None, :], 0), axis=1)
    block_scales = adapter_alpha / block_ranks.astype(f32)
    key = tenant_owner_index * tenants + tenant_ids
    slot_of = jnp.sum((key[None, :] < key[:, None]).astype(jnp.int32), axis=1)
    slots_each = tenants // owner_count
    slot_here = lax.rem(slot_of - owner * slots_each + tenants, tenants)
    block_slots = jnp.sum(jnp.where(matches, slot_here[None, :], 0), axis=1)

    own_ranks = lax.dynamic_slice_in_dim(block_ranks, owner * blocks, blocks, 0)
    own_scales = lax.dynamic_slice_in_dim(block_scales, owner * blocks, blocks, 0)

    def adapter_space():
        part = low_product(tenant_per_block, gradient, expand, link[0])
        link[:] = [part]
        return lax.psum(part, "tensor")

    def scale_low(low):
        out = scaled_low(own_ranks, own_scales, low, link[0])
        link[:] = [out]
        return out

    def expand_gradient():
        kept = jnp.arange(rank_extent, dtype=jnp.int32)[None, :] < block_ranks[:, None]
        saved = all_owners(saved_lowrank).reshape(-1, row_block, rank_extent)
        saved = (saved * kept[:, None, :].astype(bf16)).reshape(-1, rank_extent)
        out = factor_sums(
            block_slots, block_scales, saved, all_owners(gradient), slots_each, link
        )
        link[:] = [out]
        return out

    def shrink_gradient(low):
        out = factor_sums(
            block_slots, jnp.ones_like(block_scales), all_owners(projection_input), all_owners(low),
            slots_each, link,
        )
        link[:] = [out]
        return out

    firsts = (jnp.where(at_end, far, near_end) * 2 + other, upper, far * 2 + other, lower)
    out_y, out_z = product_pair(
        jnp.stack([jnp.asarray(v, jnp.int32) for v in firsts]),
        gradient, weights, piece_rows, width,
    )
    y1, direct_a = swap(out_y, every), along(out_z, pairwise)
    link[:] = [out_z]
    low_whole = adapter_space()
    y2 = swap(run(beyond, other, lower, []), every)
    direct_b = along(run(far, same, lower, []), pairwise)
    out = run(
        far,
        jnp.where(at_end, same, other),
        jnp.where(at_end, upper, lower),
        [(y1, 1), (direct_a, 2)],
    )
    upper_1, direct_a = along(out, pairwise), exchange(out)
    y3 = swap(run(jnp.where(at_end, beyond, far), other, upper, []), every)
    out = run(jnp.where(at_end, beyond, far), same, lower, [(y2, 1), (direct_b, 2)])
    lower_2, direct_b = along(out, pairwise), exchange(out)
    y4 = swap(run(jnp.where(at_end, nearer, beyond), other, lower, []), every)
    out = run(
        jnp.where(at_end, beyond, near_end),
        jnp.where(at_end, same, other),
        jnp.where(at_end, upper, lower),
        [(y3, 1), (direct_a, 2)],
    )
    both_3 = along(out, pairwise)
    upper_far = exchange(run(far, same, upper, [(y3, 0), (upper_1, 0)]))
    grad_expand = expand_gradient()
    y5 = swap(run(jnp.where(at_end, nearer, beyond), other, upper, []), every)
    out = run(jnp.where(at_end, nearer, near_end), same, lower, [(y4, 1), (direct_b, 2)])
    both_4 = along(out, pairwise)
    lower_4 = exchange(run(beyond, same, lower, [(y4, 0), (lower_2, 0)]))
    low = scale_low(low_whole)
    y6 = swap(run(node, other, upper, []), every)
    out = run(
        jnp.where(at_end, nearer, near_end), same, upper, [(y5, 1), (y1, 2), (upper_far, 2)]
    )
    both_5 = along(out, pairwise)
    y7 = swap(run(node, other, lower, [(both_3, 1)]), every)
    upper_4 = exchange(run(beyond, same, upper, [(y5, 0), (both_3, 0)]))
    link += [both_4, lower_4]
    grad_shrink = shrink_gradient(low)
    def base(piece, adds):
        in_piece = piece_rows // row_block
        scalars = [node * 2 + side, jnp.int32(piece)] + [jnp.asarray(r, jnp.int32) for r in roles]
        scalars += [tenant_per_block[piece * in_piece + i] for i in range(in_piece)]
        out = product(
            jnp.stack(scalars).astype(jnp.int32),
            gradient, weights, piece, piece_rows, width, adds, link, (low, shrink),
        )
        link[:] = [out]
        return out

    lower_base = base(lower, [(both_4, 0), (lower_4, 2)])
    upper_base = base(upper, [(y6, 0)])
    inner = jnp.reshape(roles[1].astype(jnp.int32), (1,))
    input_gradient = finish(inner, [[lower_base, y7], [upper_base, both_5, upper_4]])
    return (input_gradient, grad_shrink, grad_expand)


def per_device_any(
    query_cotangent,
    projection_input,
    saved_lowrank,
    query_matrix,
    adapter_shrink,
    adapter_expand,
    tenant_per_block,
    tenant_adapter_rank,
    tenant_owner_index,
):
    count_of_rows, shard_extent = query_cotangent.shape
    block_count = count_of_rows // 128
    tenant_count = tenant_adapter_rank.shape[0]
    rank_extent = adapter_shrink.shape[2]
    frozen_product = lax.psum_scatter(
        lax.dot_general(
            query_matrix,
            query_cotangent,
            contract_last,
            preferred_element_type=jnp.float32,
        ).astype(jnp.bfloat16),
        "tensor",
        scatter_dimension=0,
        tiled=True,
    ).astype(jnp.float32)
    tenant_ids = jnp.arange(tenant_count, dtype=jnp.int32)
    matches = tenant_per_block[:, None] == tenant_ids[None, :]
    rank_per_block = jnp.sum(jnp.where(matches, tenant_adapter_rank[None, :], 0), axis=1).astype(
        jnp.float32
    )
    scale_per_block = adapter_alpha / rank_per_block
    block_mask = (
        jnp.arange(rank_extent).astype(jnp.float32)[None, :] < rank_per_block[:, None]
    ).astype(jnp.float32)
    gradient_per_block = query_cotangent.reshape(block_count, 128, shard_extent)
    expand_per_block = jnp.take(adapter_expand, tenant_per_block, axis=0)
    low_part = jnp.einsum(
        "zuh,zsh->zus", gradient_per_block, expand_per_block, preferred_element_type=jnp.float32
    )
    low_whole = lax.psum(low_part.astype(jnp.bfloat16), "tensor").astype(jnp.float32)
    lowrank_bfloat = (low_whole * (scale_per_block[:, None, None] * block_mask[:, None, :])).astype(
        jnp.bfloat16
    )
    shrink_per_block = jnp.take(adapter_shrink, tenant_per_block, axis=0)
    adapter_term = jnp.einsum(
        "uwq,ueq->uwe", lowrank_bfloat, shrink_per_block, preferred_element_type=jnp.float32
    )
    input_gradient = (frozen_product.T + adapter_term.reshape(count_of_rows, shard_extent)).astype(
        jnp.bfloat16
    )
    slot_order = jnp.argsort(tenant_owner_index * tenant_count + tenant_ids)
    slot_of = jnp.argsort(slot_order)
    block_slot = jnp.sum(jnp.where(matches, slot_of[None, :], 0), axis=1)
    block_select = (block_slot[:, None] == tenant_ids[None, :]).astype(jnp.float32)
    saved_lowrank_masked = saved_lowrank.reshape(block_count, 128, rank_extent) * block_mask[
        :, None, :
    ].astype(jnp.bfloat16)
    input_per_block = projection_input.reshape(block_count, 128, shard_extent)
    shrink_piece = jnp.einsum(
        "tme,tmj->tej", input_per_block, lowrank_bfloat, preferred_element_type=jnp.float32
    )
    expand_piece = jnp.einsum(
        "paw,pan->pwn", saved_lowrank_masked, gradient_per_block, preferred_element_type=jnp.float32
    )
    expand_piece = expand_piece * scale_per_block[:, None, None]
    shrink_slots = jnp.einsum(
        "bs,bdr->sdr", block_select, shrink_piece, precision=lax.Precision.HIGHEST
    )
    expand_slots = jnp.einsum(
        "bs,brd->srd", block_select, expand_piece, precision=lax.Precision.HIGHEST
    )
    grad_shrink, grad_expand = (
        lax.psum_scatter(
            shrink_slots.astype(jnp.bfloat16), "dp", scatter_dimension=0, tiled=True
        ).astype(jnp.float32),
        lax.psum_scatter(
            expand_slots.astype(jnp.bfloat16), "dp", scatter_dimension=0, tiled=True
        ).astype(jnp.float32),
    )
    return (input_gradient, grad_shrink, grad_expand)


def solution(mesh):
    placed = (
        P(("groups", "dp"), "tensor"),
        P(("groups", "dp"), "tensor"),
        P(("groups", "dp"), None),
        P(None, "tensor"),
        P(None, "tensor", None),
        P(None, None, "tensor"),
        P(("groups", "dp")),
        P(),
        P(),
    )
    body = per_device_any
    if mesh.shape["tensor"] == 8 and mesh.shape["groups"] == 2:
        body = functools.partial(per_device, mesh.shape["dp"])
    return jax.shard_map(
        body,
        mesh=mesh,
        in_specs=placed,
        out_specs=(
            P(("groups", "dp"), "tensor"),
            P(("groups", "dp"), "tensor", None),
            P(("groups", "dp"), None, "tensor"),
        ),
        check_vma=False,
    )
```
